32 devices in a mesh: dp: 8 (over z, y), expert: 4 (over x, core).
Axes of the slice: x: 2, y: 2, z: 4, core: 2. Of those that a mesh axis runs over, the one named last changes fastest.
Arguments:
- tokens: bfloat16 [65536, 512], P(('dp', 'expert')), may hold values from -6 to 6
- seq_lengths: int32 [32], P(('dp', 'expert')), may hold values from 256 to 2048, as said below
- group_map: int32 [32, 2048], P(('dp', 'expert')), may hold values from 0 to 2047, each once within a row
- gain_attn: bfloat16 [512], P(('dp', 'expert')), may hold values from 0.099609375 to 1.8984375
- gain_mix: bfloat16 [512], P(('dp', 'expert')), may hold values from 0.099609375 to 1.8984375
- w_qkv: bfloat16 [512, 1536], P(('dp', 'expert')), may hold values from -0.25 to 0.25
- w_out: bfloat16 [512, 512], P(('dp', 'expert')), may hold values from -2 to 2
- w_ctrl: bfloat16 [512, 16], P(('dp', 'expert')), may hold values from -0.125 to 0.125
- w_up: bfloat16 [16, 512, 2048], P('expert'), may hold values from -1 to 1
- w_down: bfloat16 [16, 2048, 512], P('expert'), may hold values from -2 to 2
- cotangent: bfloat16 [65536, 512], P(('dp', 'expert')), may hold values from -6 to 6
Outputs:
- output: bfloat16 [65536, 512], P(('dp', 'expert'))
- grad_tokens: bfloat16 [65536, 512], P(('dp', 'expert'))
- grad_gain_attn: float32 [512], P(('dp', 'expert'))
- grad_gain_mix: float32 [512], P(('dp', 'expert'))
- grad_w_qkv: float32 [512, 1536], P(('dp', 'expert'))
- grad_w_out: float32 [512, 512], P(('dp', 'expert'))
- grad_w_ctrl: float32 [512, 16], P(('dp', 'expert'))
- grad_w_up: float32 [16, 512, 2048], P('expert', 'dp')
- grad_w_down: float32 [16, 2048, 512], P('expert', 'dp')
The draws below stay inside these ranges and needn't reach their ends.
Inputs may be any that keep to these rules, and one draw needn't show every extreme that they name: `seq_lengths`: each entry is 256 or 2048: that device's block of tokens is sequences of that length laid end to end; both values occur in every draw. `group_map`: each row is a permutation of 0 to 2047.
All inputs are finite; a program needn't handle non-finite values.
Results may differ from the reference program's by a relative error of at most 0.019.
Values may be sent and summed in bfloat16 or wider, within the bound.
No kernel may reach another device: no remote copies, remote signals or barrier semaphores. Data moves between devices by JAX's collectives and lax.ppermute only.
A program may use at most 320 MiB of HBM per device.

```python
import jax
import jax.numpy as jnp
from jax import lax

D = 512
HEADS = 8
HEAD = 64
FF = 2048
G = 32
E = 16
TOK_DEV = 2048
SHORT = 256
TOKENS = 65536
N_DP = 8
N_EXPERT = 4
DEVICES = 32


def draw_seq_lengths(key, part):
    key = jax.random.fold_in(key, 11)
    key_pick, key_first, key_second = jax.random.split(key, 3)
    picked = jax.random.randint(key_pick, (DEVICES,), 0, 8)
    first_long = jax.random.randint(key_first, (), 0, DEVICES)
    first_short = (first_long + jax.random.randint(key_second, (), 1, DEVICES)) % DEVICES
    places = jnp.arange(DEVICES, dtype=jnp.int32)
    longer = ((picked == 0) | (places == first_long)) & (places != first_short)
    return jnp.where(longer, TOK_DEV, SHORT).astype(jnp.int32)


def spiked(result, stream_key, source, target, parts, factor):
    owner, partner = [(jnp.arange(result.shape[dim]) // (result.shape[dim] // parts)).reshape([-1 if axis == dim else 1 for axis in range(result.ndim)]) for dim in (source, target)]
    chosen = jax.random.permutation(stream_key, parts)[partner]
    strong = (owner == chosen) | (owner == (partner + parts // 2) % parts)
    return jnp.where(strong, factor * result, result)


def level_of(rng, dims, pieces, least, top_value):
    level = 1.0
    for axis_at, parts in pieces:
        steps = jax.random.uniform(jax.random.fold_in(jax.random.fold_in(rng, 6), axis_at), (parts,), jnp.float32, least / len(pieces), top_value / len(pieces))
        level = level * jnp.repeat(jnp.exp(steps), dims[axis_at] // parts).reshape((-1,) + (1,) * (len(dims) - 1 - axis_at))
    return level


def gaussian(own_key, shape, deviation, reach, cuts=(), kind=jnp.bfloat16):
    loudness = level_of(own_key, shape, cuts, -0.22, 0.18) if cuts else 1.0
    drawn = jax.random.normal(own_key, shape, jnp.float32) * deviation * loudness
    return jnp.minimum(jnp.maximum(drawn, -reach), reach).astype(kind)


def heavy_noise(stream_key, shape, scale, most, shards, heavy, kind=jnp.bfloat16):
    array = scale * jax.random.normal(stream_key, shape, jnp.float32)
    if shards:
        array = array * level_of(stream_key, shape, shards, -0.22, 0.18)
    return jnp.clip(spiked(array, jax.random.fold_in(stream_key, 3), *heavy), -most, most).astype(kind)


def setup_inputs(seed: int = 0) -> dict:
    keys = jax.random.split(jax.random.key(seed), 12)
    return {
        "tokens": gaussian(keys[0], (TOKENS, D), 1.0, 6.0, ((0, 32),)),
        "seq_lengths": draw_seq_lengths(jax.random.fold_in(keys[11], 71), 0),
        "group_map": jax.vmap(lambda own: jax.random.permutation(own, TOK_DEV))(jax.random.split(keys[2], (N_DP * N_EXPERT))).reshape((N_DP * N_EXPERT, TOK_DEV)).astype(jnp.int32),
        "gain_attn": jnp.clip(1.0 + 0.18 * jax.random.normal(keys[3], (D,), jnp.float32), 0.099609375, 1.8984375).astype(jnp.bfloat16),
        "gain_mix": jnp.clip(1.0 + 0.18 * jax.random.normal(keys[4], (D,), jnp.float32), 0.099609375, 1.8984375).astype(jnp.bfloat16),
        "w_qkv": gaussian(keys[5], (D, 3 * D), D ** -0.5, 0.25, ((0, 32),)),
        "w_out": gaussian(keys[6], (D, D), (D // 64) ** -0.5, 2.0, ((0, 32),)),
        "w_ctrl": gaussian(keys[7], (D, E), (4 * D) ** -0.5, 0.125, ((0, 32),)),
        "w_up": gaussian(keys[8], (E, D, FF), (D // 16) ** -0.5, 1.0, ((0, 4),)),
        "w_down": gaussian(keys[9], (E, FF, D), (max(FF // 256, 1)) ** -0.5, 2.0, ((0, 4),)),
        "cotangent": heavy_noise(keys[10], (TOKENS, D), 1.0, 6.0, ((0, 32),), (0, 1, 32, 2.75)),
    }


@jax.custom_vjp
def low(v):
    return lax.optimization_barrier(v.astype(jnp.bfloat16)).astype(jnp.float32)

@jax.custom_vjp
def low_back(v):
    return v

def low_keep(v):
    return (low(v), None)

def low_pass(kept, grad):
    return (grad,)

def back_keep(v):
    return (v, None)

def back_low(kept, grad):
    return (low(grad),)
low.defvjp(low_keep, low_pass)
low_back.defvjp(back_keep, back_low)
precise = lax.Precision.HIGHEST
eps_norm = 1e-05
masked_value = -1e+30

def rms_scale(values):
    return lax.rsqrt(lax.optimization_barrier(jnp.mean(values * values, axis=-1, keepdims=True)) + eps_norm)

def attend_block(pair):
    qkv_rows, length = pair
    queries = qkv_rows[:, :D].reshape(TOK_DEV, HEADS, HEAD)
    key_rows = qkv_rows[:, D:2 * D].reshape(TOK_DEV, HEADS, HEAD)
    value_rows = qkv_rows[:, 2 * D:].reshape(TOK_DEV, HEADS, HEAD)
    scores = jnp.einsum('qhd,khd->hqk', queries, key_rows, precision=precise) * HEAD ** (-0.5)
    scores = low_back(scores)
    positions = jnp.arange(TOK_DEV, dtype=jnp.int32)
    same_doc = positions[:, None] // length == positions[None, :] // length
    allowed = same_doc & (positions[None, :] <= positions[:, None])
    scores = jnp.where(allowed[None], scores, masked_value)
    peak_score = lax.optimization_barrier(jnp.max(scores, axis=-1, keepdims=True))
    exp_scores = jnp.exp(scores - peak_score)
    probs_low = low(exp_scores / lax.optimization_barrier(jnp.sum(exp_scores, axis=-1, keepdims=True)))
    mixed_rows = jnp.einsum('hqk,khd->qhd', probs_low, value_rows, precision=precise)
    return mixed_rows.reshape(TOK_DEV, D)

def expert_apply(triple):
    mixed_rows, up_matrix, down_matrix = triple
    pre_act = low_back(jnp.dot(mixed_rows, up_matrix, precision=precise))
    activated = low(jax.nn.gelu(pre_act, approximate=False))
    return low_back(low(jnp.dot(activated, down_matrix, precision=precise)))

def forward(tokens, gain_attn, gain_mix, w_qkv, w_out, w_ctrl, w_up, w_down, seq_lengths, group_map):
    device_count = TOKENS // TOK_DEV
    groups_all = TOKENS // G
    normed_one = low(tokens * rms_scale(tokens) * gain_attn)
    qkv = low_back(low(jnp.dot(normed_one, w_qkv, precision=precise)))
    attended = lax.map(jax.checkpoint(attend_block), (qkv.reshape(device_count, TOK_DEV, 3 * D), seq_lengths))
    attended = low_back(low(attended.reshape(TOKENS, D)))
    hidden = tokens + low_back(jnp.dot(attended, w_out, precision=precise))
    normed_two = low(hidden * rms_scale(hidden) * gain_mix)
    logits = low_back(jnp.dot(normed_two, w_ctrl, precision=precise))
    slot_tokens = (group_map + jnp.arange(device_count, dtype=jnp.int32)[:, None] * TOK_DEV).reshape(-1)
    token_slots = jnp.zeros((TOKENS,), jnp.int32).at[slot_tokens].set(jnp.arange(TOKENS, dtype=jnp.int32))
    slot_inputs = jnp.take(normed_two, slot_tokens, axis=0).reshape(groups_all, G, D)
    slot_logits = jnp.take(logits, slot_tokens, axis=0).reshape(groups_all, G, E)
    peak_logit = lax.optimization_barrier(jnp.max(slot_logits, axis=1, keepdims=True))
    exp_logits = jnp.exp(slot_logits - peak_logit)
    weights_low = low(exp_logits / lax.optimization_barrier(jnp.sum(exp_logits, axis=1, keepdims=True)))
    mixed = low_back(low(jnp.einsum('gte,gtd->egd', weights_low, slot_inputs, precision=precise)))
    produced = lax.map(jax.checkpoint(expert_apply), (mixed, w_up, w_down))
    combined = jnp.einsum('gte,egd->gtd', weights_low, produced, precision=precise).reshape(TOKENS, D)
    return hidden + low_back(jnp.take(combined, token_slots, axis=0))

def reference(tokens, seq_lengths, group_map, gain_attn, gain_mix, w_qkv, w_out, w_ctrl, w_up, w_down, cotangent):
    floats = [arr.astype(jnp.float32) for arr in (tokens, gain_attn, gain_mix, w_qkv, w_out, w_ctrl, w_up, w_down)]

    def closed(*params):
        return forward(*params, seq_lengths, group_map)
    output, pullback = jax.vjp(closed, *floats)
    gradients = pullback(cotangent.astype(jnp.float32))
    return (output.astype(jnp.bfloat16), gradients[0].astype(jnp.bfloat16), gradients[1], gradients[2], gradients[3], gradients[4], gradients[5], gradients[6], gradients[7])
```

```python
import functools

import jax
import jax.numpy as jnp
from jax import lax
from jax.experimental import pallas as pl
from jax.experimental.pallas import tpu as pltpu
from jax.sharding import PartitionSpec as P

HEADS = 8
G = 32
BQ = 256

eps_norm = 1e-05
masked_value = -1e30
bf16 = jnp.bfloat16
f32 = jnp.float32
NN = (((1,), (0,)), ((), ()))
NT = (((1,), (1,)), ((), ()))
TN = (((0,), (0,)), ((), ()))
VMEM_BYTES = 56 * 2**20


def dot(left, right, dims=NN):
    return lax.dot_general(left, right, dims, preferred_element_type=f32)


def rms_scale(values):
    return lax.rsqrt(jnp.mean(values * values, axis=-1, keepdims=True) + eps_norm)


def call(body, out_shape, args, cost, **extra):
    return pl.pallas_call(
        body,
        out_shape=out_shape,
        compiler_params=pltpu.CompilerParams(vmem_limit_bytes=VMEM_BYTES),
        cost_estimate=pl.CostEstimate(flops=cost[0], bytes_accessed=cost[1], transcendentals=cost[2]),
        **extra,
    )(*args)


def shape_of(dims, kind):
    return jax.ShapeDtypeStruct(dims, kind)


def prep_kernel(tok_ref, gmap_ref, unit_ref, gid_ref):
    rows = tok_ref.shape[0]
    step = 256
    for at in range(0, rows, step):
        block = tok_ref[at : at + step, :].astype(f32)
        unit_ref[at : at + step, :] = (block * rms_scale(block)).astype(bf16)
    groups = rows // G
    places = lax.broadcasted_iota(jnp.int32, (groups, rows), 1)
    group_at = lax.broadcasted_iota(jnp.int32, (groups, rows), 0)
    gmap = gmap_ref[...]
    member = jnp.zeros((groups, rows), jnp.int32)
    for slot in range(G):
        member = jnp.where(gmap[:, slot : slot + 1] == places, group_at, member)
    gid_ref[...] = jnp.sum(member.astype(f32), axis=0, keepdims=True).astype(jnp.int32)


def attend_kernel(len_ref, q_ref, k_ref, v_ref, out_ref, lse_ref, vt_ref):
    rows = q_ref.shape[0]
    lane = lax.broadcasted_iota(jnp.int32, (1, 128), 1) // 64
    vt_ref[...] = jnp.transpose(v_ref[...])

    def query_block(at, low):
        high = at + BQ
        queries = q_ref[at:high, :] * bf16(0.125)
        key_pos = lax.broadcasted_iota(jnp.int32, (BQ, BQ), 0)
        query_pos = lax.broadcasted_iota(jnp.int32, (BQ, BQ), 1)
        parts = []
        for head in range(2):
            own = jnp.where(lane == head, queries, bf16(0))
            near = jnp.where(key_pos <= query_pos, dot(k_ref[at:high, :], own, NT), masked_value)
            peak = jnp.max(near, axis=0, keepdims=True)
            if at > low:
                far = dot(k_ref[low:at, :], own, NT)
                peak = jnp.maximum(peak, jnp.max(far, axis=0, keepdims=True))
            near = jnp.exp(near - peak)
            total = jnp.sum(near, axis=0, keepdims=True)
            span = slice(64 * head, 64 * head + 64)
            mixed = dot(vt_ref[span, at:high], near.astype(bf16))
            if at > low:
                far = jnp.exp(far - peak)
                total = total + jnp.sum(far, axis=0, keepdims=True)
                mixed = mixed + dot(vt_ref[span, low:at], far.astype(bf16))
            parts.append(mixed * (1.0 / total))
            lse_ref[0, head : head + 1, at:high] = peak + jnp.log(total)
        out_ref[at:high, :] = jnp.transpose(jnp.concatenate(parts, 0)).astype(bf16)

    @pl.when(len_ref[0] == BQ)
    def _():
        for at in range(0, rows, BQ):
            query_block(at, at)

    @pl.when(len_ref[0] != BQ)
    def _():
        for at in range(0, rows, BQ):
            query_block(at, 0)


def attend_forward(qkv, length):
    rows, triple = qkv.shape
    width = triple // 3
    pairs = width // 128

    def part(offset):
        return pl.BlockSpec((rows, 128), lambda pair, _: (0, offset + pair))

    return call(
        attend_kernel,
        (shape_of((rows, width), bf16), shape_of((pairs, 2, rows), f32)),
        (length, qkv, qkv, qkv),
        (2 * rows * rows * width * 2, 8 * rows * width, rows * rows * HEADS // 2),
        grid_spec=pltpu.PrefetchScalarGridSpec(
            num_scalar_prefetch=1,
            grid=(pairs,),
            in_specs=[part(0), part(pairs), part(2 * pairs)],
            out_specs=[part(0), pl.BlockSpec((1, 2, rows), lambda pair, _: (pair, 0, 0))],
            scratch_shapes=[pltpu.VMEM((128, rows), bf16)],
        ),
    )


def attend_back_kernel(
    len_ref, q_ref, k_ref, v_ref, go_ref, o_ref, lse_ref, gq_ref, gk_ref, gv_ref, gqt_ref, kt_ref, dl_ref
):
    rows = q_ref.shape[0]
    step = 512
    lane = lax.broadcasted_iota(jnp.int32, (1, 128), 1) // 64
    kt_ref[...] = jnp.transpose(k_ref[...]) * bf16(0.125)
    product = jnp.transpose(go_ref[...].astype(f32) * o_ref[...].astype(f32))
    dl_ref[0:1, :] = jnp.sum(product[0:64], axis=0, keepdims=True)
    dl_ref[1:2, :] = jnp.sum(product[64:128], axis=0, keepdims=True)
    gqt_ref[...] = jnp.zeros_like(gqt_ref)

    def key_block(low, end):
        keys = k_ref[low : low + BQ, :] * bf16(0.125)
        vals = v_ref[low : low + BQ, :]
        grad_k = [None, None]
        grad_v = [None, None]
        spans = [(low, BQ)] + [(at, min(step, end - at)) for at in range(low + BQ, end, step)]
        for head in range(2):
            own_k = jnp.where(lane == head, keys, bf16(0))
            own_v = jnp.where(lane == head, vals, bf16(0))
            for at, wide in spans:
                here = slice(at, at + wide)
                probs = jnp.exp(dot(own_k, q_ref[here, :], NT) - lse_ref[0, head : head + 1, here])
                if at == low:
                    key_pos = lax.broadcasted_iota(jnp.int32, (BQ, BQ), 0)
                    query_pos = lax.broadcasted_iota(jnp.int32, (BQ, BQ), 1)
                    probs = jnp.where(key_pos <= query_pos, probs, 0.0)
                grad_probs = dot(own_v, go_ref[here, :], NT)
                grad_scores = (probs * (grad_probs - dl_ref[head : head + 1, here])).astype(bf16)
                more_v = dot(probs.astype(bf16), go_ref[here, :])
                more_k = dot(grad_scores, q_ref[here, :])
                grad_v[head] = more_v if grad_v[head] is None else grad_v[head] + more_v
                grad_k[head] = more_k if grad_k[head] is None else grad_k[head] + more_k
                span = slice(64 * head, 64 * head + 64)
                gqt_ref[span, here] += dot(kt_ref[span, low : low + BQ], grad_scores)
        gk_ref[low : low + BQ, :] = (jnp.where(lane == 0, grad_k[0], grad_k[1]) * 0.125).astype(bf16)
        gv_ref[low : low + BQ, :] = jnp.where(lane == 0, grad_v[0], grad_v[1]).astype(bf16)

    @pl.when(len_ref[0] == BQ)
    def _():
        for low in range(0, rows, BQ):
            key_block(low, low + BQ)

    @pl.when(len_ref[0] != BQ)
    def _():
        for low in range(0, rows, BQ):
            key_block(low, rows)

    gq_ref[...] = jnp.transpose(gqt_ref[...]).astype(bf16)


def attend_backward(qkv, attended, log_totals, grad_attended, length):
    rows, triple = qkv.shape
    width = triple // 3
    pairs = width // 128

    def part(offset):
        return pl.BlockSpec((rows, 128), lambda pair, _: (0, offset + pair))

    return call(
        attend_back_kernel,
        (shape_of((rows, width), bf16),) * 3,
        (length, qkv, qkv, qkv, grad_attended, attended, log_totals),
        (5 * rows * rows * width * 2, 16 * rows * width, rows * rows * HEADS // 2),
        grid_spec=pltpu.PrefetchScalarGridSpec(
            num_scalar_prefetch=1,
            grid=(pairs,),
            in_specs=[part(0), part(pairs), part(2 * pairs), part(0), part(0)]
            + [pl.BlockSpec((1, 2, rows), lambda pair, _: (pair, 0, 0))],
            out_specs=[part(0)] * 3,
            scratch_shapes=[pltpu.VMEM((128, rows), f32), pltpu.VMEM((128, rows), bf16), pltpu.VMEM((2, rows), f32)],
        ),
    )


def member_mask(gid_ref, groups, rows):
    return lax.broadcasted_iota(jnp.int32, (groups, rows), 0) == gid_ref[...]


def spread_weights(mask, wt_ref, w_ref):
    groups = mask.shape[0]
    for slot in range(wt_ref.shape[0]):
        wide = jnp.where(mask, wt_ref[slot : slot + 1, :], 0.0)
        w_ref[slot * groups : (slot + 1) * groups, :] = wide.astype(bf16)


def mix_kernel(
    tok_ref, att_ref, out_w_ref, gain_ref, ctrl_ref, gid_ref, cot_ref,
    hidden_ref, normed_ref, wt_ref, mixed_ref, grad_ref, w_ref,
):
    rows = tok_ref.shape[0]
    groups = rows // G
    step = 256
    for at in range(0, rows, step):
        here = slice(at, at + step)
        hidden = tok_ref[here, :].astype(f32) + dot(att_ref[here, :], out_w_ref[...])
        hidden_ref[here, :] = hidden
        normed_ref[here, :] = (hidden * rms_scale(hidden) * gain_ref[...]).astype(bf16)
    logits = dot(ctrl_ref[...], normed_ref[...], NT)
    mask = member_mask(gid_ref, groups, rows)
    for slot in range(logits.shape[0]):
        wide = jnp.where(mask, logits[slot : slot + 1, :], masked_value)
        wide = jnp.exp(wide - jnp.max(wide, axis=1, keepdims=True))
        wide = wide * (1.0 / jnp.sum(wide, axis=1, keepdims=True))
        wt_ref[slot : slot + 1, :] = jnp.sum(wide, axis=0, keepdims=True)
        w_ref[slot * groups : (slot + 1) * groups, :] = wide.astype(bf16)
    for at in range(0, w_ref.shape[0], step):
        here = slice(at, at + step)
        mixed_ref[here, :] = dot(w_ref[here, :], normed_ref[...]).astype(bf16)
        grad_ref[here, :] = dot(w_ref[here, :], cot_ref[...]).astype(bf16)


def combine_kernel(returned_ref, cot_ref, hidden_ref, wt_ref, gid_ref, out_ref, gw_ref, w_ref):
    rows = cot_ref.shape[0]
    groups = rows // G
    mask = member_mask(gid_ref, groups, rows)
    spread_weights(mask, wt_ref, w_ref)
    step = 256
    for at in range(0, rows, step):
        here = slice(at, at + step)
        combined = dot(w_ref[:, here], returned_ref[...], TN)
        out_ref[here, :] = (hidden_ref[here, :] + combined).astype(bf16)
    for slot in range(wt_ref.shape[0]):
        wide = dot(returned_ref[slot * groups : (slot + 1) * groups, :], cot_ref[...], NT)
        gw_ref[slot : slot + 1, :] = jnp.sum(jnp.where(mask, wide, 0.0), axis=0, keepdims=True)


def mix_back_kernel(
    gm_ref, cot_ref, normed_ref, hidden_ref, wt_ref, gw_ref, gid_ref, ctrl_ref, gain_ref, out_w_ref, att_ref,
    gh_ref, gatt_ref, gout_ref, gctrl_ref, w_ref, gl_ref, low_ref, gn_ref,
):
    rows, width = cot_ref.shape
    groups = rows // G
    experts = wt_ref.shape[0]
    mask = member_mask(gid_ref, groups, rows)
    spread_weights(mask, wt_ref, w_ref)
    for slot in range(experts):
        wide = dot(gm_ref[slot * groups : (slot + 1) * groups, :], normed_ref[...], NT)
        part = jnp.sum(jnp.where(mask, wide, 0.0), axis=0, keepdims=True) + gw_ref[slot : slot + 1, :]
        weight = wt_ref[slot : slot + 1, :]
        scaled = weight * part
        total = jnp.sum(jnp.where(mask, scaled, 0.0), axis=1, keepdims=True)
        back = jnp.sum(jnp.where(mask, total, 0.0), axis=0, keepdims=True)
        gl_ref[slot : slot + 1, :] = (scaled - weight * back).astype(bf16)
    gain = gain_ref[...]
    step = 256
    gain_total = jnp.zeros((1, width), f32)
    for at in range(0, rows, step):
        here = slice(at, at + step)
        grad_normed = dot(w_ref[:, here], gm_ref[...], TN) + dot(gl_ref[:, here], ctrl_ref[...], TN)
        hidden = hidden_ref[here, :]
        scale = rms_scale(hidden)
        unit = hidden * scale
        weighted = gain * grad_normed
        gain_total = gain_total + jnp.sum(grad_normed * unit, axis=0, keepdims=True)
        back = scale * (weighted - unit * jnp.mean(weighted * unit, axis=-1, keepdims=True))
        grad_hidden = cot_ref[here, :].astype(f32) + back
        gh_ref[here, :] = grad_hidden
        low = grad_hidden.astype(bf16)
        low_ref[here, :] = low
        gatt_ref[here, :] = dot(low, out_w_ref[...], NT).astype(bf16)
    gout_ref[...] = dot(att_ref[...], low_ref[...], TN).astype(bf16)
    small = [dot(gl_ref[...], normed_ref[...]), gain_total, jnp.zeros((127 - experts, width), f32)]
    gctrl_ref[...] = jnp.transpose(jnp.concatenate(small, 0)).astype(bf16)


def expert_kernel(pick_ref, in_ref, up_ref, down_ref, act_ref, slope_ref, out_ref, total_ref):
    step = 256
    first = pl.program_id(0) == 0
    last = pl.program_id(0) == pl.num_programs(0) - 1

    @pl.when(first)
    def _():
        total_ref[...] = jnp.zeros_like(total_ref)

    for at in range(0, in_ref.shape[0], step):
        here = slice(at, at + step)
        pre = dot(in_ref[here, :], up_ref[0])
        cdf = 0.5 + 0.5 * lax.erf(pre * 0.7071067811865476)
        density = jnp.exp(-0.5 * pre * pre) * 0.3989422804014327
        act = (pre * cdf).astype(bf16)
        act_ref[here, :] = act
        slope_ref[here, :] = (cdf + pre * density).astype(bf16)
        total_ref[here, :] += dot(act, down_ref[0])

    @pl.when(last)
    def _():
        out_ref[...] = total_ref[...].astype(bf16)


def expert_back_kernel(
    pick_ref, gp_ref, in_ref, act_ref, slope_ref, up_ref, down_ref, gup_ref, gdown_ref, out_ref, total_ref, pre_ref
):
    step = 256
    first = pl.program_id(0) == 0
    last = pl.program_id(0) == pl.num_programs(0) - 1

    @pl.when(first)
    def _():
        total_ref[...] = jnp.zeros_like(total_ref)

    gdown_ref[...] = dot(act_ref[...], gp_ref[...], TN).astype(bf16)
    for at in range(0, in_ref.shape[0], step):
        here = slice(at, at + step)
        grad_act = dot(gp_ref[here, :], down_ref[0], NT)
        grad_pre = (grad_act * slope_ref[here, :].astype(f32)).astype(bf16)
        pre_ref[here, :] = grad_pre
        total_ref[here, :] += dot(grad_pre, up_ref[0], NT)
    gup_ref[...] = dot(in_ref[...], pre_ref[...], TN).astype(bf16)

    @pl.when(last)
    def _():
        out_ref[...] = total_ref[...].astype(bf16)


def expert_specs(rows, width, hidden, step):
    whole = pl.BlockSpec((rows, width), lambda at, _: (0, 0))
    slab = pl.BlockSpec((rows, step), lambda at, _: (0, at))
    up = pl.BlockSpec((1, width, step), lambda at, pick: (pick[0], 0, at))
    down = pl.BlockSpec((1, step, width), lambda at, pick: (pick[0], at, 0))
    return whole, slab, up, down


def expert_forward(pick, arrived, w_up, w_down):
    rows, width = arrived.shape
    hidden = w_up.shape[2]
    step = 512
    whole, slab, up, down = expert_specs(rows, width, hidden, step)
    return call(
        expert_kernel,
        (shape_of((rows, hidden), bf16), shape_of((rows, hidden), bf16), shape_of((rows, width), bf16)),
        (pick, arrived, w_up, w_down),
        (4 * rows * width * hidden, 4 * rows * hidden + 4 * width * hidden + 4 * rows * width, 2 * rows * hidden),
        grid_spec=pltpu.PrefetchScalarGridSpec(
            num_scalar_prefetch=1,
            grid=(hidden // step,),
            in_specs=[whole, up, down],
            out_specs=[slab, slab, whole],
            scratch_shapes=[pltpu.VMEM((rows, width), f32)],
        ),
    )


def expert_backward(pick, grad_produced, arrived, act, slope, w_up, w_down):
    rows, width = arrived.shape
    hidden = w_up.shape[2]
    step = 512
    whole, slab, up, down = expert_specs(rows, width, hidden, step)
    return call(
        expert_back_kernel,
        (shape_of((width, hidden), bf16), shape_of((hidden, width), bf16), shape_of((rows, width), bf16)),
        (pick, grad_produced, arrived, act, slope, w_up, w_down),
        (8 * rows * width * hidden, 4 * rows * hidden + 8 * width * hidden + 6 * rows * width, 0),
        grid_spec=pltpu.PrefetchScalarGridSpec(
            num_scalar_prefetch=1,
            grid=(hidden // step,),
            in_specs=[whole, whole, slab, slab, up, down],
            out_specs=[
                pl.BlockSpec((width, step), lambda at, _: (0, at)),
                pl.BlockSpec((step, width), lambda at, _: (at, 0)),
                whole,
            ],
            scratch_shapes=[pltpu.VMEM((rows, width), f32), pltpu.VMEM((rows, step), bf16)],
        ),
    )


def project_kernel(unit_ref, w_ref, out_ref):
    out_ref[...] = dot(unit_ref[...], w_ref[...]).astype(bf16)


def project(unit, weights):
    rows, width = unit.shape
    wide = weights.shape[1]
    step = 512
    return call(
        project_kernel,
        shape_of((rows, wide), bf16),
        (unit, weights),
        (2 * rows * width * wide, 2 * (rows * width + rows * wide + width * wide), 0),
        grid=(rows // step,),
        in_specs=[pl.BlockSpec((step, width), lambda at: (at, 0)), pl.BlockSpec((width, wide), lambda at: (0, 0))],
        out_specs=pl.BlockSpec((step, wide), lambda at: (at, 0)),
    )


def weight_grad_kernel(unit_ref, gq_ref, gk_ref, gv_ref, out_ref):
    width = unit_ref.shape[1]
    for at, ref in enumerate((gq_ref, gk_ref, gv_ref)):
        out_ref[:, at * width : (at + 1) * width] = dot(unit_ref[...], ref[...], TN).astype(bf16)


def token_grad_kernel(gq_ref, gk_ref, gv_ref, w_ref, tok_ref, gh_ref, out_ref):
    width = tok_ref.shape[1]
    weighted = dot(gq_ref[...], w_ref[:, :width], NT)
    weighted = weighted + dot(gk_ref[...], w_ref[:, width : 2 * width], NT)
    weighted = weighted + dot(gv_ref[...], w_ref[:, 2 * width :], NT)
    source = tok_ref[...].astype(f32)
    scale = rms_scale(source)
    unit = source * scale
    back = scale * (weighted - unit * jnp.mean(weighted * unit, axis=-1, keepdims=True))
    out_ref[...] = (gh_ref[...] + back).astype(bf16)


def token_grad(grads, weights, tokens, grad_hidden):
    rows, width = tokens.shape
    step = 512
    block = pl.BlockSpec((step, width), lambda at: (at, 0))
    return call(
        token_grad_kernel,
        shape_of((rows, width), bf16),
        (*grads, weights, tokens, grad_hidden),
        (6 * rows * width * width, 14 * rows * width, 0),
        grid=(rows // step,),
        in_specs=[block] * 3 + [pl.BlockSpec(weights.shape, lambda at: (0, 0)), block, block],
        out_specs=block,
    )


def swap(array, axis, size, bit):
    return lax.ppermute(array, axis, [(at, at ^ bit) for at in range(size)])


def axis_bits(sizes):
    bits = []
    for axis, size in sizes:
        bit = size // 2
        while bit:
            bits.append((axis, size, bit))
            bit //= 2
    return bits


def gather_rows(shard, sizes):
    rows = shard.shape[0]
    total = rows
    for _, size in sizes:
        total *= size
    bits = axis_bits(sizes)
    held = shard[(None,) * len(bits)]
    for place in range(len(bits)):
        axis, size, bit = bits[place]
        other = swap(held, axis, size, bit)
        upper = (lax.axis_index(axis) // bit) % 2 == 1
        first = jnp.where(upper, other, held)
        second = jnp.where(upper, held, other)
        held = jnp.concatenate([first, second], axis=place)
    return held.reshape((total,) + shard.shape[1:])


def scatter_rows(whole, sizes, order):
    bits = axis_bits(sizes)
    devices = 2 ** len(bits)
    held = whole.reshape((2,) * len(bits) + (whole.shape[0] // devices,) + whole.shape[1:])
    left = list(range(len(bits)))
    for which in order:
        axis, size, bit = bits[which]
        place = left.index(which)
        mine = (lax.axis_index(axis) // bit) % 2
        keep = lax.dynamic_index_in_dim(held, mine, place, keepdims=False)
        send = lax.dynamic_index_in_dim(held, 1 - mine, place, keepdims=False)
        got = swap(send, axis, size, bit)
        held = keep.astype(f32) + got.astype(f32)
        left.pop(place)
        if left:
            held = held.astype(bf16)
    return held


def expert_grad_shard(grad, n_dp, per_owner):
    parts = n_dp // per_owner
    dp = lax.axis_index("dp")
    part, low = dp // per_owner, dp % per_owner
    rows = grad.shape[0] // parts
    total = lax.dynamic_slice_in_dim(grad, part * rows, rows, 0).astype(f32)
    for other in range(1, parts):
        away = lax.dynamic_slice_in_dim(grad, (part ^ other) * rows, rows, 0)
        total = total + swap(away, "dp", n_dp, other * per_owner).astype(f32)
    total = total.astype(bf16)
    rows //= per_owner
    groups = [[at * per_owner + own for own in range(per_owner)] for at in range(parts)]
    split = total.reshape((per_owner, rows) + grad.shape[1:])
    return lax.all_to_all(
        split, "dp", split_axis=0, concat_axis=0, axis_index_groups=groups, tiled=True
    ).astype(f32)


def on_device(
    n_dp, n_owner, tokens, seq_lengths, group_map, gain_attn, gain_mix, w_qkv, w_out, w_ctrl, w_up, w_down, cotangent
):
    rows, width = tokens.shape
    experts = w_ctrl.shape[1]
    per_owner = w_up.shape[0]
    groups = rows // G
    parts = n_dp // per_owner
    sizes = (("dp", n_dp), ("expert", n_owner))
    pick = (lax.axis_index("dp") % per_owner).astype(jnp.int32).reshape(1)

    gained = (w_qkv.astype(f32) * gain_attn.astype(f32)[:, None]).astype(bf16)
    qkv_w = gather_rows(gained, sizes)
    ctrl_slots = w_ctrl.reshape(-1, n_owner, per_owner).swapaxes(1, 2).reshape(-1, experts)
    pad = jnp.zeros((w_ctrl.shape[0], 127 - experts), bf16)
    late = gather_rows(jnp.concatenate([w_out, ctrl_slots, gain_mix[:, None], pad], 1), sizes)
    out_w = late[:, :width]
    small_t = late[:, width:].T
    ctrl_t = small_t[:experts]
    gain_two = small_t[experts : experts + 1].astype(f32)

    unit_one, gid = call(
        prep_kernel,
        (shape_of((rows, width), bf16), shape_of((1, rows), jnp.int32)),
        (tokens, group_map.reshape(groups, G)),
        (0, 4 * rows * width, 0),
    )
    qkv = project(unit_one, qkv_w)
    attended, log_totals = attend_forward(qkv, seq_lengths)

    slot_rows = experts * groups
    hidden, normed_two, weights, mixed, grad_returned = call(
        mix_kernel,
        (
            shape_of((rows, width), f32),
            shape_of((rows, width), bf16),
            shape_of((experts, rows), f32),
            shape_of((slot_rows, width), bf16),
            shape_of((slot_rows, width), bf16),
        ),
        (tokens, attended, out_w, gain_two, ctrl_t, gid, cotangent),
        (4 * slot_rows * rows * width + 2 * rows * width * width, 14 * rows * width, slot_rows * rows),
        scratch_shapes=[pltpu.VMEM((slot_rows, rows), bf16)],
    )

    teams = [
        [(part * per_owner + low) * n_owner + owner for low in range(per_owner) for owner in range(n_owner)]
        for part in range(parts)
    ]

    def exchange(array):
        split = array.reshape(experts, groups, width)
        moved = lax.all_to_all(
            split, ("dp", "expert"), split_axis=0, concat_axis=0, axis_index_groups=teams, tiled=True
        )
        return moved.reshape(slot_rows, width)

    arrived = exchange(mixed)
    grad_produced = exchange(grad_returned)
    act, slope, produced = expert_forward(pick, arrived, w_up, w_down)
    returned = exchange(produced)
    grad_up, grad_down, grad_arrived = expert_backward(pick, grad_produced, arrived, act, slope, w_up, w_down)
    grad_mixed = exchange(grad_arrived)
    grad_up_shard = expert_grad_shard(grad_up, n_dp, per_owner)
    grad_down_shard = expert_grad_shard(grad_down, n_dp, per_owner)

    output, grad_weights = call(
        combine_kernel,
        (shape_of((rows, width), bf16), shape_of((experts, rows), f32)),
        (returned, cotangent, hidden, weights, gid),
        (4 * slot_rows * rows * width, 10 * rows * width, 0),
        scratch_shapes=[pltpu.VMEM((slot_rows, rows), bf16)],
    )
    grad_hidden, grad_attended, grad_out, grad_small = call(
        mix_back_kernel,
        (
            shape_of((rows, width), f32),
            shape_of((rows, width), bf16),
            shape_of((width, width), bf16),
            shape_of((width, 128), bf16),
        ),
        (
            grad_mixed, cotangent, normed_two, hidden, weights, grad_weights, gid, ctrl_t, gain_two, out_w, attended
        ),
        (4 * slot_rows * rows * width + 4 * rows * width * width, 18 * rows * width, 0),
        scratch_shapes=[
            pltpu.VMEM((slot_rows, rows), bf16),
            pltpu.VMEM((experts, rows), bf16),
            pltpu.VMEM((rows, width), bf16),
            pltpu.VMEM((8, 128), f32),
        ],
    )
    order = list(range(len(axis_bits(sizes))))[::-1]
    early = scatter_rows(jnp.concatenate([grad_out, grad_small], 1), sizes, order)

    grads = attend_backward(qkv, attended, log_totals, grad_attended, seq_lengths)
    grad_w = call(
        weight_grad_kernel,
        shape_of((width, 3 * width), bf16),
        (unit_one, *grads),
        (6 * rows * width * width, 8 * rows * width, 0),
    )
    grad_tokens = token_grad(grads, qkv_w, tokens, grad_hidden)
    grad_w_shard = scatter_rows(grad_w, sizes, order)
    shard_qkv = gain_attn.astype(f32)[:, None] * grad_w_shard
    shard_gain_one = jnp.sum(w_qkv.astype(f32) * grad_w_shard, axis=1)
    shard_ctrl = early[:, width : width + experts]
    shard_ctrl = shard_ctrl.reshape(-1, per_owner, n_owner).swapaxes(1, 2).reshape(-1, experts)
    return (
        output,
        grad_tokens,
        shard_gain_one,
        early[:, width + experts],
        shard_qkv,
        early[:, :width],
        shard_ctrl,
        grad_up_shard,
        grad_down_shard,
    )


def solution(mesh):
    both = ("dp", "expert")
    rows = P(both, None)
    return jax.shard_map(
        functools.partial(on_device, mesh.shape["dp"], mesh.shape["expert"]),
        mesh=mesh,
        in_specs=(
            rows, P(both), rows, P(both), P(both), rows, rows, rows,
            P("expert", None, None), P("expert", None, None), rows,
        ),
        out_specs=(
            rows, rows, P(both), P(both), rows, rows, rows,
            P("expert", "dp", None), P("expert", "dp", None),
        ),
        check_vma=False,
    )
```

```python
import functools

import jax
import jax.numpy as jnp
from jax import lax
from jax.experimental import pallas as pl
from jax.experimental.pallas import tpu as pltpu
from jax.sharding import PartitionSpec as P

HEADS = 8
G = 32
BQ = 256

ANY = pl.BlockSpec(memory_space=pl.ANY)
VMEM = pl.BlockSpec(memory_space=pltpu.VMEM)
HBM = pl.BlockSpec(memory_space=pltpu.HBM)
DMA = pltpu.SemaphoreType.DMA
SMEM = pl.BlockSpec(memory_space=pltpu.SMEM)

eps_norm = 1e-05
masked_value = -1e30
bf16 = jnp.bfloat16
f32 = jnp.float32
NN = (((1,), (0,)), ((), ()))
NT = (((1,), (1,)), ((), ()))
TN = (((0,), (0,)), ((), ()))


def dot(left, right, dims=NN):
    return lax.dot_general(left, right, dims, preferred_element_type=f32)


def rms_scale(values):
    return lax.rsqrt(jnp.mean(values * values, axis=-1, keepdims=True) + eps_norm)


def call(body, out_shape, args, room=28, **extra):
    return pl.pallas_call(
        body,
        out_shape=out_shape,
        compiler_params=pltpu.CompilerParams(vmem_limit_bytes=room * 2**20),
        name=getattr(body, "func", body).__name__,
        **extra,
    )(*args)


def shape_of(dims, kind):
    return jax.ShapeDtypeStruct(dims, kind)


def in_hbm(dims, kind):
    return pltpu.HBM(dims, kind)


def in_vmem(dims, kind):
    return pltpu.VMEM(dims, kind)


def from_hbm(array):
    return pltpu.with_memory_space_constraint(array, pltpu.HBM)


def room_for(parts, rows):
    fixed, per_block = parts
    return fixed + per_block * rows // 1024


def push(source, target, sem):
    copy = pltpu.make_async_copy(source, target, sem)
    copy.start()
    return copy


MARK = (8, 128)


def set_mark(ref):
    ref[...] = jnp.zeros(MARK, f32)


def prep_kernel(tok_ref, gmap_ref, kept_ref, kept_t_ref, gid_ref, unit_ref, unit_t_ref, sems):
    rows = tok_ref.shape[0]
    step = 256
    for at in range(0, rows, step):
        block = tok_ref[at : at + step, :].astype(f32)
        unit = (block * rms_scale(block)).astype(bf16)
        unit_ref[at : at + step, :] = unit
        unit_t_ref[:, at : at + step] = jnp.transpose(unit)
    copies = [push(unit_ref, kept_ref, sems.at[0]), push(unit_t_ref, kept_t_ref, sems.at[1])]
    groups = rows // G
    places = lax.broadcasted_iota(jnp.int32, (groups, rows), 1)
    group_at = lax.broadcasted_iota(jnp.int32, (groups, rows), 0)
    gmap = gmap_ref[...]
    member = jnp.zeros((groups, rows), jnp.int32)
    for slot in range(G):
        member = jnp.where(gmap[:, slot : slot + 1] == places, group_at, member)
    gid_ref[...] = jnp.sum(member.astype(f32), axis=0, keepdims=True).astype(jnp.int32)
    for copy in copies:
        copy.wait()


def lower_mask():
    return lax.broadcasted_iota(jnp.int32, (BQ, BQ), 0) <= lax.broadcasted_iota(jnp.int32, (BQ, BQ), 1)


def head_lanes():
    return lax.broadcasted_iota(jnp.int32, (1, 128), 1) // 64


def attend_pair(length, pair, qkv_all_ref, out_all_ref, lse_all_ref, vt_ref):
    qkv_ref = qkv_all_ref.at[:, pl.ds(pl.multiple_of(pair * 384, 384), 384)]
    out_ref = out_all_ref.at[:, pl.ds(pl.multiple_of(pair * 128, 128), 128)]
    lse_ref = lse_all_ref.at[pl.ds(pair, 1)]
    rows = qkv_ref.shape[0]
    step, ahead = 512, 4
    lane = head_lanes()
    vt_ref[...] = jnp.transpose(qkv_ref[:, 256:384])

    def run(low_of):
        items = []
        for at in range(0, rows, BQ):
            chunks = [(at, BQ)]
            top = at
            while top > low_of(at):
                down = max(low_of(at), top - step)
                chunks.append((down, top - down))
                top = down
            for place, (low, wide) in enumerate(chunks):
                for head in range(2):
                    items.append((at, head, low, wide, place == 0, place == len(chunks) - 1))

        def score(at, head, low, wide, first, last):
            own = jnp.where(lane == head, qkv_ref[at : at + BQ, 0:128] * bf16(0.125), bf16(0))
            scores = dot(qkv_ref[low : low + wide, 128:256], own, NT)
            return jnp.where(lower_mask(), scores, masked_value) if first else scores

        pending = [score(*item) for item in items[:ahead]]
        state = {}
        for place, (at, head, low, wide, first, last) in enumerate(items):
            if place + ahead < len(items):
                pending.append(score(*items[place + ahead]))
            scores = pending.pop(0)
            peak = jnp.max(scores, axis=0, keepdims=True)
            if not first:
                old_peak, old_total, old_mixed = state[head]
                peak = jnp.maximum(old_peak, peak)
                shrink = jnp.exp(old_peak - peak)
            probs = jnp.exp(scores - peak)
            total = jnp.sum(probs, axis=0, keepdims=True)
            mixed = dot(vt_ref[64 * head : 64 * head + 64, low : low + wide], probs.astype(bf16))
            if not first:
                total = total + old_total * shrink
                mixed = mixed + old_mixed * shrink
            state[head] = (peak, total, mixed)
            if last:
                lse_ref[0, head : head + 1, at : at + BQ] = peak + jnp.log(total)
                if head == 1:
                    both = [state[own][2] * (1.0 / state[own][1]) for own in range(2)]
                    out_ref[at : at + BQ, :] = jnp.transpose(jnp.concatenate(both, 0)).astype(bf16)

    @pl.when(length == BQ)
    def _():
        run(lambda at: at)

    @pl.when(length != BQ)
    def _():
        run(lambda at: 0)


def attend_pairs(len_ref, qkv_ref, out_ref, lse_ref, kept_qkv_ref, kept_out_ref, vt_ref, sems):
    copy = push(qkv_ref, kept_qkv_ref, sems.at[0])

    @pl.loop(0, qkv_ref.shape[1] // 384)
    def _(pair):
        attend_pair(len_ref[0], pair, qkv_ref, out_ref, lse_ref, vt_ref)

    copy.wait()
    push(out_ref, kept_out_ref, sems.at[1]).wait()


def attend_kernel(len_ref, qkv_ref, hint_ref, out_ref, lse_ref, kept_qkv_ref, kept_out_ref, vt_ref, sems):
    attend_pairs(len_ref, qkv_ref, out_ref, lse_ref, kept_qkv_ref, kept_out_ref, vt_ref, sems)


def project_attend_kernel(
    len_ref, kept_ref, w_ref, out_ref, lse_ref, kept_qkv_ref, kept_out_ref, vt_ref, sems, qkv_ref, unit_ref, unit_sems
):
    load_project(kept_ref, w_ref, qkv_ref, 0, unit_ref, unit_sems)
    attend_pairs(len_ref, qkv_ref, out_ref, lse_ref, kept_qkv_ref, kept_out_ref, vt_ref, sems)


def attend_shapes(rows, pairs):
    return dict(
        out_shape=(
            shape_of((rows, 128 * pairs), bf16),
            shape_of((pairs, 2, rows), f32),
            in_hbm((rows, 384 * pairs), bf16),
            in_hbm((rows, 128 * pairs), bf16),
        ),
        room=ATTEND_ROOM,
        out_specs=[VMEM, VMEM, HBM, HBM],
    )


def attend_forward(length, qkv, hint):
    rows = qkv.shape[0]
    return call(
        attend_kernel,
        args=(length, qkv, hint),
        in_specs=[SMEM, VMEM, ANY],
        scratch_shapes=[pltpu.VMEM((128, rows), bf16), DMA((2,))],
        **attend_shapes(rows, qkv.shape[1] // 384),
    )


def project_attend(length, unit, weights, pairs):
    rows = unit.shape[0]
    return call(
        project_attend_kernel,
        args=(length, from_hbm(unit), weights),
        in_specs=[SMEM, HBM, VMEM],
        scratch_shapes=[
            pltpu.VMEM((128, rows), bf16),
            DMA((2,)),
            pltpu.VMEM((rows, 384 * pairs), bf16),
            pltpu.VMEM(unit.shape, bf16),
            DMA((4,)),
        ],
        **attend_shapes(rows, pairs),
    )


def attend_back_kernel(len_ref, qkv_ref, go_ref, o_ref, lse_ref, hint_ref, grad_ref, *scratch):
    @pl.loop(0, qkv_ref.shape[1] // 384)
    def _(pair):
        wide = pl.ds(pl.multiple_of(pair * 384, 384), 384)
        thin = pl.ds(pl.multiple_of(pair * 128, 128), 128)
        refs = [qkv_ref.at[:, wide], go_ref.at[:, thin], o_ref.at[:, thin], lse_ref.at[pl.ds(pair, 1)]]
        attend_back_pair(len_ref, *refs, grad_ref.at[:, wide], *scratch)


def attend_back_pair(len_ref, qkv_ref, go_ref, o_ref, lse_ref, grad_ref, gqt_ref, kt_ref, dl_ref):
    rows = qkv_ref.shape[0]
    step, ahead = 512, 1
    lane = head_lanes()
    kt_ref[...] = jnp.transpose(qkv_ref[:, 128:256]) * bf16(0.125)
    product = jnp.transpose(go_ref[...].astype(f32) * o_ref[...].astype(f32))
    dl_ref[0:1, :] = jnp.sum(product[0:64], axis=0, keepdims=True)
    dl_ref[1:2, :] = jnp.sum(product[64:128], axis=0, keepdims=True)

    def run(end_of):
        items = []
        for low in range(0, rows, BQ):
            end = end_of(low)
            chunks = [(low, BQ)] + [(at, min(step, end - at)) for at in range(low + BQ, end, step)]
            for place, (at, wide) in enumerate(chunks):
                for head in range(2):
                    items.append((low, head, at, wide, place == 0, place == len(chunks) - 1))
        blocks = {}
        written = set()

        def products(low, head, at, wide, first, last):
            if (low, head) not in blocks:
                keys = qkv_ref[low : low + BQ, 128:256] * bf16(0.125)
                vals = qkv_ref[low : low + BQ, 256:384]
                blocks[low, head] = [jnp.where(lane == head, own, bf16(0)) for own in (keys, vals)]
            keys, vals = blocks[low, head]
            return (
                dot(keys, qkv_ref[at : at + wide, 0:128], NT),
                dot(vals, go_ref[at : at + wide, :], NT),
            )

        pending = [products(*item) for item in items[:ahead]]
        grad_k, grad_v = {}, {}
        for place, (low, head, at, wide, first, last) in enumerate(items):
            if place + ahead < len(items):
                pending.append(products(*items[place + ahead]))
            scores, grad_probs = pending.pop(0)
            here = slice(at, at + wide)
            probs = jnp.exp(scores - lse_ref[0, head : head + 1, here])
            if first:
                probs = jnp.where(lower_mask(), probs, 0.0)
            grad_scores = (probs * (grad_probs - dl_ref[head : head + 1, here])).astype(bf16)
            more_v = dot(probs.astype(bf16), go_ref[here, :])
            more_k = dot(grad_scores, qkv_ref[here, 0:128])
            grad_v[head] = more_v if first else grad_v[head] + more_v
            grad_k[head] = more_k if first else grad_k[head] + more_k
            span = slice(64 * head, 64 * head + 64)
            more_q = dot(kt_ref[span, low : low + BQ], grad_scores)
            fresh = (head, at + wide) not in written
            written.update((head, top) for top in range(at + BQ, at + wide + BQ, BQ))
            if fresh:
                gqt_ref[span, here] = more_q
            else:
                gqt_ref[span, here] += more_q
            if last and head == 1:
                there = slice(low, low + BQ)
                grad_ref[there, 128:256] = (jnp.where(lane == 0, grad_k[0], grad_k[1]) * 0.125).astype(bf16)
                grad_ref[there, 256:384] = jnp.where(lane == 0, grad_v[0], grad_v[1]).astype(bf16)

    @pl.when(len_ref[0] == BQ)
    def _():
        run(lambda low: low + BQ)

    @pl.when(len_ref[0] != BQ)
    def _():
        run(lambda low: rows)

    grad_ref[:, 0:128] = jnp.transpose(gqt_ref[...]).astype(bf16)


def attend_backward(length, qkv, grad_attended, attended, log_totals, hint):
    rows = qkv.shape[0]
    return call(
        attend_back_kernel,
        shape_of(qkv.shape, bf16),
        (length, qkv, grad_attended, attended, log_totals, hint),
        room=ATTEND_ROOM,
        in_specs=[SMEM, VMEM, VMEM, VMEM, VMEM, ANY],
        out_specs=VMEM,
        scratch_shapes=[pltpu.VMEM((128, rows), f32), pltpu.VMEM((128, rows), bf16), pltpu.VMEM((2, rows), f32)],
    )


STEP = 512
UNMIX_ROOM = (24, 12)
MIX_ROOM = (12, 12)
ATTEND_ROOM = 24
EXPERT_ROOM = (20, 16)
GRAD_ROOM = (16, 20)
EXPERT_ROWS = 512
MIX_ROWS = 1024


def member_mask(gid_ref, groups):
    wide = gid_ref.shape[1]
    return lax.broadcasted_iota(jnp.int32, (groups, wide), 0) == gid_ref[...]


def mix_kernel(
    tok_ref, own_ref, away_ref, w_all_ref, gid_ref, cot_ref,
    kept_hidden_ref, wt_ref, sent_ref, kept_away_ref, normed_ref, w_ref, hidden_ref, mixed_ref, sems,
):
    copies = [push(away_ref, kept_away_ref, sems.at[0])]
    rows, width = tok_ref.shape
    experts, _, groups, _ = mixed_ref.shape
    half = width // 2
    out_w = w_all_ref[:, 3 * width : 4 * width]
    small = jnp.transpose(w_all_ref[:, 4 * width :])
    gain = small[experts : experts + 1, :].astype(f32)
    for at in range(0, rows, 512):
        here = slice(at, at + 512)
        hidden = tok_ref[here, :].astype(f32) + dot(own_ref[here, :], out_w[:half])
        hidden = (hidden + dot(away_ref[here, :], out_w[half:])).astype(bf16)
        hidden_ref[here, :] = hidden
        hidden = hidden.astype(f32)
        normed_ref[here, :] = (hidden * rms_scale(hidden) * gain).astype(bf16)
    copies.append(push(hidden_ref, kept_hidden_ref, sems.at[1]))
    logits = dot(small[:experts], normed_ref[...], NT)
    mask = member_mask(gid_ref, groups)
    for slot in range(experts):
        wide = jnp.where(mask, logits[slot : slot + 1, :], masked_value)
        wide = jnp.exp(wide - jnp.max(wide, axis=1, keepdims=True))
        wide = wide * (1.0 / jnp.sum(wide, axis=1, keepdims=True))
        wt_ref[slot : slot + 1, :] = jnp.sum(wide, axis=0, keepdims=True)
        w_ref[slot * groups : (slot + 1) * groups, :] = wide.astype(bf16)
    many = min(MIX_ROWS // groups, experts)
    for place, ref in enumerate((normed_ref, cot_ref)):
        for slot in range(0, experts, many):
            mixed = dot(w_ref[slot * groups : (slot + many) * groups, :], ref[...]).astype(bf16)
            mixed_ref[slot : slot + many, place] = mixed.reshape(many, groups, width)
        copies.append(push(mixed_ref.at[:, place], sent_ref.at[:, place], sems.at[2 + place]))
    for copy in copies:
        copy.wait()


def mix(tokens, att_own, att_away, gathered, gid, cotangent, experts):
    rows, width = tokens.shape
    groups = rows // G
    sent = (experts, 2, groups, width)
    return call(
        mix_kernel,
        (
            in_hbm((rows, width), bf16),
            shape_of((experts, rows), f32),
            in_hbm(sent, bf16),
            in_hbm(att_away.shape, bf16),
        ),
        (tokens, att_own, att_away, gathered, gid, cotangent),
        room=room_for(MIX_ROOM, experts * groups),
        in_specs=[VMEM] * 6,
        out_specs=[HBM, VMEM, HBM, HBM],
        scratch_shapes=[
            pltpu.VMEM((rows, width), bf16),
            pltpu.VMEM((experts * groups, rows), bf16),
            pltpu.VMEM((rows, width), bf16),
            pltpu.VMEM(sent, bf16),
            DMA((4,)),
        ],
    )


def turn_kernel(wt_ref, gid_ref, kept_ref, mark_ref, turned_ref, sem):
    set_mark(mark_ref)
    experts, rows = wt_ref.shape
    groups = turned_ref.shape[1] // experts
    many = 256 // groups
    for at in range(0, rows, STEP):
        here = slice(at, at + STEP)
        mask = lax.broadcasted_iota(jnp.int32, (groups, STEP), 0) == gid_ref[:, here]
        for slot in range(0, experts, many):
            parts = [
                jnp.where(mask, wt_ref[own : own + 1, here], 0.0).astype(bf16) for own in range(slot, slot + many)
            ]
            turned_ref[here, slot * groups : (slot + many) * groups] = jnp.transpose(jnp.concatenate(parts, 0))
    push(turned_ref, kept_ref, sem).wait()


def turn(weights, gid, groups):
    experts, rows = weights.shape
    return call(
        turn_kernel,
        (in_hbm((rows, experts * groups), bf16), shape_of(MARK, f32)),
        (weights, gid),
        room=16,
        in_specs=[VMEM] * 2,
        out_specs=[HBM, VMEM],
        scratch_shapes=[pltpu.VMEM((rows, experts * groups), bf16), DMA],
    )


def unmix_kernel(
    back_ref, wt_ref, gid_ref, w_all_ref, kept_turned_ref, kept_cot_ref, kept_hidden_ref, kept_own_ref, kept_away_ref,
    kept_out_ref, kept_gh_ref, gown_ref, gaway_ref, small_ref,
    turned_ref, cot_ref, hidden_ref, own_ref, away_ref, normed_ref, part_ref, total_ref, gl_ref, sems,
):
    experts, _, groups, width = back_ref.shape
    rows = cot_ref.shape[0]
    half = width // 2
    many = min(MIX_ROWS // groups, experts)
    blocks = [slice(at, at + STEP) for at in range(0, rows, STEP)]
    sources = (kept_cot_ref, kept_hidden_ref, kept_turned_ref)
    targets = (cot_ref, hidden_ref, turned_ref)
    arriving = {}

    def load(kinds, at):
        for kind in kinds:
            here = blocks[at]
            arriving[kind, at] = push(sources[kind].at[here], targets[kind].at[here], sems.at[kind, at])

    load((0, 1), 0)
    out_w = w_all_ref[:, 3 * width : 4 * width]
    small = jnp.transpose(w_all_ref[:, 4 * width :])
    gain = small[experts : experts + 1, :].astype(f32)
    total_ref[...] = jnp.zeros_like(total_ref)

    def slots(place, first=0, count=experts):
        return back_ref[first : first + count, place].reshape(count * groups, width)

    for at, here in enumerate(blocks):
        arriving[0, at].wait()
        arriving[1, at].wait()
        if at + 1 < len(blocks):
            load((0, 1), at + 1)
        else:
            load((2,), 0)
            atts = [push(kept_own_ref, own_ref, sems.at[3, 0]), push(kept_away_ref, away_ref, sems.at[3, 1])]
        hidden = hidden_ref[here, :].astype(f32)
        normed = (hidden * rms_scale(hidden) * gain).astype(bf16)
        normed_ref[here, :] = normed
        mask = lax.broadcasted_iota(jnp.int32, (groups, STEP), 0) == gid_ref[:, here]
        for slot in range(0, experts, many):
            wide = dot(slots(0, slot, many), cot_ref[here, :], NT) + dot(slots(1, slot, many), normed, NT)
            for own in range(slot, slot + many):
                part = wide[(own - slot) * groups : (own - slot + 1) * groups]
                scaled = jnp.where(mask, part * wt_ref[own : own + 1, here], 0.0)
                part_ref[own : own + 1, here] = jnp.sum(scaled, axis=0, keepdims=True)
                total_ref[own] += jnp.sum(scaled, axis=1, keepdims=True)
    gain_total = jnp.zeros((1, width), f32)
    leaving = []
    for at, here in enumerate(blocks):
        mask = lax.broadcasted_iota(jnp.int32, (groups, STEP), 0) == gid_ref[:, here]
        for slot in range(experts):
            own = slice(slot, slot + 1)
            total = jnp.sum(jnp.where(mask, total_ref[slot], 0.0), axis=0, keepdims=True)
            gl_ref[own, here] = (part_ref[own, here] - wt_ref[own, here] * total).astype(bf16)
        hidden = hidden_ref[here, :].astype(f32)
        scale = rms_scale(hidden)
        unit = hidden * scale
        arriving[2, at].wait()
        if at + 1 < len(blocks):
            load((2,), at + 1)
        hidden_ref[here, :] = (hidden + dot(turned_ref[here, :], slots(0))).astype(bf16)
        leaving.append(push(hidden_ref.at[here], kept_out_ref.at[here], sems.at[4, at]))
        grad_normed = dot(turned_ref[here, :], slots(1)) + dot(gl_ref[:, here], small[:experts], TN)
        weighted = gain * grad_normed
        gain_total = gain_total + jnp.sum(grad_normed * unit, axis=0, keepdims=True)
        back = scale * (weighted - unit * jnp.mean(weighted * unit, axis=-1, keepdims=True))
        low = (cot_ref[here, :].astype(f32) + back).astype(bf16)
        cot_ref[here, :] = low
        leaving.append(push(cot_ref.at[here], kept_gh_ref.at[here], sems.at[5, at]))
        grad_att = dot(low, out_w, NT).astype(bf16)
        gown_ref[here, :] = grad_att[:, :half]
        gaway_ref[here, :] = grad_att[:, half:]
    for copy in atts:
        copy.wait()
    small_ref[:half, :width] = dot(own_ref[...], cot_ref[...], TN).astype(bf16)
    small_ref[half:, :width] = dot(away_ref[...], cot_ref[...], TN).astype(bf16)
    tail = [dot(gl_ref[...], normed_ref[...]), gain_total, jnp.zeros((127 - experts, width), f32)]
    small_ref[:, width:] = jnp.transpose(jnp.concatenate(tail, 0)).astype(bf16)
    for copy in leaving:
        copy.wait()


def unmix(back, weights, gid, gathered, turned, cotangent, hidden, att_own, att_away):
    rows, width = cotangent.shape
    experts, _, groups, _ = back.shape
    kept = (turned, cotangent, hidden, att_own, att_away)
    return call(
        unmix_kernel,
        (
            in_hbm((rows, width), bf16),
            in_hbm((rows, width), bf16),
            shape_of((rows, width // 2), bf16),
            shape_of((rows, width // 2), bf16),
            shape_of((width, width + 128), bf16),
        ),
        (back, weights, gid, gathered, *[from_hbm(array) for array in kept]),
        room=room_for(UNMIX_ROOM, experts * groups),
        in_specs=[VMEM] * 4 + [HBM] * 5,
        out_specs=[HBM] * 2 + [VMEM] * 3,
        scratch_shapes=[pltpu.VMEM(array.shape, bf16) for array in kept]
        + [
            pltpu.VMEM((rows, width), bf16),
            pltpu.VMEM((experts, rows), f32),
            pltpu.VMEM((experts, groups, 1), f32),
            pltpu.VMEM((experts, rows), bf16),
            DMA((6, rows // STEP)),
        ],
    )


def expert_kernel(
    pick_ref, in_ref, up_all_ref, down_all_ref, hint_ref, sent_ref, kept_act_ref, kept_pre_ref, mark_ref,
    up_ref, down_ref, act_ref, pre_ref, out_ref, load_sems, sems,
):
    parts, _, groups, width = in_ref.shape
    many = min(EXPERT_ROWS // groups, parts)
    pick = pick_ref[0]
    load_up = push(up_all_ref.at[pick], up_ref, load_sems.at[0])
    set_mark(mark_ref)
    copies = []
    for at, part in enumerate(range(0, parts, many)):
        here = slice(part * groups, (part + many) * groups)
        owners = slice(part, part + many)
        rows, grad = [in_ref[owners, place].reshape(many * groups, width) for place in range(2)]
        if at == 0:
            load_up.wait()
            load_down = push(down_all_ref.at[pick], down_ref, load_sems.at[1])
        pre = dot(rows, up_ref[...])
        if at == 0:
            load_down.wait()
        cdf = 0.5 + 0.5 * lax.erf(pre * 0.7071067811865476)
        slope = cdf + pre * (jnp.exp(-0.5 * pre * pre) * 0.3989422804014327)
        act = (pre * cdf).astype(bf16)
        act_ref[here, :] = act
        copies.append(push(act_ref.at[here], kept_act_ref.at[here], sems.at[0, at]))
        grad_pre = (dot(grad, down_ref[...], NT) * slope).astype(bf16)
        pre_ref[here, :] = grad_pre
        copies.append(push(pre_ref.at[here], kept_pre_ref.at[here], sems.at[1, at]))
        out_ref[owners, 0] = dot(act, down_ref[...]).astype(bf16).reshape(many, groups, width)
        out_ref[owners, 1] = dot(grad_pre, up_ref[...], NT).astype(bf16).reshape(many, groups, width)
        copies.append(push(out_ref.at[owners], sent_ref.at[owners], sems.at[2, at]))
    for copy in copies:
        copy.wait()


def expert_pass(pick, arrived, w_up, w_down, hint):
    parts, _, groups, width = arrived.shape
    rows = parts * groups
    hidden = w_up.shape[2]
    return call(
        expert_kernel,
        (
            in_hbm(arrived.shape, bf16),
            in_hbm((rows, hidden), bf16),
            in_hbm((rows, hidden), bf16),
            shape_of(MARK, f32),
        ),
        (pick, arrived, from_hbm(w_up), from_hbm(w_down), hint),
        room=room_for(EXPERT_ROOM, rows),
        in_specs=[SMEM, VMEM, HBM, HBM, ANY],
        out_specs=[HBM, HBM, HBM, VMEM],
        scratch_shapes=[
            pltpu.VMEM(w_up.shape[1:], bf16),
            pltpu.VMEM(w_down.shape[1:], bf16),
            pltpu.VMEM((rows, hidden), bf16),
            pltpu.VMEM((rows, hidden), bf16),
            pltpu.VMEM(arrived.shape, bf16),
            DMA((2,)),
            DMA((3, max(rows // EXPERT_ROWS, 1))),
        ],
    )


def expert_grad_kernel(
    in_ref, kept_act_ref, kept_pre_ref, hint_ref, grad_ref, mark_ref, act_ref, pre_ref, out_ref, load_sems, sems
):
    shards, pieces, per, width = grad_ref.shape
    rows, hidden = act_ref.shape
    slabs = [slice(at, at + width) for at in range(0, hidden, width)]
    loads = [
        [push(kept.at[:, slab], ref.at[:, slab], load_sems.at[place, at]) for at, slab in enumerate(slabs)]
        for place, (kept, ref) in enumerate(((kept_act_ref, act_ref), (kept_pre_ref, pre_ref)))
    ]
    down_pieces = hidden // shards // per
    set_mark(mark_ref)
    mixed, grad = [in_ref[:, place].reshape(rows, width) for place in range(2)]
    for at, slab in enumerate(slabs):
        loads[0][at].wait()
        grad_down = dot(act_ref[:, slab], grad, TN).astype(bf16)
        span = width // (down_pieces * per)
        out_ref[at * span : (at + 1) * span, :down_pieces] = grad_down.reshape(span, down_pieces, per, width)
    copies = [push(out_ref.at[:, :down_pieces], grad_ref.at[:, :down_pieces], sems.at[0])]
    for at, slab in enumerate(slabs):
        loads[1][at].wait()
        grad_up = dot(mixed, pre_ref[:, slab], TN).astype(bf16)
        out_ref[:, down_pieces + at] = grad_up.reshape(shards, per, width)
    copies.append(push(out_ref.at[:, down_pieces:], grad_ref.at[:, down_pieces:], sems.at[1]))
    for copy in copies:
        copy.wait()


def expert_grads(arrived, act, grad_pre, shards, hint):
    width = arrived.shape[3]
    hidden = act.shape[1]
    per = width // shards
    grad = (shards, (hidden // shards) // per + hidden // width, per, width)
    return call(
        expert_grad_kernel,
        (in_hbm(grad, bf16), shape_of(MARK, f32)),
        (arrived, from_hbm(act), from_hbm(grad_pre), hint),
        room=room_for(GRAD_ROOM, act.shape[0]),
        in_specs=[VMEM, HBM, HBM, ANY],
        out_specs=[HBM, VMEM],
        scratch_shapes=[
            pltpu.VMEM(act.shape, bf16),
            pltpu.VMEM(act.shape, bf16),
            pltpu.VMEM(grad, bf16),
            DMA((2, hidden // width)),
            DMA((2,)),
        ],
    )


def shard_sum_kernel(in_ref, down_ref, up_ref):
    total = in_ref[0, 0].astype(f32)
    for part in range(1, in_ref.shape[0]):
        total = total + in_ref[part, 0].astype(f32)
    down_rows, width = down_ref.shape[1:]
    down_ref[0] = total[:down_rows]
    per = up_ref.shape[1]
    for at in range(0, up_ref.shape[2] // width):
        here = down_rows + at * per
        up_ref[0, :, at * width : (at + 1) * width] = total[here : here + per]


def shard_sum(parts, per_owner, down_rows, up_rows):
    shards, tall, width = parts.shape
    parts = parts.reshape(shards // per_owner, per_owner, tall, width)
    hidden = (tall - down_rows) // up_rows * width
    return call(
        shard_sum_kernel,
        (
            in_hbm((per_owner, down_rows, width), f32),
            in_hbm((per_owner, up_rows, hidden), f32),
        ),
        (parts,),
        grid=(per_owner,),
        in_specs=[pl.BlockSpec((parts.shape[0], 1, tall, width), lambda at: (0, at, 0, 0))],
        out_specs=[
            pl.BlockSpec((1, down_rows, width), lambda at: (at, 0, 0)),
            pl.BlockSpec((1, up_rows, hidden), lambda at: (at, 0, 0)),
        ],
    )


def load_project(kept_ref, w_ref, out_ref, first, unit_ref, sems):
    wide = out_ref.shape[1]
    rows = unit_ref.shape[0]
    count = sems.shape[0]
    blocks = [slice(at, at + rows // count) for at in range(0, rows, rows // count)]
    copies = []

    def load(at):
        if at < count:
            copies.append(push(kept_ref.at[blocks[at]], unit_ref.at[blocks[at]], sems.at[at]))

    load(0)
    load(1)
    for at, here in enumerate(blocks):
        copies[at].wait()
        load(at + 2)
        out_ref[here, :] = dot(unit_ref[here, :], w_ref[:, first : first + wide]).astype(bf16)


def project_kernel(first, kept_ref, w_ref, out_ref, unit_ref, sems):
    load_project(kept_ref, w_ref, out_ref, first, unit_ref, sems)


def project(unit, weights, half):
    rows, width = unit.shape
    wide = 3 * width // 2
    return call(
        functools.partial(project_kernel, half * wide),
        shape_of((rows, wide), bf16),
        (from_hbm(unit), weights),
        room=16,
        in_specs=[HBM, VMEM],
        out_specs=VMEM,
        scratch_shapes=[pltpu.VMEM((rows, width), bf16), DMA((4,))],
    )


def own_grad_kernel(unit_t_ref, grad_ref, w_ref, grad_w_ref, part_ref):
    wide = grad_ref.shape[1]
    grad_w_ref[...] = dot(unit_t_ref[...], grad_ref[...])
    for at in range(0, part_ref.shape[0], 1024):
        here = slice(at, at + 1024)
        part_ref[here, :] = dot(grad_ref[here, :], w_ref[:, :wide], NT)


def own_grad(unit_t, grad, weights):
    width, rows = unit_t.shape
    return call(
        own_grad_kernel,
        (shape_of((width, grad.shape[1]), f32), shape_of((rows, width), f32)),
        (unit_t, grad, weights),
        room=16,
        in_specs=[VMEM] * 3,
        out_specs=[VMEM] * 2,
    )


def away_grad_kernel(mine_ref, unit_t_ref, grad_ref, own_ref, small_ref, keep_ref, send_ref, total_ref):
    total_ref[...] = dot(unit_t_ref[...], grad_ref[...])
    many, per, _ = keep_ref.shape
    mine = mine_ref[0]
    left = own_ref.shape[1]
    right = left + total_ref.shape[1]
    for place in range(many):
        for part, ref in ((mine, keep_ref), (1 - mine, send_ref)):
            rows = pl.ds(pl.multiple_of((2 * place + part) * per, per), per)
            ref[place, :, :left] = own_ref[rows, :].astype(ref.dtype)
            ref[place, :, left:right] = total_ref[rows, :].astype(ref.dtype)
            ref[place, :, right:] = small_ref[rows, :].astype(ref.dtype)


def halves(array, mine):
    keep, send = [lax.dynamic_index_in_dim(array, part[0], 1, keepdims=False) for part in (mine, 1 - mine)]
    return keep, send.astype(bf16)


def away_grad(mine, unit_t, grad, own, small, devices):
    width, rows = unit_t.shape
    wide = grad.shape[1]
    per = width // devices
    if per % 16:
        total = jnp.concatenate([own, dot(unit_t, grad), small.astype(f32)], 1)
        return halves(total.reshape(devices // 2, 2, per, -1), mine)
    dims = (devices // 2, per, own.shape[1] + wide + small.shape[1])
    return call(
        away_grad_kernel,
        (shape_of(dims, f32), shape_of(dims, bf16)),
        (mine, unit_t, grad, own, small),
        room=16,
        in_specs=[SMEM] + [VMEM] * 4,
        out_specs=[VMEM] * 2,
        scratch_shapes=[pltpu.VMEM((width, wide), f32)],
    )


def token_grad_kernel(part_ref, grad_ref, w_ref, tok_ref, gh_ref, out_ref, mark_ref):
    set_mark(mark_ref)
    wide = grad_ref.shape[1]
    for at in range(0, tok_ref.shape[0], 512):
        here = slice(at, at + 512)
        weighted = part_ref[here, :] + dot(grad_ref[here, :], w_ref[:, wide : 2 * wide], NT)
        source = tok_ref[here, :].astype(f32)
        scale = rms_scale(source)
        unit = source * scale
        back = scale * (weighted - unit * jnp.mean(weighted * unit, axis=-1, keepdims=True))
        out_ref[here, :] = (gh_ref[here, :].astype(f32) + back).astype(bf16)


def token_grad(part, grad, weights, tokens, grad_hidden):
    return call(
        token_grad_kernel,
        (shape_of(tokens.shape, bf16), shape_of(MARK, f32)),
        (part, grad, weights, tokens, grad_hidden),
        room=16,
        in_specs=[VMEM] * 5,
        out_specs=[VMEM] * 2,
    )


def swap(array, axis, size, bit):
    return lax.ppermute(array, axis, [(at, at ^ bit) for at in range(size)])


def axis_bits(sizes):
    bits = []
    for axis, size in sizes:
        bit = size // 2
        while bit:
            bits.append((axis, size, bit))
            bit //= 2
    return bits


def gather_rows(shard, sizes, meanwhile):
    rows = shard.shape[0]
    total = rows
    for _, size in sizes:
        total *= size
    bits = axis_bits(sizes)
    held = shard[(None,) * len(bits)]
    for place in range(len(bits)):
        axis, size, bit = bits[place]
        if place == len(bits) - 1:
            held, meanwhile = lax.optimization_barrier((held, meanwhile))
        other = swap(held, axis, size, bit)
        upper = (lax.axis_index(axis) // bit) % 2 == 1
        first = jnp.where(upper, other, held)
        second = jnp.where(upper, held, other)
        held = jnp.concatenate([first, second], axis=place)
    return held.reshape((total,) + shard.shape[1:]), meanwhile


def add_split_kernel(mine_ref, keep_ref, got_ref, hint_ref, next_keep_ref, send_ref):
    mine = mine_ref[0]
    for part, ref in ((mine, next_keep_ref), (1 - mine, send_ref)):
        value = keep_ref[:, pl.ds(part, 1)] + got_ref[:, pl.ds(part, 1)].astype(f32)
        ref[...] = value[:, 0].astype(ref.dtype)


def add_split(mine, keep, got, hint):
    many, per, wide = keep.shape
    dims = (many // 2, per, wide)
    keep, got = [array.reshape(many // 2, 2, per, wide) for array in (keep, got)]
    if per % 16:
        return halves(keep + got.astype(f32), mine)
    return call(
        add_split_kernel,
        (shape_of(dims, f32), shape_of(dims, bf16)),
        (mine, keep, got, hint),
        room=16,
        in_specs=[SMEM, VMEM, VMEM, ANY],
        out_specs=[VMEM] * 2,
    )


def scatter_rows(keep, send, sizes, hints):
    bits = axis_bits(sizes)[::-1]
    for place, (axis, size, bit) in enumerate(bits):
        got = swap(send, axis, size, bit)
        if place + 1 == len(bits):
            return (keep + got.astype(f32))[0]
        axis, size, bit = bits[place + 1]
        mine = ((lax.axis_index(axis) // bit) % 2).astype(jnp.int32).reshape(1)
        keep, send = add_split(mine, keep, got, hints.get(place, got))


def pair_columns(array, back=False):
    rows, wide = array.shape
    pairs = wide // 384
    dims = (rows, pairs, 3, 128) if back else (rows, 3, pairs, 128)
    return array.reshape(dims).swapaxes(1, 2).reshape(rows, wide)


def on_device(
    n_dp, n_owner, tokens, seq_lengths, group_map, gain_attn, gain_mix, w_qkv, w_out, w_ctrl, w_up, w_down, cotangent
):
    rows, width = tokens.shape
    experts = w_ctrl.shape[1]
    per_owner = w_up.shape[0]
    groups = rows // G
    parts = n_dp // per_owner
    sizes = (("dp", n_dp), ("expert", n_owner))
    dp = lax.axis_index("dp")
    pick = (dp % per_owner).astype(jnp.int32).reshape(1)

    gained = pair_columns((w_qkv.astype(f32) * gain_attn.astype(f32)[:, None]).astype(bf16))
    ctrl_slots = w_ctrl.reshape(-1, n_owner, per_owner).swapaxes(1, 2).reshape(-1, experts)
    pad = jnp.zeros((w_ctrl.shape[0], 127 - experts), bf16)
    shard = jnp.concatenate([gained, w_out, ctrl_slots, gain_mix[:, None], pad], 1)
    unit_one, unit_t, gid = call(
        prep_kernel,
        (in_hbm((rows, width), bf16), in_hbm((width, rows), bf16), shape_of((1, rows), jnp.int32)),
        (tokens, group_map.reshape(groups, G)),
        room=16,
        in_specs=[VMEM] * 2,
        out_specs=[HBM, HBM, VMEM],
        scratch_shapes=[pltpu.VMEM((rows, width), bf16), pltpu.VMEM((width, rows), bf16), DMA((2,))],
    )

    def neighbour(array):
        return swap(array, "expert", n_owner, 1)

    away_length = neighbour(seq_lengths.astype(f32)).astype(jnp.int32)
    gathered, (unit_one, away_length) = gather_rows(shard, sizes, (unit_one, away_length))
    triple = 3 * width

    away_qkv = neighbour(project(unit_one, gathered, 1))
    att_own, lse_own, own_qkv, kept_own = project_attend(seq_lengths, unit_one, gathered, width // 256)
    att_away, lse_away, away_qkv, kept_away = attend_forward(away_length, away_qkv, lse_own)
    hidden, weights, mixed, kept_back = mix(
        tokens, att_own, neighbour(att_away), gathered, gid, cotangent, experts
    )

    teams = [
        [(part * per_owner + low) * n_owner + owner for low in range(per_owner) for owner in range(n_owner)]
        for part in range(parts)
    ]

    def exchange(array):
        return lax.all_to_all(
            array, ("dp", "expert"), split_axis=0, concat_axis=0, axis_index_groups=teams, tiled=True
        )

    arrived = exchange(mixed)
    turned, mark = turn(weights, gid, groups)
    results, act, grad_pre, mark = expert_pass(pick, arrived, w_up, w_down, mark)
    back = exchange(results)
    grad_experts, mark = expert_grads(arrived, act, grad_pre, n_dp, mark)
    shards = lax.all_to_all(
        grad_experts.reshape(n_dp, -1, width), "dp", split_axis=0, concat_axis=0, tiled=True
    )
    output, grad_hidden, grad_own, grad_away, grad_small = unmix(
        back, weights, gid, gathered, turned, cotangent, hidden, kept_own, kept_back
    )

    grad_here = neighbour(grad_away)
    grad_one = attend_backward(seq_lengths, own_qkv, grad_own, kept_own, lse_own, grad_own)
    grad_two = neighbour(attend_backward(away_length, away_qkv, grad_here, kept_away, lse_away, grad_one))
    grad_w_own, token_part = own_grad(unit_t, grad_one, gathered)
    axis, size, bit = axis_bits(sizes)[-1]
    mine = ((lax.axis_index(axis) // bit) % 2).astype(jnp.int32).reshape(1)
    keep, send = away_grad(mine, unit_t, grad_two, grad_w_own, grad_small, n_dp * n_owner)
    grad_tokens, token_mark = token_grad(token_part, grad_two, gathered, tokens, grad_hidden)
    grad_down_shard, grad_up_shard = shard_sum(shards, per_owner, w_down.shape[1] // n_dp, width // n_dp)
    summed_small = scatter_rows(keep, send, sizes, {1: token_mark})

    grad_w_shard = pair_columns(summed_small[:, :triple], back=True)
    early = summed_small[:, triple:]
    shard_qkv = gain_attn.astype(f32)[:, None] * grad_w_shard
    shard_gain_one = jnp.sum(w_qkv.astype(f32) * grad_w_shard, axis=1)
    shard_ctrl = early[:, width : width + experts]
    shard_ctrl = shard_ctrl.reshape(-1, per_owner, n_owner).swapaxes(1, 2).reshape(-1, experts)
    return (
        output,
        grad_tokens,
        shard_gain_one,
        early[:, width + experts],
        shard_qkv,
        early[:, :width],
        shard_ctrl,
        grad_up_shard,
        grad_down_shard,
    )


def solution(mesh):
    both = ("dp", "expert")
    rows = P(both, None)
    return jax.shard_map(
        functools.partial(on_device, mesh.shape["dp"], mesh.shape["expert"]),
        mesh=mesh,
        in_specs=(
            rows, P(both), rows, P(both), P(both), rows, rows, rows,
            P("expert", None, None), P("expert", None, None), rows,
        ),
        out_specs=(
            rows, rows, P(both), P(both), rows, rows, rows,
            P("expert", "dp", None), P("expert", "dp", None),
        ),
        check_vma=False,
    )
```

```python
import functools

import jax
import jax.numpy as jnp
from jax import lax
from jax.experimental import pallas as pl
from jax.experimental.pallas import tpu as pltpu
from jax.sharding import PartitionSpec as P

HEADS = 8
G = 32
BQ = 256

ANY = pl.BlockSpec(memory_space=pl.ANY)
VMEM = pl.BlockSpec(memory_space=pltpu.VMEM)
HBM = pl.BlockSpec(memory_space=pltpu.HBM)
DMA = pltpu.SemaphoreType.DMA
SMEM = pl.BlockSpec(memory_space=pltpu.SMEM)

eps_norm = 1e-05
masked_value = -1e30
bf16 = jnp.bfloat16
f32 = jnp.float32
NN = (((1,), (0,)), ((), ()))
NT = (((1,), (1,)), ((), ()))
TN = (((0,), (0,)), ((), ()))


def dot(left, right, dims=NN):
    return lax.dot_general(left, right, dims, preferred_element_type=f32)


def rms_scale(values):
    return lax.rsqrt(jnp.mean(values * values, axis=-1, keepdims=True) + eps_norm)


def call(body, out_shape, args, room=28, **extra):
    return pl.pallas_call(
        body,
        out_shape=out_shape,
        compiler_params=pltpu.CompilerParams(vmem_limit_bytes=room * 2**20),
        name=getattr(body, "func", body).__name__,
        **extra,
    )(*args)


def shape_of(dims, kind):
    return jax.ShapeDtypeStruct(dims, kind)


def in_hbm(dims, kind):
    return pltpu.HBM(dims, kind)


def in_vmem(dims, kind):
    return pltpu.VMEM(dims, kind)


def from_hbm(array):
    return pltpu.with_memory_space_constraint(array, pltpu.HBM)


def room_for(parts, rows):
    fixed, per_block = parts
    return fixed + per_block * rows // 1024


def push(source, target, sem):
    copy = pltpu.make_async_copy(source, target, sem)
    copy.start()
    return copy


MARK = (8, 128)


def set_mark(ref):
    ref[...] = jnp.zeros(MARK, f32)


def diagonal(size):
    return lax.broadcasted_iota(jnp.int32, (size, size), 0) == lax.broadcasted_iota(jnp.int32, (size, size), 1)


def column_of(row):
    return jnp.sum(jnp.where(diagonal(row.shape[1]), row, 0.0), axis=1, keepdims=True)


def row_of(column):
    return jnp.sum(jnp.where(diagonal(column.shape[0]), column, 0.0), axis=0, keepdims=True)


def slot_matrix(experts, wide, n_owner, kind):
    expert = lax.broadcasted_iota(jnp.int32, (experts, wide), 0)
    slot = lax.broadcasted_iota(jnp.int32, (experts, wide), 1)
    per_owner = experts // n_owner
    return jnp.where(expert % per_owner * n_owner + expert // per_owner == slot, 1.0, 0.0).astype(kind)


def pack_kernel(n_owner, len_ref, wqkv_ref, gain_ref, wout_ref, ctrl_ref, mix_ref, out_ref):
    width = wout_ref.shape[1]
    experts = ctrl_ref.shape[1]
    gain = column_of(gain_ref[...].astype(f32))
    for pair in range(width // 128):
        for part in range(3):
            at = part * width + pair * 128
            to = pair * 384 + part * 128
            out_ref[:, to : to + 128] = (wqkv_ref[:, at : at + 128].astype(f32) * gain).astype(bf16)
    out_ref[:, 3 * width : 4 * width] = wout_ref[...]
    small = dot(ctrl_ref[...], slot_matrix(experts, 128, n_owner, bf16))
    lane = lax.broadcasted_iota(jnp.int32, small.shape, 1)
    small = jnp.where(lane == experts, column_of(mix_ref[...].astype(f32)), small)
    small = jnp.where(lane == 127, len_ref[0].astype(f32), small)
    out_ref[:, 4 * width :] = small.astype(bf16)


def finish_kernel(n_owner, keep_ref, got_ref, gain_ref, wqkv_ref, qkv_ref, out_ref, ctrl_ref, one_ref, mix_ref):
    width = out_ref.shape[1]
    experts = ctrl_ref.shape[1]
    total = keep_ref[0] + got_ref[0].astype(f32)
    gain = column_of(gain_ref[...].astype(f32))
    grad_gain = jnp.zeros((total.shape[0], 128), f32)
    for pair in range(width // 128):
        for part in range(3):
            to = part * width + pair * 128
            at = pair * 384 + part * 128
            grad = total[:, at : at + 128]
            qkv_ref[:, to : to + 128] = gain * grad
            grad_gain = grad_gain + wqkv_ref[:, to : to + 128].astype(f32) * grad
    out_ref[...] = total[:, 3 * width : 4 * width]
    small = total[:, 4 * width :]
    slots = slot_matrix(experts, 128, n_owner, f32)
    ctrl_ref[...] = lax.dot_general(small, slots, NT, precision=lax.Precision.HIGHEST, preferred_element_type=f32)
    one_ref[...] = row_of(jnp.sum(grad_gain, axis=1, keepdims=True))
    lane = lax.broadcasted_iota(jnp.int32, small.shape, 1)
    mix_ref[...] = row_of(jnp.sum(jnp.where(lane == experts, small, 0.0), axis=1, keepdims=True))


def prep_kernel(
    tok_ref, tok_away_ref, gmap_ref, kept_ref, kept_away_ref, kept_t_ref, gid_ref, unit_ref, away_ref, unit_t_ref, sems
):
    rows = tok_ref.shape[0]
    step = 256
    for source, target in ((tok_ref, unit_ref), (tok_away_ref, away_ref)):
        for at in range(0, rows, step):
            block = source[at : at + step, :].astype(f32)
            unit = (block * rms_scale(block)).astype(bf16)
            target[at : at + step, :] = unit
            if source is tok_ref:
                unit_t_ref[:, at : at + step] = jnp.transpose(unit)
    pairs = ((unit_ref, kept_ref), (away_ref, kept_away_ref), (unit_t_ref, kept_t_ref))
    copies = [push(source, target, sems.at[at]) for at, (source, target) in enumerate(pairs)]
    groups = rows // G
    places = lax.broadcasted_iota(jnp.int32, (groups, rows), 1)
    group_at = lax.broadcasted_iota(jnp.int32, (groups, rows), 0)
    gmap = gmap_ref[...]
    member = jnp.zeros((groups, rows), jnp.int32)
    for slot in range(G):
        member = jnp.where(gmap[:, slot : slot + 1] == places, group_at, member)
    gid_ref[...] = jnp.sum(member.astype(f32), axis=0, keepdims=True).astype(jnp.int32)
    for copy in copies:
        copy.wait()


def lower_mask():
    return lax.broadcasted_iota(jnp.int32, (BQ, BQ), 0) <= lax.broadcasted_iota(jnp.int32, (BQ, BQ), 1)


def head_lanes():
    return lax.broadcasted_iota(jnp.int32, (1, 128), 1) // 64


def attend_pair(length, pair, qkv_all_ref, out_ref, lse_all_ref, vt_ref):
    qkv_ref = qkv_all_ref.at[:, pl.ds(pl.multiple_of(pair * 384, 384), 384)]
    lse_ref = lse_all_ref.at[pl.ds(pair, 1)]
    rows = qkv_ref.shape[0]
    step, ahead = 512, 4
    lane = head_lanes()
    vt_ref[...] = jnp.transpose(qkv_ref[:, 256:384])

    def run(low_of):
        items = []
        for at in range(0, rows, BQ):
            chunks = [(at, BQ)]
            top = at
            while top > low_of(at):
                down = max(low_of(at), top - step)
                chunks.append((down, top - down))
                top = down
            for place, (low, wide) in enumerate(chunks):
                for head in range(2):
                    items.append((at, head, low, wide, place == 0, place == len(chunks) - 1))

        def score(at, head, low, wide, first, last):
            own = jnp.where(lane == head, qkv_ref[at : at + BQ, 0:128] * bf16(0.125), bf16(0))
            scores = dot(qkv_ref[low : low + wide, 128:256], own, NT)
            return jnp.where(lower_mask(), scores, masked_value) if first else scores

        pending = [score(*item) for item in items[:ahead]]
        state = {}
        for place, (at, head, low, wide, first, last) in enumerate(items):
            if place + ahead < len(items):
                pending.append(score(*items[place + ahead]))
            scores = pending.pop(0)
            peak = jnp.max(scores, axis=0, keepdims=True)
            if not first:
                old_peak, old_total, old_mixed = state[head]
                peak = jnp.maximum(old_peak, peak)
                shrink = jnp.exp(old_peak - peak)
            probs = jnp.exp(scores - peak)
            total = jnp.sum(probs, axis=0, keepdims=True)
            mixed = dot(vt_ref[64 * head : 64 * head + 64, low : low + wide], probs.astype(bf16))
            if not first:
                total = total + old_total * shrink
                mixed = mixed + old_mixed * shrink
            state[head] = (peak, total, mixed)
            if last:
                lse_ref[0, head : head + 1, at : at + BQ] = peak + jnp.log(total)
                if head == 1:
                    both = [state[own][2] * (1.0 / state[own][1]) for own in range(2)]
                    out_ref[at : at + BQ, :] = jnp.transpose(jnp.concatenate(both, 0)).astype(bf16)

    @pl.when(length == BQ)
    def _():
        run(lambda at: at)

    @pl.when(length != BQ)
    def _():
        run(lambda at: 0)


def attend_kernel(
    len_ref, place_ref, kept_own_ref, kept_away_ref, w_ref,
    lens_ref, own_ref, away_ref, lse_own_ref, lse_away_ref, kept_qkv_own_ref, kept_qkv_away_ref, kept_out_ref,
    unit_ref, qkv_ref, out_ref, lse_ref, vt_ref, unit_sems, sems,
):
    row = pl.multiple_of(place_ref[0] // 16 * 16, 16)
    tile = w_ref[pl.ds(row, 16), w_ref.shape[1] - 128 :].astype(f32)
    chosen = lax.broadcasted_iota(jnp.int32, tile.shape, 1) == 127
    chosen = chosen & (lax.broadcasted_iota(jnp.int32, tile.shape, 0) == place_ref[0] % 16)
    lens_ref[0] = len_ref[0]
    lens_ref[1] = jnp.max(jnp.where(chosen, tile, 0.0)).astype(jnp.int32)
    rows, wide = qkv_ref.shape
    half = wide // 2
    pairs = wide // 384
    count = unit_sems.shape[0] // 2
    blocks = [slice(at, at + rows // count) for at in range(0, rows, rows // count)]
    kept = (kept_qkv_own_ref, kept_qkv_away_ref)
    copies, keeping = [], []

    def load(at):
        if at < 2 * count:
            source = (kept_own_ref, kept_away_ref)[at // count]
            copies.append(push(source.at[blocks[at % count]], unit_ref.at[at % 3], unit_sems.at[at]))

    load(0)
    load(1)
    for at in range(2 * count):
        side = at // count
        copies[at].wait()
        load(at + 2)
        columns = slice(side * half, (side + 1) * half)
        qkv_ref[blocks[at % count], columns] = dot(unit_ref[at % 3], w_ref[:, columns]).astype(bf16)
        if at % count == count - 1:
            keeping.append(push(qkv_ref.at[:, columns], kept[side], sems.at[side]))

    def keep_out(pair):
        thin = pl.ds(pl.multiple_of((pair - pairs // 2) * 128, 128), 128)
        return pltpu.make_async_copy(away_ref.at[:, thin], kept_out_ref.at[:, thin], sems.at[2 + pair])

    @pl.loop(0, pairs)
    def _(pair):
        mine = pair < pairs // 2
        attend_pair(lens_ref[jnp.where(mine, 0, 1)], pair, qkv_ref, out_ref, lse_ref, vt_ref)

        @pl.when(mine)
        def _():
            own_ref[:, pl.ds(pl.multiple_of(pair * 128, 128), 128)] = out_ref[...]

        @pl.when(jnp.logical_not(mine))
        def _():
            away_ref[:, pl.ds(pl.multiple_of((pair - pairs // 2) * 128, 128), 128)] = out_ref[...]
            keep_out(pair).start()

    lse_own_ref[...] = lse_ref[: pairs // 2]
    lse_away_ref[...] = lse_ref[pairs // 2 :]
    for copy in keeping:
        copy.wait()
    for pair in range(pairs // 2, pairs):
        keep_out(pair).wait()


def attend_forward(length, place, unit, unit_away, gathered):
    rows, width = unit.shape
    pairs = width // 128
    count = 4
    half = pairs // 2
    lse = shape_of((half, 2, rows), f32)
    return call(
        attend_kernel,
        (
            shape_of((2,), jnp.int32),
            shape_of((rows, 128 * half), bf16),
            shape_of((rows, 128 * half), bf16),
            lse,
            lse,
            in_hbm((rows, 384 * half), bf16),
            in_hbm((rows, 384 * half), bf16),
            in_hbm((rows, 128 * half), bf16),
        ),
        (length, place, from_hbm(unit), from_hbm(unit_away), gathered),
        room=ATTEND_ROOM,
        in_specs=[SMEM, SMEM, HBM, HBM, VMEM],
        out_specs=[SMEM] + [VMEM] * 4 + [HBM] * 3,
        scratch_shapes=[
            pltpu.VMEM((3, rows // count, width), bf16),
            pltpu.VMEM((rows, 384 * pairs), bf16),
            pltpu.VMEM((rows, 128), bf16),
            pltpu.VMEM((pairs, 2, rows), f32),
            pltpu.VMEM((128, rows), bf16),
            DMA((2 * count,)),
            DMA((2 + pairs,)),
        ],
    )


def attend_back_kernel(side, lens_ref, qkv_ref, go_ref, o_ref, lse_ref, hint_ref, grad_ref, *scratch):
    @pl.loop(0, qkv_ref.shape[1] // 384)
    def _(pair):
        wide = pl.ds(pl.multiple_of(pair * 384, 384), 384)
        thin = pl.ds(pl.multiple_of(pair * 128, 128), 128)
        refs = [qkv_ref.at[:, wide], go_ref.at[:, thin], o_ref.at[:, thin], lse_ref.at[pl.ds(pair, 1)]]
        attend_back_pair(lens_ref[side], *refs, grad_ref.at[:, wide], *scratch)


def attend_back_pair(length, qkv_ref, go_ref, o_ref, lse_ref, grad_ref, gqt_ref, kt_ref, dl_ref):
    rows = qkv_ref.shape[0]
    step, ahead = 512, 1
    lane = head_lanes()
    kt_ref[...] = jnp.transpose(qkv_ref[:, 128:256]) * bf16(0.125)
    product = jnp.transpose(go_ref[...].astype(f32) * o_ref[...].astype(f32))
    dl_ref[0:1, :] = jnp.sum(product[0:64], axis=0, keepdims=True)
    dl_ref[1:2, :] = jnp.sum(product[64:128], axis=0, keepdims=True)

    def run(end_of):
        items = []
        for low in range(0, rows, BQ):
            end = end_of(low)
            chunks = [(low, BQ)] + [(at, min(step, end - at)) for at in range(low + BQ, end, step)]
            for place, (at, wide) in enumerate(chunks):
                for head in range(2):
                    items.append((low, head, at, wide, place == 0, place == len(chunks) - 1))
        blocks = {}
        written = set()

        def products(low, head, at, wide, first, last):
            if (low, head) not in blocks:
                keys = qkv_ref[low : low + BQ, 128:256] * bf16(0.125)
                vals = qkv_ref[low : low + BQ, 256:384]
                blocks[low, head] = [jnp.where(lane == head, own, bf16(0)) for own in (keys, vals)]
            keys, vals = blocks[low, head]
            return (
                dot(keys, qkv_ref[at : at + wide, 0:128], NT),
                dot(vals, go_ref[at : at + wide, :], NT),
            )

        pending = [products(*item) for item in items[:ahead]]
        grad_k, grad_v = {}, {}
        for place, (low, head, at, wide, first, last) in enumerate(items):
            if place + ahead < len(items):
                pending.append(products(*items[place + ahead]))
            scores, grad_probs = pending.pop(0)
            here = slice(at, at + wide)
            probs = jnp.exp(scores - lse_ref[0, head : head + 1, here])
            if first:
                probs = jnp.where(lower_mask(), probs, 0.0)
            grad_scores = (probs * (grad_probs - dl_ref[head : head + 1, here])).astype(bf16)
            more_v = dot(probs.astype(bf16), go_ref[here, :])
            more_k = dot(grad_scores, qkv_ref[here, 0:128])
            grad_v[head] = more_v if first else grad_v[head] + more_v
            grad_k[head] = more_k if first else grad_k[head] + more_k
            span = slice(64 * head, 64 * head + 64)
            more_q = dot(kt_ref[span, low : low + BQ], grad_scores)
            fresh = (head, at + wide) not in written
            written.update((head, top) for top in range(at + BQ, at + wide + BQ, BQ))
            if fresh:
                gqt_ref[span, here] = more_q
            else:
                gqt_ref[span, here] += more_q
            if last and head == 1:
                there = slice(low, low + BQ)
                grad_ref[there, 128:256] = (jnp.where(lane == 0, grad_k[0], grad_k[1]) * 0.125).astype(bf16)
                grad_ref[there, 256:384] = jnp.where(lane == 0, grad_v[0], grad_v[1]).astype(bf16)

    @pl.when(length == BQ)
    def _():
        run(lambda low: low + BQ)

    @pl.when(length != BQ)
    def _():
        run(lambda low: rows)

    grad_ref[:, 0:128] = jnp.transpose(gqt_ref[...]).astype(bf16)


def attend_backward(side, lengths, qkv, grad_attended, attended, log_totals, hint):
    rows = qkv.shape[0]
    return call(
        functools.partial(attend_back_kernel, side),
        shape_of(qkv.shape, bf16),
        (lengths, qkv, grad_attended, attended, log_totals, hint),
        room=ATTEND_ROOM,
        in_specs=[SMEM, VMEM, VMEM, VMEM, VMEM, ANY],
        out_specs=VMEM,
        scratch_shapes=[pltpu.VMEM((128, rows), f32), pltpu.VMEM((128, rows), bf16), pltpu.VMEM((2, rows), f32)],
    )


STEP = 512
UNMIX_ROOM = (24, 12)
MIX_ROOM = (12, 12)
ATTEND_ROOM = 24
EXPERT_ROOM = (20, 16)
GRAD_ROOM = (16, 20)
EXPERT_ROWS = 512
MIX_ROWS = 1024


def member_mask(gid_ref, groups):
    wide = gid_ref.shape[1]
    return lax.broadcasted_iota(jnp.int32, (groups, wide), 0) == gid_ref[...]


def mix_kernel(
    tok_ref, own_ref, away_ref, w_all_ref, gid_ref, cot_ref,
    kept_hidden_ref, wt_ref, sent_ref, kept_own_ref, kept_away_ref, normed_ref, w_ref, hidden_ref, mixed_ref, sems,
):
    copies = [push(away_ref, kept_away_ref, sems.at[0]), push(own_ref, kept_own_ref, sems.at[4])]
    rows, width = tok_ref.shape
    experts, _, groups, _ = mixed_ref.shape
    half = width // 2
    out_w = w_all_ref[:, 3 * width : 4 * width]
    small = jnp.transpose(w_all_ref[:, 4 * width :])
    gain = small[experts : experts + 1, :].astype(f32)
    for at in range(0, rows, 512):
        here = slice(at, at + 512)
        hidden = tok_ref[here, :].astype(f32) + dot(own_ref[here, :], out_w[:half])
        hidden = (hidden + dot(away_ref[here, :], out_w[half:])).astype(bf16)
        hidden_ref[here, :] = hidden
        hidden = hidden.astype(f32)
        normed_ref[here, :] = (hidden * rms_scale(hidden) * gain).astype(bf16)
    copies.append(push(hidden_ref, kept_hidden_ref, sems.at[1]))
    logits = dot(small[:experts], normed_ref[...], NT)
    mask = member_mask(gid_ref, groups)
    for slot in range(experts):
        wide = jnp.where(mask, logits[slot : slot + 1, :], masked_value)
        wide = jnp.exp(wide - jnp.max(wide, axis=1, keepdims=True))
        wide = wide * (1.0 / jnp.sum(wide, axis=1, keepdims=True))
        wt_ref[slot : slot + 1, :] = jnp.sum(wide, axis=0, keepdims=True)
        w_ref[slot * groups : (slot + 1) * groups, :] = wide.astype(bf16)
    many = min(MIX_ROWS // groups, experts)
    for place, ref in enumerate((normed_ref, cot_ref)):
        for slot in range(0, experts, many):
            mixed = dot(w_ref[slot * groups : (slot + many) * groups, :], ref[...]).astype(bf16)
            mixed_ref[slot : slot + many, place] = mixed.reshape(many, groups, width)
        copies.append(push(mixed_ref.at[:, place], sent_ref.at[:, place], sems.at[2 + place]))
    for copy in copies:
        copy.wait()


def mix(tokens, att_own, att_away, gathered, gid, cotangent, experts):
    rows, width = tokens.shape
    groups = rows // G
    sent = (experts, 2, groups, width)
    return call(
        mix_kernel,
        (
            in_hbm((rows, width), bf16),
            shape_of((experts, rows), f32),
            in_hbm(sent, bf16),
            in_hbm(att_own.shape, bf16),
            in_hbm(att_away.shape, bf16),
        ),
        (tokens, att_own, att_away, gathered, gid, cotangent),
        room=room_for(MIX_ROOM, experts * groups),
        in_specs=[VMEM] * 6,
        out_specs=[HBM, VMEM, HBM, HBM, HBM],
        scratch_shapes=[
            pltpu.VMEM((rows, width), bf16),
            pltpu.VMEM((experts * groups, rows), bf16),
            pltpu.VMEM((rows, width), bf16),
            pltpu.VMEM(sent, bf16),
            DMA((5,)),
        ],
    )


def turn_kernel(wt_ref, gid_ref, kept_ref, mark_ref, turned_ref, sem):
    set_mark(mark_ref)
    experts, rows = wt_ref.shape
    groups = turned_ref.shape[1] // experts
    many = 256 // groups
    for at in range(0, rows, STEP):
        here = slice(at, at + STEP)
        mask = lax.broadcasted_iota(jnp.int32, (groups, STEP), 0) == gid_ref[:, here]
        for slot in range(0, experts, many):
            parts = [
                jnp.where(mask, wt_ref[own : own + 1, here], 0.0).astype(bf16) for own in range(slot, slot + many)
            ]
            turned_ref[here, slot * groups : (slot + many) * groups] = jnp.transpose(jnp.concatenate(parts, 0))
    push(turned_ref, kept_ref, sem).wait()


def turn(weights, gid, groups):
    experts, rows = weights.shape
    return call(
        turn_kernel,
        (in_hbm((rows, experts * groups), bf16), shape_of(MARK, f32)),
        (weights, gid),
        room=16,
        in_specs=[VMEM] * 2,
        out_specs=[HBM, VMEM],
        scratch_shapes=[pltpu.VMEM((rows, experts * groups), bf16), DMA],
    )


def unmix_kernel(
    back_ref, wt_ref, gid_ref, w_all_ref, kept_turned_ref, kept_cot_ref, kept_hidden_ref, kept_own_ref,
    kept_away_ref, kept_out_ref, kept_gh_ref, gown_ref, gaway_ref, small_ref,
    turned_ref, cot_ref, hidden_ref, own_ref, away_ref, rest_ref, normed_ref, part_ref, total_ref, gl_ref,
    sems,
):
    experts, _, groups, width = back_ref.shape
    rows = cot_ref.shape[0]
    half = width // 2
    many = min(MIX_ROWS // groups, experts)
    blocks = [slice(at, at + STEP) for at in range(0, rows, STEP)]
    sources = (kept_cot_ref, kept_hidden_ref, kept_turned_ref)
    targets = (cot_ref, hidden_ref, turned_ref)
    arriving = {}

    def load(kinds, at):
        for kind in kinds:
            here = blocks[at]
            arriving[kind, at] = push(sources[kind].at[here], targets[kind].at[here], sems.at[kind, at])

    rest = push(w_all_ref.at[:, 3 * width :], rest_ref, sems.at[6, 0])
    load((0, 1), 0)
    rest.wait()
    out_w = rest_ref[:, :width]
    small = jnp.transpose(rest_ref[:, width:])
    gain = small[experts : experts + 1, :].astype(f32)
    total_ref[...] = jnp.zeros_like(total_ref)

    def slots(place, first=0, count=experts):
        return back_ref[first : first + count, place].reshape(count * groups, width)

    for at, here in enumerate(blocks):
        arriving[0, at].wait()
        arriving[1, at].wait()
        if at + 1 < len(blocks):
            load((0, 1), at + 1)
        else:
            load((2,), 0)
            atts = [push(kept_own_ref, own_ref, sems.at[3, 0]), push(kept_away_ref, away_ref, sems.at[3, 1])]
        hidden = hidden_ref[here, :].astype(f32)
        normed = (hidden * rms_scale(hidden) * gain).astype(bf16)
        normed_ref[here, :] = normed
        mask = lax.broadcasted_iota(jnp.int32, (groups, STEP), 0) == gid_ref[:, here]
        for slot in range(0, experts, many):
            wide = dot(slots(0, slot, many), cot_ref[here, :], NT) + dot(slots(1, slot, many), normed, NT)
            for own in range(slot, slot + many):
                part = wide[(own - slot) * groups : (own - slot + 1) * groups]
                scaled = jnp.where(mask, part * wt_ref[own : own + 1, here], 0.0)
                part_ref[own : own + 1, here] = jnp.sum(scaled, axis=0, keepdims=True)
                total_ref[own] += jnp.sum(scaled, axis=1, keepdims=True)
    gain_total = jnp.zeros((1, width), f32)
    leaving = []
    for at, here in enumerate(blocks):
        mask = lax.broadcasted_iota(jnp.int32, (groups, STEP), 0) == gid_ref[:, here]
        for slot in range(experts):
            own = slice(slot, slot + 1)
            total = jnp.sum(jnp.where(mask, total_ref[slot], 0.0), axis=0, keepdims=True)
            gl_ref[own, here] = (part_ref[own, here] - wt_ref[own, here] * total).astype(bf16)
        hidden = hidden_ref[here, :].astype(f32)
        scale = rms_scale(hidden)
        unit = hidden * scale
        arriving[2, at].wait()
        if at + 1 < len(blocks):
            load((2,), at + 1)
        hidden_ref[here, :] = (hidden + dot(turned_ref[here, :], slots(0))).astype(bf16)
        leaving.append(push(hidden_ref.at[here], kept_out_ref.at[here], sems.at[4, at]))
        grad_normed = dot(turned_ref[here, :], slots(1)) + dot(gl_ref[:, here], small[:experts], TN)
        weighted = gain * grad_normed
        gain_total = gain_total + jnp.sum(grad_normed * unit, axis=0, keepdims=True)
        back = scale * (weighted - unit * jnp.mean(weighted * unit, axis=-1, keepdims=True))
        low = (cot_ref[here, :].astype(f32) + back).astype(bf16)
        cot_ref[here, :] = low
        leaving.append(push(cot_ref.at[here], kept_gh_ref.at[here], sems.at[5, at]))
        grad_att = dot(low, out_w, NT).astype(bf16)
        gown_ref[here, :] = grad_att[:, :half]
        gaway_ref[here, :] = grad_att[:, half:]
    for copy in atts:
        copy.wait()
    small_ref[:half, :width] = dot(own_ref[...], cot_ref[...], TN).astype(bf16)
    small_ref[half:, :width] = dot(away_ref[...], cot_ref[...], TN).astype(bf16)
    tail = [dot(gl_ref[...], normed_ref[...]), gain_total, jnp.zeros((127 - experts, width), f32)]
    small_ref[:, width:] = jnp.transpose(jnp.concatenate(tail, 0)).astype(bf16)
    for copy in leaving:
        copy.wait()


def unmix(back, weights, gid, gathered, turned, cotangent, hidden, att_own, att_away):
    rows, width = cotangent.shape
    experts, _, groups, _ = back.shape
    kept = (turned, cotangent, hidden, att_own, att_away)
    return call(
        unmix_kernel,
        (
            in_hbm((rows, width), bf16),
            in_hbm((rows, width), bf16),
            shape_of((rows, width // 2), bf16),
            shape_of((rows, width // 2), bf16),
            shape_of((width, width + 128), bf16),
        ),
        (pltpu.with_memory_space_constraint(back, pltpu.VMEM), weights, gid, from_hbm(gathered), *[from_hbm(array) for array in kept]),
        room=room_for(UNMIX_ROOM, experts * groups),
        in_specs=[VMEM, VMEM, VMEM] + [HBM] * 6,
        out_specs=[HBM] * 2 + [VMEM] * 3,
        scratch_shapes=[pltpu.VMEM(array.shape, bf16) for array in kept]
        + [
            pltpu.VMEM((width, width + 128), bf16),
            pltpu.VMEM((rows, width), bf16),
            pltpu.VMEM((experts, rows), f32),
            pltpu.VMEM((experts, groups, 1), f32),
            pltpu.VMEM((experts, rows), bf16),
            DMA((7, max(rows // STEP, 4))),
        ],
    )


def expert_kernel(
    pick_ref, in_ref, up_all_ref, down_all_ref, hint_ref,
    sent_ref, kept_act_ref, kept_pre_ref, kept_in_ref, mark_ref,
    up_ref, down_ref, act_ref, pre_ref, out_ref, load_sems, sems,
):
    parts, _, groups, width = in_ref.shape
    many = min(EXPERT_ROWS // groups, parts)
    pick = pick_ref[0]
    load_up = push(up_all_ref.at[pick], up_ref, load_sems.at[0])
    set_mark(mark_ref)
    copies = []
    for at, part in enumerate(range(0, parts, many)):
        here = slice(part * groups, (part + many) * groups)
        owners = slice(part, part + many)
        rows, grad = [in_ref[owners, place].reshape(many * groups, width) for place in range(2)]
        if at == 0:
            load_up.wait()
            load_down = push(down_all_ref.at[pick], down_ref, load_sems.at[1])
        pre = dot(rows, up_ref[...])
        if at == 0:
            load_down.wait()
            copies.append(push(in_ref, kept_in_ref, load_sems.at[2]))
        cdf = 0.5 + 0.5 * lax.erf(pre * 0.7071067811865476)
        slope = cdf + pre * (jnp.exp(-0.5 * pre * pre) * 0.3989422804014327)
        act = (pre * cdf).astype(bf16)
        act_ref[here, :] = act
        copies.append(push(act_ref.at[here], kept_act_ref.at[here], sems.at[0, at]))
        grad_pre = (dot(grad, down_ref[...], NT) * slope).astype(bf16)
        pre_ref[here, :] = grad_pre
        copies.append(push(pre_ref.at[here], kept_pre_ref.at[here], sems.at[1, at]))
        out_ref[owners, 0] = dot(act, down_ref[...]).astype(bf16).reshape(many, groups, width)
        out_ref[owners, 1] = dot(grad_pre, up_ref[...], NT).astype(bf16).reshape(many, groups, width)
        copies.append(push(out_ref.at[owners], sent_ref.at[owners], sems.at[2, at]))
    for copy in copies:
        copy.wait()


def expert_pass(pick, arrived, w_up, w_down, hint):
    parts, _, groups, width = arrived.shape
    rows = parts * groups
    hidden = w_up.shape[2]
    return call(
        expert_kernel,
        (
            in_hbm(arrived.shape, bf16),
            in_hbm((rows, hidden), bf16),
            in_hbm((rows, hidden), bf16),
            in_hbm(arrived.shape, bf16),
            shape_of(MARK, f32),
        ),
        (pick, pltpu.with_memory_space_constraint(arrived, pltpu.VMEM), from_hbm(w_up), from_hbm(w_down), hint),
        room=room_for(EXPERT_ROOM, rows),
        in_specs=[SMEM, VMEM, HBM, HBM, ANY],
        out_specs=[HBM, HBM, HBM, HBM, VMEM],
        scratch_shapes=[
            pltpu.VMEM(w_up.shape[1:], bf16),
            pltpu.VMEM(w_down.shape[1:], bf16),
            pltpu.VMEM((rows, hidden), bf16),
            pltpu.VMEM((rows, hidden), bf16),
            pltpu.VMEM(arrived.shape, bf16),
            DMA((3,)),
            DMA((3, max(rows // EXPERT_ROWS, 1))),
        ],
    )


def expert_grad_kernel(
    in_ref, kept_act_ref, kept_pre_ref, hint_ref, grad_ref, mark_ref, act_ref, pre_ref, out_ref, load_sems, sems
):
    shards, pieces, per, width = grad_ref.shape
    rows, hidden = act_ref.shape
    slabs = [slice(at, at + width) for at in range(0, hidden, width)]
    loads = [
        [push(kept.at[:, slab], ref.at[:, slab], load_sems.at[place, at]) for at, slab in enumerate(slabs)]
        for place, (kept, ref) in enumerate(((kept_act_ref, act_ref), (kept_pre_ref, pre_ref)))
    ]
    down_pieces = hidden // shards // per
    set_mark(mark_ref)
    mixed, grad = [in_ref[:, place].reshape(rows, width) for place in range(2)]
    for at, slab in enumerate(slabs):
        loads[0][at].wait()
        grad_down = dot(act_ref[:, slab], grad, TN).astype(bf16)
        span = width // (down_pieces * per)
        out_ref[at * span : (at + 1) * span, :down_pieces] = grad_down.reshape(span, down_pieces, per, width)
    copies = [push(out_ref.at[:, :down_pieces], grad_ref.at[:, :down_pieces], sems.at[0])]
    for at, slab in enumerate(slabs):
        loads[1][at].wait()
        grad_up = dot(mixed, pre_ref[:, slab], TN).astype(bf16)
        out_ref[:, down_pieces + at] = grad_up.reshape(shards, per, width)
    copies.append(push(out_ref.at[:, down_pieces:], grad_ref.at[:, down_pieces:], sems.at[1]))
    for copy in copies:
        copy.wait()


def expert_grads(arrived, act, grad_pre, shards, hint):
    width = arrived.shape[3]
    hidden = act.shape[1]
    per = width // shards
    grad = (shards, (hidden // shards) // per + hidden // width, per, width)
    return call(
        expert_grad_kernel,
        (in_hbm(grad, bf16), shape_of(MARK, f32)),
        (arrived, from_hbm(act), from_hbm(grad_pre), hint),
        room=room_for(GRAD_ROOM, act.shape[0]),
        in_specs=[VMEM, HBM, HBM, ANY],
        out_specs=[HBM, VMEM],
        scratch_shapes=[
            pltpu.VMEM(act.shape, bf16),
            pltpu.VMEM(act.shape, bf16),
            pltpu.VMEM(grad, bf16),
            DMA((2, hidden // width)),
            DMA((2,)),
        ],
    )


def shard_sum_kernel(in_ref, down_ref, up_ref):
    total = in_ref[0, 0].astype(f32)
    for part in range(1, in_ref.shape[0]):
        total = total + in_ref[part, 0].astype(f32)
    down_rows, width = down_ref.shape[1:]
    down_ref[0] = total[:down_rows]
    per = up_ref.shape[1]
    for at in range(0, up_ref.shape[2] // width):
        here = down_rows + at * per
        up_ref[0, :, at * width : (at + 1) * width] = total[here : here + per]


def shard_sum(parts, per_owner, down_rows, up_rows):
    shards, tall, width = parts.shape
    parts = parts.reshape(shards // per_owner, per_owner, tall, width)
    hidden = (tall - down_rows) // up_rows * width
    return call(
        shard_sum_kernel,
        (
            in_hbm((per_owner, down_rows, width), f32),
            in_hbm((per_owner, up_rows, hidden), f32),
        ),
        (parts,),
        grid=(per_owner,),
        in_specs=[pl.BlockSpec((parts.shape[0], 1, tall, width), lambda at: (0, at, 0, 0))],
        out_specs=[
            pl.BlockSpec((1, down_rows, width), lambda at: (at, 0, 0)),
            pl.BlockSpec((1, up_rows, hidden), lambda at: (at, 0, 0)),
        ],
    )


def own_grad_kernel(unit_t_ref, grad_ref, w_ref, grad_w_ref, part_ref):
    wide = grad_ref.shape[1]
    grad_w_ref[...] = dot(unit_t_ref[...], grad_ref[...])
    for at in range(0, part_ref.shape[0], 1024):
        here = slice(at, at + 1024)
        part_ref[here, :] = dot(grad_ref[here, :], w_ref[:, :wide], NT)


def own_grad(unit_t, grad, weights):
    width, rows = unit_t.shape
    return call(
        own_grad_kernel,
        (shape_of((width, grad.shape[1]), f32), shape_of((rows, width), f32)),
        (unit_t, grad, weights),
        room=16,
        in_specs=[VMEM] * 3,
        out_specs=[VMEM] * 2,
    )


def away_grad_kernel(mine_ref, unit_t_ref, grad_ref, own_ref, small_ref, keep_ref, send_ref, total_ref):
    total_ref[...] = dot(unit_t_ref[...], grad_ref[...])
    many, per, _ = keep_ref.shape
    mine = mine_ref[0]
    left = own_ref.shape[1]
    right = left + total_ref.shape[1]
    for place in range(many):
        for part, ref in ((mine, keep_ref), (1 - mine, send_ref)):
            rows = pl.ds(pl.multiple_of((2 * place + part) * per, per), per)
            ref[place, :, :left] = own_ref[rows, :].astype(ref.dtype)
            ref[place, :, left:right] = total_ref[rows, :].astype(ref.dtype)
            ref[place, :, right:] = small_ref[rows, :].astype(ref.dtype)


def halves(array, mine):
    keep, send = [lax.dynamic_index_in_dim(array, part[0], 1, keepdims=False) for part in (mine, 1 - mine)]
    return keep, send.astype(bf16)


def away_grad(mine, unit_t, grad, own, small, devices):
    width, rows = unit_t.shape
    wide = grad.shape[1]
    per = width // devices
    if per % 16:
        total = jnp.concatenate([own, dot(unit_t, grad), small.astype(f32)], 1)
        return halves(total.reshape(devices // 2, 2, per, -1), mine)
    dims = (devices // 2, per, own.shape[1] + wide + small.shape[1])
    return call(
        away_grad_kernel,
        (shape_of(dims, f32), shape_of(dims, bf16)),
        (mine, unit_t, grad, own, small),
        room=16,
        in_specs=[SMEM] + [VMEM] * 4,
        out_specs=[VMEM] * 2,
        scratch_shapes=[pltpu.VMEM((width, wide), f32)],
    )


def token_grad_kernel(part_ref, grad_ref, w_ref, tok_ref, gh_ref, out_ref, mark_ref):
    set_mark(mark_ref)
    wide = grad_ref.shape[1]
    for at in range(0, tok_ref.shape[0], 512):
        here = slice(at, at + 512)
        weighted = part_ref[here, :] + dot(grad_ref[here, :], w_ref[:, wide : 2 * wide], NT)
        source = tok_ref[here, :].astype(f32)
        scale = rms_scale(source)
        unit = source * scale
        back = scale * (weighted - unit * jnp.mean(weighted * unit, axis=-1, keepdims=True))
        out_ref[here, :] = (gh_ref[here, :].astype(f32) + back).astype(bf16)


def token_grad(part, grad, weights, tokens, grad_hidden):
    return call(
        token_grad_kernel,
        (shape_of(tokens.shape, bf16), shape_of(MARK, f32)),
        (part, grad, weights, tokens, grad_hidden),
        room=16,
        in_specs=[VMEM] * 5,
        out_specs=[VMEM] * 2,
    )


def swap(array, axis, size, bit):
    return lax.ppermute(array, axis, [(at, at ^ bit) for at in range(size)])


def axis_bits(sizes):
    bits = []
    for axis, size in sizes:
        bit = size // 2
        while bit:
            bits.append((axis, size, bit))
            bit //= 2
    return bits


def gather_rows(shard, sizes, meanwhile):
    bits = axis_bits(sizes)
    held = shard[(None,) * len(bits)]
    for place, (axis, size, bit) in enumerate(bits):
        other = swap(held, axis, size, bit)
        if place == len(bits) - 2:
            other, meanwhile = lax.optimization_barrier((other, meanwhile))
        upper = (lax.axis_index(axis) // bit) % 2 == 1
        first = jnp.where(upper, other, held)
        second = jnp.where(upper, held, other)
        held = jnp.concatenate([first, second], axis=place)
    return held.reshape((shard.shape[0] * 2 ** len(bits),) + shard.shape[1:]), meanwhile


def add_split_kernel(mine_ref, keep_ref, got_ref, hint_ref, next_keep_ref, send_ref):
    mine = mine_ref[0]
    for part, ref in ((mine, next_keep_ref), (1 - mine, send_ref)):
        value = keep_ref[:, pl.ds(part, 1)] + got_ref[:, pl.ds(part, 1)].astype(f32)
        ref[...] = value[:, 0].astype(ref.dtype)


def add_split(mine, keep, got, hint):
    many, per, wide = keep.shape
    dims = (many // 2, per, wide)
    keep, got = [array.reshape(many // 2, 2, per, wide) for array in (keep, got)]
    if per % 16:
        return halves(keep + got.astype(f32), mine)
    return call(
        add_split_kernel,
        (shape_of(dims, f32), shape_of(dims, bf16)),
        (mine, keep, got, hint),
        room=16,
        in_specs=[SMEM, VMEM, VMEM, ANY],
        out_specs=[VMEM] * 2,
    )


def scatter_rows(keep, send, sizes, hints):
    bits = axis_bits(sizes)[::-1]
    for place, (axis, size, bit) in enumerate(bits):
        got = swap(send, axis, size, bit)
        if place + 1 == len(bits):
            return keep, got
        axis, size, bit = bits[place + 1]
        mine = ((lax.axis_index(axis) // bit) % 2).astype(jnp.int32).reshape(1)
        keep, send = add_split(mine, keep, got, hints.get(place, got))


def on_device(
    n_dp, n_owner, tokens, seq_lengths, group_map, gain_attn, gain_mix, w_qkv, w_out, w_ctrl, w_up, w_down, cotangent
):
    rows, width = tokens.shape
    experts = w_ctrl.shape[1]
    per_owner = w_up.shape[0]
    groups = rows // G
    parts = n_dp // per_owner
    sizes = (("dp", n_dp), ("expert", n_owner))
    dp = lax.axis_index("dp")
    pick = (dp % per_owner).astype(jnp.int32).reshape(1)

    gain_row = gain_attn.reshape(1, -1)
    shard = call(
        functools.partial(pack_kernel, n_owner),
        shape_of((w_ctrl.shape[0], 4 * width + 128), bf16),
        (seq_lengths, *[from_hbm(array) for array in (w_qkv, gain_row, w_out, w_ctrl, gain_mix.reshape(1, -1))]),
        room=8,
        in_specs=[SMEM] + [VMEM] * 5,
        out_specs=VMEM,
    )

    def neighbour(array):
        return swap(array, "expert", n_owner, 1)

    unit_one, unit_away, unit_t, gid = call(
        prep_kernel,
        (
            in_hbm((rows, width), bf16),
            in_hbm((rows, width), bf16),
            in_hbm((width, rows), bf16),
            shape_of((1, rows), jnp.int32),
        ),
        (tokens, neighbour(tokens), group_map.reshape(groups, G)),
        room=16,
        in_specs=[VMEM] * 3,
        out_specs=[HBM, HBM, HBM, VMEM],
        scratch_shapes=[pltpu.VMEM((rows, width), bf16)] * 2 + [pltpu.VMEM((width, rows), bf16), DMA((3,))],
    )
    gathered, (unit_one, unit_away) = gather_rows(shard, sizes, (unit_one, unit_away))
    triple = 3 * width

    near = (dp * n_owner + (lax.axis_index("expert") ^ 1)) * w_ctrl.shape[0]
    lengths, att_own, att_away, lse_own, lse_away, own_qkv, away_qkv, kept_away = attend_forward(
        seq_lengths, near.astype(jnp.int32).reshape(1), unit_one, unit_away, gathered
    )
    hidden, weights, mixed, kept_own, kept_back = mix(
        tokens, att_own, neighbour(att_away), gathered, gid, cotangent, experts
    )

    teams = [
        [(part * per_owner + low) * n_owner + owner for low in range(per_owner) for owner in range(n_owner)]
        for part in range(parts)
    ]

    def exchange(array):
        return lax.all_to_all(
            array, ("dp", "expert"), split_axis=0, concat_axis=0, axis_index_groups=teams, tiled=True
        )

    arrived = exchange(mixed)
    turned, mark = turn(weights, gid, groups)
    results, act, grad_pre, arrived, mark = expert_pass(pick, arrived, w_up, w_down, mark)
    back = exchange(results)
    grad_experts, mark = expert_grads(arrived, act, grad_pre, n_dp, mark)
    shards = lax.all_to_all(
        grad_experts.reshape(n_dp, -1, width), "dp", split_axis=0, concat_axis=0, tiled=True
    )
    output, grad_hidden, grad_own, grad_away, grad_small = unmix(
        back, weights, gid, gathered, turned, cotangent, hidden, kept_own, kept_back
    )

    grad_here = neighbour(grad_away)
    grad_one = attend_backward(0, lengths, own_qkv, grad_own, kept_own, lse_own, grad_own)
    grad_two = neighbour(attend_backward(1, lengths, away_qkv, grad_here, kept_away, lse_away, grad_one))
    grad_w_own, token_part = own_grad(unit_t, grad_one, gathered)
    axis, size, bit = axis_bits(sizes)[-1]
    mine = ((lax.axis_index(axis) // bit) % 2).astype(jnp.int32).reshape(1)
    keep, send = away_grad(mine, unit_t, grad_two, grad_w_own, grad_small, n_dp * n_owner)
    grad_tokens, token_mark = token_grad(token_part, grad_two, gathered, tokens, grad_hidden)
    grad_down_shard, grad_up_shard = shard_sum(shards, per_owner, w_down.shape[1] // n_dp, width // n_dp)
    keep, got = scatter_rows(keep, send, sizes, {1: token_mark})
    own_rows = w_qkv.shape[0]
    shard_qkv, shard_out, shard_ctrl, shard_gain_one, shard_gain_two = call(
        functools.partial(finish_kernel, n_owner),
        (
            shape_of(w_qkv.shape, f32),
            shape_of(w_out.shape, f32),
            shape_of(w_ctrl.shape, f32),
            shape_of((1, own_rows), f32),
            shape_of((1, own_rows), f32),
        ),
        (keep, got, gain_row, w_qkv),
        room=8,
        in_specs=[VMEM] * 4,
        out_specs=[VMEM] * 5,
    )
    return (
        output,
        grad_tokens,
        shard_gain_one.reshape(-1),
        shard_gain_two.reshape(-1),
        shard_qkv,
        shard_out,
        shard_ctrl,
        grad_up_shard,
        grad_down_shard,
    )


def solution(mesh):
    both = ("dp", "expert")
    rows = P(both, None)
    return jax.shard_map(
        functools.partial(on_device, mesh.shape["dp"], mesh.shape["expert"]),
        mesh=mesh,
        in_specs=(
            rows, P(both), rows, P(both), P(both), rows, rows, rows,
            P("expert", None, None), P("expert", None, None), rows,
        ),
        out_specs=(
            rows, rows, P(both), P(both), rows, rows, rows,
            P("expert", "dp", None), P("expert", "dp", None),
        ),
        check_vma=False,
    )
```

```python
import functools

import jax
import jax.numpy as jnp
from jax import lax
from jax.experimental import pallas as pl
from jax.experimental.pallas import tpu as pltpu
from jax.sharding import PartitionSpec as P

HEADS = 8
G = 32
BQ = 256

ANY = pl.BlockSpec(memory_space=pl.ANY)
VMEM = pl.BlockSpec(memory_space=pltpu.VMEM)
HBM = pl.BlockSpec(memory_space=pltpu.HBM)
DMA = pltpu.SemaphoreType.DMA
SMEM = pl.BlockSpec(memory_space=pltpu.SMEM)

eps_norm = 1e-05
masked_value = -1e30
bf16 = jnp.bfloat16
f32 = jnp.float32
NN = (((1,), (0,)), ((), ()))
NT = (((1,), (1,)), ((), ()))
TN = (((0,), (0,)), ((), ()))


def dot(left, right, dims=NN):
    return lax.dot_general(left, right, dims, preferred_element_type=f32)


def rms_scale(values):
    return lax.rsqrt(jnp.mean(values * values, axis=-1, keepdims=True) + eps_norm)


def call(body, out_shape, args, room=28, **extra):
    return pl.pallas_call(
        body,
        out_shape=out_shape,
        compiler_params=pltpu.CompilerParams(vmem_limit_bytes=room * 2**20),
        name=getattr(body, "func", body).__name__,
        **extra,
    )(*args)


def shape_of(dims, kind):
    return jax.ShapeDtypeStruct(dims, kind)


def in_hbm(dims, kind):
    return pltpu.HBM(dims, kind)


def in_vmem(dims, kind):
    return pltpu.VMEM(dims, kind)


def from_hbm(array):
    return pltpu.with_memory_space_constraint(array, pltpu.HBM)


def room_for(parts, rows):
    fixed, per_block = parts
    return fixed + per_block * rows // 1024


def push(source, target, sem):
    copy = pltpu.make_async_copy(source, target, sem)
    copy.start()
    return copy


MARK = (8, 128)


def set_mark(ref):
    ref[...] = jnp.zeros(MARK, f32)


def diagonal(size):
    return lax.broadcasted_iota(jnp.int32, (size, size), 0) == lax.broadcasted_iota(jnp.int32, (size, size), 1)


def column_of(row):
    return jnp.sum(jnp.where(diagonal(row.shape[1]), row, 0.0), axis=1, keepdims=True)


def row_of(column):
    return jnp.sum(jnp.where(diagonal(column.shape[0]), column, 0.0), axis=0, keepdims=True)


def slot_matrix(experts, wide, n_owner, kind):
    expert = lax.broadcasted_iota(jnp.int32, (experts, wide), 0)
    slot = lax.broadcasted_iota(jnp.int32, (experts, wide), 1)
    per_owner = experts // n_owner
    return jnp.where(expert % per_owner * n_owner + expert // per_owner == slot, 1.0, 0.0).astype(kind)


def pack_kernel(n_owner, len_ref, wqkv_ref, gain_ref, wout_ref, ctrl_ref, mix_ref, out_ref):
    width = wout_ref.shape[1]
    experts = ctrl_ref.shape[1]
    gain = column_of(gain_ref[...].astype(f32))
    for pair in range(width // 128):
        for part in range(3):
            at = part * width + pair * 128
            to = pair * 384 + part * 128
            out_ref[:, to : to + 128] = (wqkv_ref[:, at : at + 128].astype(f32) * gain).astype(bf16)
    out_ref[:, 3 * width : 4 * width] = wout_ref[...]
    small = dot(ctrl_ref[...], slot_matrix(experts, 128, n_owner, bf16))
    lane = lax.broadcasted_iota(jnp.int32, small.shape, 1)
    small = jnp.where(lane == experts, column_of(mix_ref[...].astype(f32)), small)
    small = jnp.where(lane == 127, len_ref[0].astype(f32), small)
    out_ref[:, 4 * width :] = small.astype(bf16)


def finish_kernel(n_owner, keep_ref, got_ref, gain_ref, wqkv_ref, qkv_ref, out_ref, ctrl_ref, one_ref, mix_ref):
    width = out_ref.shape[1]
    experts = ctrl_ref.shape[1]
    total = keep_ref[0] + got_ref[0].astype(f32)
    gain = column_of(gain_ref[...].astype(f32))
    grad_gain = jnp.zeros((total.shape[0], 128), f32)
    for pair in range(width // 128):
        for part in range(3):
            to = part * width + pair * 128
            at = pair * 384 + part * 128
            grad = total[:, at : at + 128]
            qkv_ref[:, to : to + 128] = gain * grad
            grad_gain = grad_gain + wqkv_ref[:, to : to + 128].astype(f32) * grad
    out_ref[...] = total[:, 3 * width : 4 * width]
    small = total[:, 4 * width :]
    slots = slot_matrix(experts, 128, n_owner, f32)
    ctrl_ref[...] = lax.dot_general(small, slots, NT, precision=lax.Precision.HIGHEST, preferred_element_type=f32)
    one_ref[...] = row_of(jnp.sum(grad_gain, axis=1, keepdims=True))
    lane = lax.broadcasted_iota(jnp.int32, small.shape, 1)
    mix_ref[...] = row_of(jnp.sum(jnp.where(lane == experts, small, 0.0), axis=1, keepdims=True))


def prep_kernel(
    tok_ref, tok_away_ref, gmap_ref, kept_ref, kept_away_ref, kept_t_ref, gid_ref, unit_ref, away_ref, unit_t_ref, sems
):
    rows = tok_ref.shape[0]
    step = 512
    copies = []
    sides = ((tok_ref, unit_ref, kept_ref), (tok_away_ref, away_ref, kept_away_ref))
    for side, (source, target, kept) in enumerate(sides):
        for at in range(0, rows, step):
            here = slice(at, at + step)
            block = source[here, :].astype(f32)
            unit = (block * rms_scale(block)).astype(bf16)
            target[here, :] = unit
            copies.append(push(target.at[here], kept.at[here], sems.at[side, at // step]))
            if side == 0:
                unit_t_ref[:, here] = jnp.transpose(unit)
        if side == 0:
            copies.append(push(unit_t_ref, kept_t_ref, sems.at[2, 0]))
    groups = rows // G
    places = lax.broadcasted_iota(jnp.int32, (groups, rows), 1)
    group_at = lax.broadcasted_iota(jnp.int32, (groups, rows), 0)
    gmap = gmap_ref[...]
    member = jnp.zeros((groups, rows), jnp.int32)
    for slot in range(G):
        member = jnp.where(gmap[:, slot : slot + 1] == places, group_at, member)
    gid_ref[...] = jnp.sum(member.astype(f32), axis=0, keepdims=True).astype(jnp.int32)
    for copy in copies:
        copy.wait()


def lower_mask():
    return lax.broadcasted_iota(jnp.int32, (BQ, BQ), 0) <= lax.broadcasted_iota(jnp.int32, (BQ, BQ), 1)


def head_lanes():
    return lax.broadcasted_iota(jnp.int32, (1, 128), 1) // 64


def attend_pair(length, pair, qkv_all_ref, out_ref, lse_all_ref, vt_ref):
    qkv_ref = qkv_all_ref.at[:, pl.ds(pl.multiple_of(pair * 384, 384), 384)]
    lse_ref = lse_all_ref.at[pl.ds(pair, 1)]
    rows = qkv_ref.shape[0]
    step, ahead = 512, 4
    lane = head_lanes()
    vt_ref[...] = jnp.transpose(qkv_ref[:, 256:384])

    def run(low_of):
        items = []
        for at in range(0, rows, BQ):
            chunks = [(at, BQ)]
            top = at
            while top > low_of(at):
                down = max(low_of(at), top - step)
                chunks.append((down, top - down))
                top = down
            for place, (low, wide) in enumerate(chunks):
                for head in range(2):
                    items.append((at, head, low, wide, place == 0, place == len(chunks) - 1))

        def score(at, head, low, wide, first, last):
            own = jnp.where(lane == head, qkv_ref[at : at + BQ, 0:128] * bf16(0.125), bf16(0))
            scores = dot(qkv_ref[low : low + wide, 128:256], own, NT)
            return jnp.where(lower_mask(), scores, masked_value) if first else scores

        pending = [score(*item) for item in items[:ahead]]
        state = {}
        for place, (at, head, low, wide, first, last) in enumerate(items):
            if place + ahead < len(items):
                pending.append(score(*items[place + ahead]))
            scores = pending.pop(0)
            peak = jnp.max(scores, axis=0, keepdims=True)
            if not first:
                old_peak, old_total, old_mixed = state[head]
                peak = jnp.maximum(old_peak, peak)
                shrink = jnp.exp(old_peak - peak)
            probs = jnp.exp(scores - peak)
            total = jnp.sum(probs, axis=0, keepdims=True)
            mixed = dot(vt_ref[64 * head : 64 * head + 64, low : low + wide], probs.astype(bf16))
            if not first:
                total = total + old_total * shrink
                mixed = mixed + old_mixed * shrink
            state[head] = (peak, total, mixed)
            if last:
                lse_ref[0, head : head + 1, at : at + BQ] = peak + jnp.log(total)
                if head == 1:
                    both = [state[own][2] * (1.0 / state[own][1]) for own in range(2)]
                    out_ref[at : at + BQ, :] = jnp.transpose(jnp.concatenate(both, 0)).astype(bf16)

    @pl.when(length == BQ)
    def _():
        run(lambda at: at)

    @pl.when(length != BQ)
    def _():
        run(lambda at: 0)


def attend_kernel(
    len_ref, place_ref, kept_own_ref, kept_away_ref, w_ref,
    lens_ref, own_ref, away_ref, lse_own_ref, lse_away_ref, kept_qkv_own_ref, kept_qkv_away_ref, kept_out_ref,
    unit_ref, qkv_ref, out_ref, lse_ref, vt_ref, unit_sems, sems,
):
    row = pl.multiple_of(place_ref[0] // 16 * 16, 16)
    tile = w_ref[pl.ds(row, 16), w_ref.shape[1] - 128 :].astype(f32)
    chosen = lax.broadcasted_iota(jnp.int32, tile.shape, 1) == 127
    chosen = chosen & (lax.broadcasted_iota(jnp.int32, tile.shape, 0) == place_ref[0] % 16)
    lens_ref[0] = len_ref[0]
    lens_ref[1] = jnp.max(jnp.where(chosen, tile, 0.0)).astype(jnp.int32)
    rows, wide = qkv_ref.shape
    half = wide // 2
    pairs = wide // 384
    count = unit_sems.shape[0] // 2
    blocks = [slice(at, at + rows // count) for at in range(0, rows, rows // count)]
    kept = (kept_qkv_own_ref, kept_qkv_away_ref)
    copies, keeping = [], []

    def load(at):
        if at < 2 * count:
            source = (kept_own_ref, kept_away_ref)[at // count]
            copies.append(push(source.at[blocks[at % count]], unit_ref.at[at % 3], unit_sems.at[at]))

    load(0)
    load(1)
    for at in range(2 * count):
        side = at // count
        copies[at].wait()
        load(at + 2)
        columns = slice(side * half, (side + 1) * half)
        qkv_ref[blocks[at % count], columns] = dot(unit_ref[at % 3], w_ref[:, columns]).astype(bf16)
        if at % count == count - 1:
            keeping.append(push(qkv_ref.at[:, columns], kept[side], sems.at[side]))

    def keep_out(pair):
        thin = pl.ds(pl.multiple_of((pair - pairs // 2) * 128, 128), 128)
        return pltpu.make_async_copy(away_ref.at[:, thin], kept_out_ref.at[:, thin], sems.at[2 + pair])

    @pl.loop(0, pairs)
    def _(pair):
        mine = pair < pairs // 2
        attend_pair(lens_ref[jnp.where(mine, 0, 1)], pair, qkv_ref, out_ref, lse_ref, vt_ref)

        @pl.when(mine)
        def _():
            own_ref[:, pl.ds(pl.multiple_of(pair * 128, 128), 128)] = out_ref[...]

        @pl.when(jnp.logical_not(mine))
        def _():
            away_ref[:, pl.ds(pl.multiple_of((pair - pairs // 2) * 128, 128), 128)] = out_ref[...]
            keep_out(pair).start()

    lse_own_ref[...] = lse_ref[: pairs // 2]
    lse_away_ref[...] = lse_ref[pairs // 2 :]
    for copy in keeping:
        copy.wait()
    for pair in range(pairs // 2, pairs):
        keep_out(pair).wait()


def attend_forward(length, place, unit, unit_away, gathered):
    rows, width = unit.shape
    pairs = width // 128
    count = 4
    half = pairs // 2
    lse = shape_of((half, 2, rows), f32)
    return call(
        attend_kernel,
        (
            shape_of((2,), jnp.int32),
            shape_of((rows, 128 * half), bf16),
            shape_of((rows, 128 * half), bf16),
            lse,
            lse,
            in_hbm((rows, 384 * half), bf16),
            in_hbm((rows, 384 * half), bf16),
            in_hbm((rows, 128 * half), bf16),
        ),
        (length, place, from_hbm(unit), from_hbm(unit_away), gathered),
        room=ATTEND_ROOM,
        in_specs=[SMEM, SMEM, HBM, HBM, VMEM],
        out_specs=[SMEM] + [VMEM] * 4 + [HBM] * 3,
        scratch_shapes=[
            pltpu.VMEM((3, rows // count, width), bf16),
            pltpu.VMEM((rows, 384 * pairs), bf16),
            pltpu.VMEM((rows, 128), bf16),
            pltpu.VMEM((pairs, 2, rows), f32),
            pltpu.VMEM((128, rows), bf16),
            DMA((2 * count,)),
            DMA((2 + pairs,)),
        ],
    )


def attend_back_kernel(side, lens_ref, qkv_ref, go_ref, o_ref, lse_ref, hint_ref, grad_ref, *scratch):
    @pl.loop(0, qkv_ref.shape[1] // 384)
    def _(pair):
        wide = pl.ds(pl.multiple_of(pair * 384, 384), 384)
        thin = pl.ds(pl.multiple_of(pair * 128, 128), 128)
        refs = [qkv_ref.at[:, wide], go_ref.at[:, thin], o_ref.at[:, thin], lse_ref.at[pl.ds(pair, 1)]]
        attend_back_pair(lens_ref[side], *refs, grad_ref.at[:, wide], *scratch)


def attend_back_pair(length, qkv_ref, go_ref, o_ref, lse_ref, grad_ref, gqt_ref, kt_ref, dl_ref):
    rows = qkv_ref.shape[0]
    step, ahead = 512, 1
    lane = head_lanes()
    kt_ref[...] = jnp.transpose(qkv_ref[:, 128:256]) * bf16(0.125)
    product = (go_ref[...].astype(f32) * o_ref[...].astype(f32)).astype(bf16)
    of_head = lax.broadcasted_iota(jnp.int32, (8, 128), 0) == lax.broadcasted_iota(jnp.int32, (8, 128), 1) // 64
    dl_ref[...] = dot(jnp.where(of_head, 1.0, 0.0).astype(bf16), product, NT)

    def run(end_of):
        items = []
        for low in range(0, rows, BQ):
            end = end_of(low)
            chunks = [(low, BQ)] + [(at, min(step, end - at)) for at in range(low + BQ, end, step)]
            for place, (at, wide) in enumerate(chunks):
                for head in range(2):
                    items.append((low, head, at, wide, place == 0, place == len(chunks) - 1))
        blocks = {}
        written = set()

        def products(low, head, at, wide, first, last):
            if (low, head) not in blocks:
                keys = qkv_ref[low : low + BQ, 128:256] * bf16(0.125)
                vals = qkv_ref[low : low + BQ, 256:384]
                blocks[low, head] = [jnp.where(lane == head, own, bf16(0)) for own in (keys, vals)]
            keys, vals = blocks[low, head]
            return (
                dot(keys, qkv_ref[at : at + wide, 0:128], NT),
                dot(vals, go_ref[at : at + wide, :], NT),
            )

        pending = [products(*item) for item in items[:ahead]]
        grad_k, grad_v = {}, {}
        for place, (low, head, at, wide, first, last) in enumerate(items):
            if place + ahead < len(items):
                pending.append(products(*items[place + ahead]))
            scores, grad_probs = pending.pop(0)
            here = slice(at, at + wide)
            probs = jnp.exp(scores - lse_ref[0, head : head + 1, here])
            if first:
                probs = jnp.where(lower_mask(), probs, 0.0)
            grad_scores = (probs * (grad_probs - dl_ref[head : head + 1, here])).astype(bf16)
            more_v = dot(probs.astype(bf16), go_ref[here, :])
            more_k = dot(grad_scores, qkv_ref[here, 0:128])
            grad_v[head] = more_v if first else grad_v[head] + more_v
            grad_k[head] = more_k if first else grad_k[head] + more_k
            span = slice(64 * head, 64 * head + 64)
            more_q = dot(kt_ref[span, low : low + BQ], grad_scores)
            fresh = (head, at + wide) not in written
            written.update((head, top) for top in range(at + BQ, at + wide + BQ, BQ))
            if fresh:
                gqt_ref[span, here] = more_q
            else:
                gqt_ref[span, here] += more_q
            if last and head == 1:
                there = slice(low, low + BQ)
                grad_ref[there, 128:256] = (jnp.where(lane == 0, grad_k[0], grad_k[1]) * 0.125).astype(bf16)
                grad_ref[there, 256:384] = jnp.where(lane == 0, grad_v[0], grad_v[1]).astype(bf16)

    @pl.when(length == BQ)
    def _():
        run(lambda low: low + BQ)

    @pl.when(length != BQ)
    def _():
        run(lambda low: rows)

    grad_ref[:, 0:128] = jnp.transpose(gqt_ref[...]).astype(bf16)


def attend_backward(side, lengths, qkv, grad_attended, attended, log_totals, hint):
    rows = qkv.shape[0]
    return call(
        functools.partial(attend_back_kernel, side),
        shape_of(qkv.shape, bf16),
        (lengths, qkv, grad_attended, attended, log_totals, hint),
        room=ATTEND_ROOM,
        in_specs=[SMEM, VMEM, VMEM, VMEM, VMEM, ANY],
        out_specs=VMEM,
        scratch_shapes=[pltpu.VMEM((128, rows), f32), pltpu.VMEM((128, rows), bf16), pltpu.VMEM((8, rows), f32)],
    )


STEP = 512
UNMIX_ROOM = (24, 12)
MIX_ROOM = (12, 12)
ATTEND_ROOM = 24
EXPERT_ROOM = (20, 16)
GRAD_ROOM = (16, 20)
EXPERT_ROWS = 512
MIX_ROWS = 1024


def member_mask(gid_ref, groups):
    wide = gid_ref.shape[1]
    return lax.broadcasted_iota(jnp.int32, (groups, wide), 0) == gid_ref[...]


def mix_kernel(
    tok_ref, own_ref, away_ref, w_all_ref, gid_ref, cot_ref,
    kept_hidden_ref, wt_ref, sent_ref, kept_own_ref, kept_away_ref, normed_ref, w_ref, hidden_ref, mixed_ref, sems, send_sems,
):
    copies = [push(away_ref, kept_away_ref, sems.at[0]), push(own_ref, kept_own_ref, sems.at[2])]
    rows, width = tok_ref.shape
    experts, _, groups, _ = mixed_ref.shape
    half = width // 2
    out_w = w_all_ref[:, 3 * width : 4 * width]
    small = jnp.transpose(w_all_ref[:, 4 * width :])
    gain = small[experts : experts + 1, :].astype(f32)
    for at in range(0, rows, 512):
        here = slice(at, at + 512)
        hidden = tok_ref[here, :].astype(f32) + dot(own_ref[here, :], out_w[:half])
        hidden = (hidden + dot(away_ref[here, :], out_w[half:])).astype(bf16)
        hidden_ref[here, :] = hidden
        hidden = hidden.astype(f32)
        normed_ref[here, :] = (hidden * rms_scale(hidden) * gain).astype(bf16)
    copies.append(push(hidden_ref, kept_hidden_ref, sems.at[1]))
    logits = dot(small[:experts], normed_ref[...], NT)
    mask = member_mask(gid_ref, groups)
    for slot in range(experts):
        wide = jnp.where(mask, logits[slot : slot + 1, :], masked_value)
        wide = jnp.exp(wide - jnp.max(wide, axis=1, keepdims=True))
        wide = wide * (1.0 / jnp.sum(wide, axis=1, keepdims=True))
        wt_ref[slot : slot + 1, :] = jnp.sum(wide, axis=0, keepdims=True)
        w_ref[slot * groups : (slot + 1) * groups, :] = wide.astype(bf16)
    many = min(512 // groups, experts)
    for place, ref in enumerate((normed_ref, cot_ref)):
        for slot in range(0, experts, many):
            mixed = dot(w_ref[slot * groups : (slot + many) * groups, :], ref[...]).astype(bf16)
            own = slice(slot, slot + many)
            mixed_ref[own, place] = mixed.reshape(many, groups, width)
            copies.append(push(mixed_ref.at[own, place], sent_ref.at[own, place], send_sems.at[place, slot // many]))
    for copy in copies:
        copy.wait()


def mix(tokens, att_own, att_away, gathered, gid, cotangent, experts):
    rows, width = tokens.shape
    groups = rows // G
    sent = (experts, 2, groups, width)
    return call(
        mix_kernel,
        (
            in_hbm((rows, width), bf16),
            shape_of((experts, rows), f32),
            in_hbm(sent, bf16),
            in_hbm(att_own.shape, bf16),
            in_hbm(att_away.shape, bf16),
        ),
        (tokens, att_own, att_away, gathered, gid, cotangent),
        room=room_for(MIX_ROOM, experts * groups),
        in_specs=[VMEM] * 6,
        out_specs=[HBM, VMEM, HBM, HBM, HBM],
        scratch_shapes=[
            pltpu.VMEM((rows, width), bf16),
            pltpu.VMEM((experts * groups, rows), bf16),
            pltpu.VMEM((rows, width), bf16),
            pltpu.VMEM(sent, bf16),
            DMA((3,)),
            DMA((2, max(experts * groups // 512, 1))),
        ],
    )


def turn_kernel(wt_ref, gid_ref, kept_ref, mark_ref, turned_ref, sem):
    set_mark(mark_ref)
    experts, rows = wt_ref.shape
    groups = turned_ref.shape[1] // experts
    many = 256 // groups
    for at in range(0, rows, STEP):
        here = slice(at, at + STEP)
        mask = lax.broadcasted_iota(jnp.int32, (groups, STEP), 0) == gid_ref[:, here]
        for slot in range(0, experts, many):
            parts = [
                jnp.where(mask, wt_ref[own : own + 1, here], 0.0).astype(bf16) for own in range(slot, slot + many)
            ]
            turned_ref[here, slot * groups : (slot + many) * groups] = jnp.transpose(jnp.concatenate(parts, 0))
    push(turned_ref, kept_ref, sem).wait()


def turn(weights, gid, groups):
    experts, rows = weights.shape
    return call(
        turn_kernel,
        (in_hbm((rows, experts * groups), bf16), shape_of(MARK, f32)),
        (weights, gid),
        room=16,
        in_specs=[VMEM] * 2,
        out_specs=[HBM, VMEM],
        scratch_shapes=[pltpu.VMEM((rows, experts * groups), bf16), DMA],
    )


def unmix_kernel(
    back_ref, wt_ref, gid_ref, w_all_ref, kept_turned_ref, kept_cot_ref, kept_hidden_ref, kept_own_ref,
    kept_away_ref, kept_out_ref, kept_gh_ref, gown_ref, gaway_ref, small_ref,
    turned_ref, cot_ref, hidden_ref, own_ref, away_ref, rest_ref, normed_ref, part_ref, total_ref, gl_ref,
    sems,
):
    experts, _, groups, width = back_ref.shape
    rows = cot_ref.shape[0]
    half = width // 2
    many = min(MIX_ROWS // groups, experts)
    blocks = [slice(at, at + STEP) for at in range(0, rows, STEP)]
    sources = (kept_cot_ref, kept_hidden_ref, kept_turned_ref)
    targets = (cot_ref, hidden_ref, turned_ref)
    arriving = {}

    def load(kinds, at):
        for kind in kinds:
            here = blocks[at]
            arriving[kind, at] = push(sources[kind].at[here], targets[kind].at[here], sems.at[kind, at])

    rest = push(w_all_ref.at[:, 3 * width :], rest_ref, sems.at[6, 0])
    load((0, 1), 0)
    rest.wait()
    out_w = rest_ref[:, :width]
    small = jnp.transpose(rest_ref[:, width:])
    gain = small[experts : experts + 1, :].astype(f32)
    total_ref[...] = jnp.zeros_like(total_ref)

    def slots(place, first=0, count=experts):
        return back_ref[first : first + count, place].reshape(count * groups, width)

    for at, here in enumerate(blocks):
        arriving[0, at].wait()
        arriving[1, at].wait()
        if at + 1 < len(blocks):
            load((0, 1), at + 1)
        else:
            load((2,), 0)
            atts = [push(kept_own_ref, own_ref, sems.at[3, 0]), push(kept_away_ref, away_ref, sems.at[3, 1])]
        hidden = hidden_ref[here, :].astype(f32)
        normed = (hidden * rms_scale(hidden) * gain).astype(bf16)
        normed_ref[here, :] = normed
        mask = lax.broadcasted_iota(jnp.int32, (groups, STEP), 0) == gid_ref[:, here]
        for slot in range(0, experts, many):
            wide = dot(slots(0, slot, many), cot_ref[here, :], NT) + dot(slots(1, slot, many), normed, NT)
            for own in range(slot, slot + many):
                part = wide[(own - slot) * groups : (own - slot + 1) * groups]
                scaled = jnp.where(mask, part * wt_ref[own : own + 1, here], 0.0)
                part_ref[own : own + 1, here] = jnp.sum(scaled, axis=0, keepdims=True)
                total_ref[own] += jnp.sum(scaled, axis=1, keepdims=True)
    gain_total = jnp.zeros((1, width), f32)
    leaving = []
    for at, here in enumerate(blocks):
        mask = lax.broadcasted_iota(jnp.int32, (groups, STEP), 0) == gid_ref[:, here]
        for slot in range(experts):
            own = slice(slot, slot + 1)
            total = jnp.sum(jnp.where(mask, total_ref[slot], 0.0), axis=0, keepdims=True)
            gl_ref[own, here] = (part_ref[own, here] - wt_ref[own, here] * total).astype(bf16)
        hidden = hidden_ref[here, :].astype(f32)
        scale = rms_scale(hidden)
        unit = hidden * scale
        arriving[2, at].wait()
        if at + 1 < len(blocks):
            load((2,), at + 1)
        hidden_ref[here, :] = (hidden + dot(turned_ref[here, :], slots(0))).astype(bf16)
        leaving.append(push(hidden_ref.at[here], kept_out_ref.at[here], sems.at[4, at]))
        grad_normed = dot(turned_ref[here, :], slots(1)) + dot(gl_ref[:, here], small[:experts], TN)
        weighted = gain * grad_normed
        gain_total = gain_total + jnp.sum(grad_normed * unit, axis=0, keepdims=True)
        back = scale * (weighted - unit * jnp.mean(weighted * unit, axis=-1, keepdims=True))
        low = (cot_ref[here, :].astype(f32) + back).astype(bf16)
        cot_ref[here, :] = low
        leaving.append(push(cot_ref.at[here], kept_gh_ref.at[here], sems.at[5, at]))
        grad_att = dot(low, out_w, NT).astype(bf16)
        gown_ref[here, :] = grad_att[:, :half]
        gaway_ref[here, :] = grad_att[:, half:]
    for copy in atts:
        copy.wait()
    small_ref[:half, :width] = dot(own_ref[...], cot_ref[...], TN).astype(bf16)
    small_ref[half:, :width] = dot(away_ref[...], cot_ref[...], TN).astype(bf16)
    tail = [dot(gl_ref[...], normed_ref[...]), gain_total, jnp.zeros((127 - experts, width), f32)]
    small_ref[:, width:] = jnp.transpose(jnp.concatenate(tail, 0)).astype(bf16)
    for copy in leaving:
        copy.wait()


def unmix(back, weights, gid, gathered, turned, cotangent, hidden, att_own, att_away):
    rows, width = cotangent.shape
    experts, _, groups, _ = back.shape
    kept = (turned, cotangent, hidden, att_own, att_away)
    return call(
        unmix_kernel,
        (
            in_hbm((rows, width), bf16),
            in_hbm((rows, width), bf16),
            shape_of((rows, width // 2), bf16),
            shape_of((rows, width // 2), bf16),
            shape_of((width, width + 128), bf16),
        ),
        (pltpu.with_memory_space_constraint(back, pltpu.VMEM), weights, gid, from_hbm(gathered), *[from_hbm(array) for array in kept]),
        room=room_for(UNMIX_ROOM, experts * groups),
        in_specs=[VMEM, VMEM, VMEM] + [HBM] * 6,
        out_specs=[HBM] * 2 + [VMEM] * 3,
        scratch_shapes=[pltpu.VMEM(array.shape, bf16) for array in kept]
        + [
            pltpu.VMEM((width, width + 128), bf16),
            pltpu.VMEM((rows, width), bf16),
            pltpu.VMEM((experts, rows), f32),
            pltpu.VMEM((experts, groups, 1), f32),
            pltpu.VMEM((experts, rows), bf16),
            DMA((7, max(rows // STEP, 4))),
        ],
    )


def expert_kernel(
    pick_ref, in_ref, up_all_ref, down_all_ref, hint_ref,
    sent_ref, kept_act_ref, kept_pre_ref, kept_in_ref, mark_ref,
    up_ref, down_ref, act_ref, pre_ref, out_ref, load_sems, sems,
):
    parts, _, groups, width = in_ref.shape
    many = min(EXPERT_ROWS // groups, parts)
    pick = pick_ref[0]
    load_up = push(up_all_ref.at[pick], up_ref, load_sems.at[0])
    set_mark(mark_ref)
    copies = []
    for at, part in enumerate(range(0, parts, many)):
        here = slice(part * groups, (part + many) * groups)
        owners = slice(part, part + many)
        rows, grad = [in_ref[owners, place].reshape(many * groups, width) for place in range(2)]
        if at == 0:
            load_up.wait()
            load_down = push(down_all_ref.at[pick], down_ref, load_sems.at[1])
        pre = dot(rows, up_ref[...])
        if at == 0:
            load_down.wait()
            copies.append(push(in_ref, kept_in_ref, load_sems.at[2]))
        cdf = 0.5 + 0.5 * lax.erf(pre * 0.7071067811865476)
        slope = cdf + pre * (jnp.exp(-0.5 * pre * pre) * 0.3989422804014327)
        act = (pre * cdf).astype(bf16)
        act_ref[here, :] = act
        copies.append(push(act_ref.at[here], kept_act_ref.at[here], sems.at[0, at]))
        grad_pre = (dot(grad, down_ref[...], NT) * slope).astype(bf16)
        pre_ref[here, :] = grad_pre
        copies.append(push(pre_ref.at[here], kept_pre_ref.at[here], sems.at[1, at]))
        for place, result in enumerate((dot(act, down_ref[...]), dot(grad_pre, up_ref[...], NT))):
            out_ref[owners, place] = result.astype(bf16).reshape(many, groups, width)
            copies.append(push(out_ref.at[owners, place], sent_ref.at[owners, place], sems.at[2 + place, at]))
    for copy in copies:
        copy.wait()


def expert_pass(pick, arrived, w_up, w_down, hint):
    parts, _, groups, width = arrived.shape
    rows = parts * groups
    hidden = w_up.shape[2]
    return call(
        expert_kernel,
        (
            in_hbm(arrived.shape, bf16),
            in_hbm((rows, hidden), bf16),
            in_hbm((rows, hidden), bf16),
            in_hbm(arrived.shape, bf16),
            shape_of(MARK, f32),
        ),
        (pick, pltpu.with_memory_space_constraint(arrived, pltpu.VMEM), from_hbm(w_up), from_hbm(w_down), hint),
        room=room_for(EXPERT_ROOM, rows),
        in_specs=[SMEM, VMEM, HBM, HBM, ANY],
        out_specs=[HBM, HBM, HBM, HBM, VMEM],
        scratch_shapes=[
            pltpu.VMEM(w_up.shape[1:], bf16),
            pltpu.VMEM(w_down.shape[1:], bf16),
            pltpu.VMEM((rows, hidden), bf16),
            pltpu.VMEM((rows, hidden), bf16),
            pltpu.VMEM(arrived.shape, bf16),
            DMA((3,)),
            DMA((4, max(rows // EXPERT_ROWS, 1))),
        ],
    )


def expert_grad_kernel(
    in_ref, kept_act_ref, kept_pre_ref, hint_ref, grad_ref, mark_ref, act_ref, pre_ref, out_ref, load_sems, sems
):
    shards, pieces, per, width = grad_ref.shape
    rows, hidden = act_ref.shape
    slabs = [slice(at, at + width) for at in range(0, hidden, width)]
    loads = [
        [push(kept.at[:, slab], ref.at[:, slab], load_sems.at[place, at]) for at, slab in enumerate(slabs)]
        for place, (kept, ref) in enumerate(((kept_act_ref, act_ref), (kept_pre_ref, pre_ref)))
    ]
    down_pieces = hidden // shards // per
    set_mark(mark_ref)
    mixed, grad = [in_ref[:, place].reshape(rows, width) for place in range(2)]
    for at, slab in enumerate(slabs):
        loads[0][at].wait()
        grad_down = dot(act_ref[:, slab], grad, TN).astype(bf16)
        span = width // (down_pieces * per)
        out_ref[at * span : (at + 1) * span, :down_pieces] = grad_down.reshape(span, down_pieces, per, width)
    copies = [push(out_ref.at[:, :down_pieces], grad_ref.at[:, :down_pieces], sems.at[0])]
    for at, slab in enumerate(slabs):
        loads[1][at].wait()
        grad_up = dot(mixed, pre_ref[:, slab], TN).astype(bf16)
        out_ref[:, down_pieces + at] = grad_up.reshape(shards, per, width)
    copies.append(push(out_ref.at[:, down_pieces:], grad_ref.at[:, down_pieces:], sems.at[1]))
    for copy in copies:
        copy.wait()


def expert_grads(arrived, act, grad_pre, shards, hint):
    width = arrived.shape[3]
    hidden = act.shape[1]
    per = width // shards
    grad = (shards, (hidden // shards) // per + hidden // width, per, width)
    return call(
        expert_grad_kernel,
        (in_hbm(grad, bf16), shape_of(MARK, f32)),
        (arrived, from_hbm(act), from_hbm(grad_pre), hint),
        room=room_for(GRAD_ROOM, act.shape[0]),
        in_specs=[VMEM, HBM, HBM, ANY],
        out_specs=[HBM, VMEM],
        scratch_shapes=[
            pltpu.VMEM(act.shape, bf16),
            pltpu.VMEM(act.shape, bf16),
            pltpu.VMEM(grad, bf16),
            DMA((2, hidden // width)),
            DMA((2,)),
        ],
    )


def shard_sum_kernel(in_ref, *refs):
    down_ref, up_ref, mark_ref = refs[-3:]
    set_mark(mark_ref)
    total = in_ref[0, 0].astype(f32)
    for part in range(1, in_ref.shape[0]):
        total = total + in_ref[part, 0].astype(f32)
    down_rows, width = down_ref.shape[1:]
    down_ref[0] = total[:down_rows]
    per = up_ref.shape[1]
    for at in range(0, up_ref.shape[2] // width):
        here = down_rows + at * per
        up_ref[0, :, at * width : (at + 1) * width] = total[here : here + per]


def shard_sum(parts, per_owner, down_rows, up_rows, experts, before=()):
    shards, tall, width = parts.shape
    parts = parts.reshape(shards // per_owner, per_owner, tall, width)
    hidden = (tall - down_rows) // up_rows * width
    first = experts.start
    return call(
        shard_sum_kernel,
        (
            in_hbm((per_owner, down_rows, width), f32),
            in_hbm((per_owner, up_rows, hidden), f32),
            shape_of(MARK, f32),
        ),
        (parts, *before),
        grid=(len(experts),),
        in_specs=[pl.BlockSpec((parts.shape[0], 1, tall, width), lambda at: (0, first + at, 0, 0))]
        + [ANY] * len(before),
        out_specs=[
            pl.BlockSpec((1, down_rows, width), lambda at: (first + at, 0, 0)),
            pl.BlockSpec((1, up_rows, hidden), lambda at: (first + at, 0, 0)),
            pl.BlockSpec(MARK, lambda at: (0, 0)),
        ],
        input_output_aliases={1 + at: at for at in range(len(before))},
    )


def own_grad_kernel(unit_t_ref, grad_ref, w_ref, grad_w_ref, part_ref):
    wide = grad_ref.shape[1]
    grad_w_ref[...] = dot(unit_t_ref[...], grad_ref[...])
    for at in range(0, part_ref.shape[0], 1024):
        here = slice(at, at + 1024)
        part_ref[here, :] = dot(grad_ref[here, :], w_ref[:, :wide], NT)


def own_grad(unit_t, grad, weights):
    width, rows = unit_t.shape
    return call(
        own_grad_kernel,
        (shape_of((width, grad.shape[1]), f32), shape_of((rows, width), f32)),
        (unit_t, grad, weights),
        room=16,
        in_specs=[VMEM] * 3,
        out_specs=[VMEM] * 2,
    )


def away_grad_kernel(mine_ref, unit_t_ref, grad_ref, own_ref, small_ref, keep_ref, send_ref, total_ref):
    total_ref[...] = dot(unit_t_ref[...], grad_ref[...])
    many, per, _ = keep_ref.shape
    mine = mine_ref[0]
    left = own_ref.shape[1]
    right = left + total_ref.shape[1]
    for place in range(many):
        for part, ref in ((mine, keep_ref), (1 - mine, send_ref)):
            rows = pl.ds(pl.multiple_of((2 * place + part) * per, per), per)
            ref[place, :, :left] = own_ref[rows, :].astype(ref.dtype)
            ref[place, :, left:right] = total_ref[rows, :].astype(ref.dtype)
            ref[place, :, right:] = small_ref[rows, :].astype(ref.dtype)


def halves(array, mine):
    keep, send = [lax.dynamic_index_in_dim(array, part[0], 1, keepdims=False) for part in (mine, 1 - mine)]
    return keep, send.astype(bf16)


def away_grad(mine, unit_t, grad, own, small, devices):
    width, rows = unit_t.shape
    wide = grad.shape[1]
    per = width // devices
    if per % 16:
        total = jnp.concatenate([own, dot(unit_t, grad), small.astype(f32)], 1)
        return halves(total.reshape(devices // 2, 2, per, -1), mine)
    dims = (devices // 2, per, own.shape[1] + wide + small.shape[1])
    return call(
        away_grad_kernel,
        (shape_of(dims, f32), shape_of(dims, bf16)),
        (mine, unit_t, grad, own, small),
        room=16,
        in_specs=[SMEM] + [VMEM] * 4,
        out_specs=[VMEM] * 2,
        scratch_shapes=[pltpu.VMEM((width, wide), f32)],
    )


def token_grad_kernel(part_ref, grad_ref, w_ref, tok_ref, gh_ref, out_ref, mark_ref):
    set_mark(mark_ref)
    wide = grad_ref.shape[1]
    for at in range(0, tok_ref.shape[0], 512):
        here = slice(at, at + 512)
        weighted = part_ref[here, :] + dot(grad_ref[here, :], w_ref[:, wide : 2 * wide], NT)
        source = tok_ref[here, :].astype(f32)
        scale = rms_scale(source)
        unit = source * scale
        back = scale * (weighted - unit * jnp.mean(weighted * unit, axis=-1, keepdims=True))
        out_ref[here, :] = (gh_ref[here, :].astype(f32) + back).astype(bf16)


def token_grad(part, grad, weights, tokens, grad_hidden):
    return call(
        token_grad_kernel,
        (shape_of(tokens.shape, bf16), shape_of(MARK, f32)),
        (part, grad, weights, tokens, grad_hidden),
        room=16,
        in_specs=[VMEM] * 5,
        out_specs=[VMEM] * 2,
    )


def swap(array, axis, size, bit):
    return lax.ppermute(array, axis, [(at, at ^ bit) for at in range(size)])


def axis_bits(sizes):
    bits = []
    for axis, size in sizes:
        bit = size // 2
        while bit:
            bits.append((axis, size, bit))
            bit //= 2
    return bits


def gather_rows(shard, sizes, meanwhile):
    bits = axis_bits(sizes)
    held = shard[(None,) * len(bits)]
    for place, (axis, size, bit) in enumerate(bits):
        other = swap(held, axis, size, bit)
        if place == len(bits) - 2:
            other, meanwhile = lax.optimization_barrier((other, meanwhile))
        upper = (lax.axis_index(axis) // bit) % 2 == 1
        first = jnp.where(upper, other, held)
        second = jnp.where(upper, held, other)
        held = jnp.concatenate([first, second], axis=place)
    return held.reshape((shard.shape[0] * 2 ** len(bits),) + shard.shape[1:]), meanwhile


def add_split_kernel(mine_ref, keep_ref, got_ref, hint_ref, next_keep_ref, send_ref):
    mine = mine_ref[0]
    for part, ref in ((mine, next_keep_ref), (1 - mine, send_ref)):
        value = keep_ref[:, pl.ds(part, 1)] + got_ref[:, pl.ds(part, 1)].astype(f32)
        ref[...] = value[:, 0].astype(ref.dtype)


def add_split(mine, keep, got, hint):
    many, per, wide = keep.shape
    dims = (many // 2, per, wide)
    keep, got = [array.reshape(many // 2, 2, per, wide) for array in (keep, got)]
    if per % 16:
        return halves(keep + got.astype(f32), mine)
    return call(
        add_split_kernel,
        (shape_of(dims, f32), shape_of(dims, bf16)),
        (mine, keep, got, hint),
        room=16,
        in_specs=[SMEM, VMEM, VMEM, ANY],
        out_specs=[VMEM] * 2,
    )


def scatter_rows(keep, send, sizes, hints):
    bits = axis_bits(sizes)[::-1]
    for place, (axis, size, bit) in enumerate(bits):
        got = swap(send, axis, size, bit)
        if place + 1 == len(bits):
            return keep, got
        axis, size, bit = bits[place + 1]
        mine = ((lax.axis_index(axis) // bit) % 2).astype(jnp.int32).reshape(1)
        keep, send = add_split(mine, keep, got, hints.get(place, got))


def on_device(
    n_dp, n_owner, tokens, seq_lengths, group_map, gain_attn, gain_mix, w_qkv, w_out, w_ctrl, w_up, w_down, cotangent
):
    rows, width = tokens.shape
    experts = w_ctrl.shape[1]
    per_owner = w_up.shape[0]
    groups = rows // G
    parts = n_dp // per_owner
    sizes = (("dp", n_dp), ("expert", n_owner))
    dp = lax.axis_index("dp")
    pick = (dp % per_owner).astype(jnp.int32).reshape(1)

    gain_row = gain_attn.reshape(1, -1)
    shard = call(
        functools.partial(pack_kernel, n_owner),
        shape_of((w_ctrl.shape[0], 4 * width + 128), bf16),
        (seq_lengths, *[from_hbm(array) for array in (w_qkv, gain_row, w_out, w_ctrl, gain_mix.reshape(1, -1))]),
        room=8,
        in_specs=[SMEM] + [VMEM] * 5,
        out_specs=VMEM,
    )

    def neighbour(array):
        return swap(array, "expert", n_owner, 1)

    unit_one, unit_away, unit_t, gid = call(
        prep_kernel,
        (
            in_hbm((rows, width), bf16),
            in_hbm((rows, width), bf16),
            in_hbm((width, rows), bf16),
            shape_of((1, rows), jnp.int32),
        ),
        (tokens, neighbour(tokens), group_map.reshape(groups, G)),
        room=16,
        in_specs=[VMEM] * 3,
        out_specs=[HBM, HBM, HBM, VMEM],
        scratch_shapes=[pltpu.VMEM((rows, width), bf16)] * 2 + [pltpu.VMEM((width, rows), bf16), DMA((3, rows // 512))],
    )
    gathered, (unit_one, unit_away) = gather_rows(shard, sizes, (unit_one, unit_away))
    triple = 3 * width

    near = (dp * n_owner + (lax.axis_index("expert") ^ 1)) * w_ctrl.shape[0]
    lengths, att_own, att_away, lse_own, lse_away, own_qkv, away_qkv, kept_away = attend_forward(
        seq_lengths, near.astype(jnp.int32).reshape(1), unit_one, unit_away, gathered
    )
    hidden, weights, mixed, kept_own, kept_back = mix(
        tokens, att_own, neighbour(att_away), gathered, gid, cotangent, experts
    )

    teams = [
        [(part * per_owner + low) * n_owner + owner for low in range(per_owner) for owner in range(n_owner)]
        for part in range(parts)
    ]

    def exchange(array):
        return lax.all_to_all(
            array, ("dp", "expert"), split_axis=0, concat_axis=0, axis_index_groups=teams, tiled=True
        )

    arrived = exchange(mixed)
    turned, mark = turn(weights, gid, groups)
    results, act, grad_pre, arrived, mark = expert_pass(pick, arrived, w_up, w_down, mark)
    back = exchange(results)
    grad_experts, mark = expert_grads(arrived, act, grad_pre, n_dp, mark)
    shards = lax.all_to_all(
        grad_experts.reshape(n_dp, -1, width), "dp", split_axis=0, concat_axis=0, tiled=True
    )
    output, grad_hidden, grad_own, grad_away, grad_small = unmix(
        back, weights, gid, gathered, turned, cotangent, hidden, kept_own, kept_back
    )

    grad_here = neighbour(grad_away)
    grad_one = attend_backward(0, lengths, own_qkv, grad_own, kept_own, lse_own, grad_own)
    grad_two = neighbour(attend_backward(1, lengths, away_qkv, grad_here, kept_away, lse_away, grad_one))
    grad_w_own, token_part = own_grad(unit_t, grad_one, gathered)
    axis, size, bit = axis_bits(sizes)[-1]
    mine = ((lax.axis_index(axis) // bit) % 2).astype(jnp.int32).reshape(1)
    keep, send = away_grad(mine, unit_t, grad_two, grad_w_own, grad_small, n_dp * n_owner)
    grad_tokens, token_mark = token_grad(token_part, grad_two, gathered, tokens, grad_hidden)
    shapes = (per_owner, w_down.shape[1] // n_dp, width // n_dp)
    *some, shard_mark = shard_sum(shards, *shapes, range(per_owner // 2))
    grad_down_shard, grad_up_shard, _ = shard_sum(shards, *shapes, range(per_owner // 2, per_owner), some)
    keep, got = scatter_rows(keep, send, sizes, {1: token_mark, len(axis_bits(sizes)) - 2: shard_mark})
    own_rows = w_qkv.shape[0]
    shard_qkv, shard_out, shard_ctrl, shard_gain_one, shard_gain_two = call(
        functools.partial(finish_kernel, n_owner),
        (
            shape_of(w_qkv.shape, f32),
            shape_of(w_out.shape, f32),
            shape_of(w_ctrl.shape, f32),
            shape_of((1, own_rows), f32),
            shape_of((1, own_rows), f32),
        ),
        (keep, got, gain_row, w_qkv),
        room=8,
        in_specs=[VMEM] * 4,
        out_specs=[VMEM] * 5,
    )
    return (
        output,
        grad_tokens,
        shard_gain_one.reshape(-1),
        shard_gain_two.reshape(-1),
        shard_qkv,
        shard_out,
        shard_ctrl,
        grad_up_shard,
        grad_down_shard,
    )


def solution(mesh):
    both = ("dp", "expert")
    rows = P(both, None)
    return jax.shard_map(
        functools.partial(on_device, mesh.shape["dp"], mesh.shape["expert"]),
        mesh=mesh,
        in_specs=(
            rows, P(both), rows, P(both), P(both), rows, rows, rows,
            P("expert", None, None), P("expert", None, None), rows,
        ),
        out_specs=(
            rows, rows, P(both), P(both), rows, rows, rows,
            P("expert", "dp", None), P("expert", "dp", None),
        ),
        check_vma=False,
    )
```

```python
import functools

import jax
import jax.numpy as jnp
from jax import lax
from jax.experimental import pallas as pl
from jax.experimental.pallas import tpu as pltpu
from jax.sharding import PartitionSpec as P

HEADS = 8
G = 32
BQ = 256

ANY = pl.BlockSpec(memory_space=pl.ANY)
VMEM = pl.BlockSpec(memory_space=pltpu.VMEM)
HBM = pl.BlockSpec(memory_space=pltpu.HBM)
DMA = pltpu.SemaphoreType.DMA
SMEM = pl.BlockSpec(memory_space=pltpu.SMEM)

eps_norm = 1e-05
masked_value = -1e30
bf16 = jnp.bfloat16
f32 = jnp.float32
NN = (((1,), (0,)), ((), ()))
NT = (((1,), (1,)), ((), ()))
TN = (((0,), (0,)), ((), ()))


def dot(left, right, dims=NN):
    return lax.dot_general(left, right, dims, preferred_element_type=f32)


def rms_scale(values):
    return lax.rsqrt(jnp.mean(values * values, axis=-1, keepdims=True) + eps_norm)


def call(body, out_shape, args, room=28, **extra):
    return pl.pallas_call(
        body,
        out_shape=out_shape,
        compiler_params=pltpu.CompilerParams(vmem_limit_bytes=room * 2**20),
        name=getattr(body, "func", body).__name__,
        **extra,
    )(*args)


def shape_of(dims, kind):
    return jax.ShapeDtypeStruct(dims, kind)


def in_hbm(dims, kind):
    return pltpu.HBM(dims, kind)


def in_vmem(dims, kind):
    return pltpu.VMEM(dims, kind)


def from_hbm(array):
    return pltpu.with_memory_space_constraint(array, pltpu.HBM)


def room_for(parts, rows):
    fixed, per_block = parts
    return fixed + per_block * rows // 1024


def push(source, target, sem):
    copy = pltpu.make_async_copy(source, target, sem)
    copy.start()
    return copy


MARK = (8, 128)


def set_mark(ref):
    ref[...] = jnp.zeros(MARK, f32)


def diagonal(size):
    return lax.broadcasted_iota(jnp.int32, (size, size), 0) == lax.broadcasted_iota(jnp.int32, (size, size), 1)


def column_of(row):
    return jnp.sum(jnp.where(diagonal(row.shape[1]), row, 0.0), axis=1, keepdims=True)


def row_of(column):
    return jnp.sum(jnp.where(diagonal(column.shape[0]), column, 0.0), axis=0, keepdims=True)


def slot_matrix(experts, wide, n_owner, kind):
    expert = lax.broadcasted_iota(jnp.int32, (experts, wide), 0)
    slot = lax.broadcasted_iota(jnp.int32, (experts, wide), 1)
    per_owner = experts // n_owner
    return jnp.where(expert % per_owner * n_owner + expert // per_owner == slot, 1.0, 0.0).astype(kind)


def pack_kernel(n_owner, len_ref, wqkv_ref, gain_ref, wout_ref, ctrl_ref, mix_ref, out_ref):
    width = wout_ref.shape[1]
    experts = ctrl_ref.shape[1]
    gain = column_of(gain_ref[...].astype(f32))
    for pair in range(width // 128):
        for part in range(3):
            at = part * width + pair * 128
            to = pair * 384 + part * 128
            out_ref[:, to : to + 128] = (wqkv_ref[:, at : at + 128].astype(f32) * gain).astype(bf16)
    out_ref[:, 3 * width : 4 * width] = wout_ref[...]
    small = dot(ctrl_ref[...], slot_matrix(experts, 128, n_owner, bf16))
    lane = lax.broadcasted_iota(jnp.int32, small.shape, 1)
    small = jnp.where(lane == experts, column_of(mix_ref[...].astype(f32)), small)
    small = jnp.where(lane == 127, len_ref[0].astype(f32), small)
    out_ref[:, 4 * width :] = small.astype(bf16)


def finish_kernel(n_owner, keep_ref, got_ref, gain_ref, wqkv_ref, qkv_ref, out_ref, ctrl_ref, one_ref, mix_ref):
    width = out_ref.shape[1]
    experts = ctrl_ref.shape[1]
    total = keep_ref[0] + got_ref[0].astype(f32)
    gain = column_of(gain_ref[...].astype(f32))
    grad_gain = jnp.zeros((total.shape[0], 128), f32)
    for pair in range(width // 128):
        for part in range(3):
            to = part * width + pair * 128
            at = pair * 384 + part * 128
            grad = total[:, at : at + 128]
            qkv_ref[:, to : to + 128] = gain * grad
            grad_gain = grad_gain + wqkv_ref[:, to : to + 128].astype(f32) * grad
    out_ref[...] = total[:, 3 * width : 4 * width]
    small = total[:, 4 * width :]
    slots = slot_matrix(experts, 128, n_owner, f32)
    ctrl_ref[...] = lax.dot_general(small, slots, NT, precision=lax.Precision.HIGHEST, preferred_element_type=f32)
    one_ref[...] = row_of(jnp.sum(grad_gain, axis=1, keepdims=True))
    lane = lax.broadcasted_iota(jnp.int32, small.shape, 1)
    mix_ref[...] = row_of(jnp.sum(jnp.where(lane == experts, small, 0.0), axis=1, keepdims=True))


def prep_kernel(
    tok_ref, tok_away_ref, gmap_ref, kept_ref, kept_away_ref, kept_t_ref, gid_ref, unit_ref, away_ref, unit_t_ref, sems
):
    rows = tok_ref.shape[0]
    step = 512
    copies = []
    sides = ((tok_ref, unit_ref, kept_ref), (tok_away_ref, away_ref, kept_away_ref))
    for side, (source, target, kept) in enumerate(sides):
        for at in range(0, rows, step):
            here = slice(at, at + step)
            block = source[here, :].astype(f32)
            unit = (block * rms_scale(block)).astype(bf16)
            target[here, :] = unit
            copies.append(push(target.at[here], kept.at[here], sems.at[side, at // step]))
            if side == 0:
                unit_t_ref[:, here] = jnp.transpose(unit)
        if side == 0:
            copies.append(push(unit_t_ref, kept_t_ref, sems.at[2, 0]))
    groups = rows // G
    places = lax.broadcasted_iota(jnp.int32, (groups, rows), 1)
    group_at = lax.broadcasted_iota(jnp.int32, (groups, rows), 0)
    gmap = gmap_ref[...]
    member = jnp.zeros((groups, rows), jnp.int32)
    for slot in range(G):
        member = jnp.where(gmap[:, slot : slot + 1] == places, group_at, member)
    gid_ref[...] = jnp.sum(member.astype(f32), axis=0, keepdims=True).astype(jnp.int32)
    for copy in copies:
        copy.wait()


def lower_mask():
    return lax.broadcasted_iota(jnp.int32, (BQ, BQ), 0) <= lax.broadcasted_iota(jnp.int32, (BQ, BQ), 1)


def head_lanes():
    return lax.broadcasted_iota(jnp.int32, (1, 128), 1) // 64


def attend_pair(length, pair, qkv_all_ref, out_ref, lse_all_ref, vt_ref):
    qkv_ref = qkv_all_ref.at[:, pl.ds(pl.multiple_of(pair * 384, 384), 384)]
    lse_ref = lse_all_ref.at[pl.ds(pair, 1)]
    rows = qkv_ref.shape[0]
    step, ahead = 512, 6
    lane = head_lanes()
    vt_ref[...] = jnp.transpose(qkv_ref[:, 256:384])

    def run(low_of):
        items = []
        for at in range(0, rows, BQ):
            chunks = [(at, BQ)]
            top = at
            while top > low_of(at):
                down = max(low_of(at), top - step)
                chunks.append((down, top - down))
                top = down
            for place, (low, wide) in enumerate(chunks):
                for head in range(2):
                    items.append((at, head, low, wide, place == 0, place == len(chunks) - 1))

        def score(at, head, low, wide, first, last):
            own = jnp.where(lane == head, qkv_ref[at : at + BQ, 0:128] * bf16(0.125), bf16(0))
            scores = dot(qkv_ref[low : low + wide, 128:256], own, NT)
            return jnp.where(lower_mask(), scores, masked_value) if first else scores

        pending = [score(*item) for item in items[:ahead]]
        state = {}
        for place, (at, head, low, wide, first, last) in enumerate(items):
            if place + ahead < len(items):
                pending.append(score(*items[place + ahead]))
            scores = pending.pop(0)
            peak = jnp.max(scores, axis=0, keepdims=True)
            if not first:
                old_peak, old_total, old_mixed = state[head]
                peak = jnp.maximum(old_peak, peak)
                shrink = jnp.exp(old_peak - peak)
            probs = jnp.exp(scores - peak)
            total = jnp.sum(probs, axis=0, keepdims=True)
            mixed = dot(vt_ref[64 * head : 64 * head + 64, low : low + wide], probs.astype(bf16))
            if not first:
                total = total + old_total * shrink
                mixed = mixed + old_mixed * shrink
            state[head] = (peak, total, mixed)
            if last:
                lse_ref[0, head : head + 1, at : at + BQ] = peak + jnp.log(total)
                if head == 1:
                    both = [state[own][2] * (1.0 / state[own][1]) for own in range(2)]
                    out_ref[at : at + BQ, :] = jnp.transpose(jnp.concatenate(both, 0)).astype(bf16)

    @pl.when(length == BQ)
    def _():
        run(lambda at: at)

    @pl.when(length != BQ)
    def _():
        run(lambda at: 0)


def attend_kernel(
    len_ref, place_ref, kept_own_ref, kept_away_ref, w_ref,
    lens_ref, own_ref, away_ref, lse_own_ref, lse_away_ref, kept_qkv_own_ref, kept_qkv_away_ref, kept_out_ref,
    unit_ref, qkv_ref, out_ref, lse_ref, vt_ref, unit_sems, sems,
):
    row = pl.multiple_of(place_ref[0] // 16 * 16, 16)
    tile = w_ref[pl.ds(row, 16), w_ref.shape[1] - 128 :].astype(f32)
    chosen = lax.broadcasted_iota(jnp.int32, tile.shape, 1) == 127
    chosen = chosen & (lax.broadcasted_iota(jnp.int32, tile.shape, 0) == place_ref[0] % 16)
    lens_ref[0] = len_ref[0]
    lens_ref[1] = jnp.max(jnp.where(chosen, tile, 0.0)).astype(jnp.int32)
    rows, wide = qkv_ref.shape
    half = wide // 2
    pairs = wide // 384
    count = unit_sems.shape[0] // 2
    blocks = [slice(at, at + rows // count) for at in range(0, rows, rows // count)]
    kept = (kept_qkv_own_ref, kept_qkv_away_ref)
    copies, keeping = [], []

    def load(at):
        if at < 2 * count:
            source = (kept_own_ref, kept_away_ref)[at // count]
            copies.append(push(source.at[blocks[at % count]], unit_ref.at[at % 3], unit_sems.at[at]))

    load(0)
    load(1)
    for at in range(2 * count):
        side = at // count
        copies[at].wait()
        load(at + 2)
        columns = slice(side * half, (side + 1) * half)
        qkv_ref[blocks[at % count], columns] = dot(unit_ref[at % 3], w_ref[:, columns]).astype(bf16)
        if at % count == count - 1:
            keeping.append(push(qkv_ref.at[:, columns], kept[side], sems.at[side]))

    def keep_out(pair):
        thin = pl.ds(pl.multiple_of((pair - pairs // 2) * 128, 128), 128)
        return pltpu.make_async_copy(away_ref.at[:, thin], kept_out_ref.at[:, thin], sems.at[2 + pair])

    @pl.loop(0, pairs)
    def _(pair):
        mine = pair < pairs // 2
        attend_pair(lens_ref[jnp.where(mine, 0, 1)], pair, qkv_ref, out_ref, lse_ref, vt_ref)

        @pl.when(mine)
        def _():
            own_ref[:, pl.ds(pl.multiple_of(pair * 128, 128), 128)] = out_ref[...]

        @pl.when(jnp.logical_not(mine))
        def _():
            away_ref[:, pl.ds(pl.multiple_of((pair - pairs // 2) * 128, 128), 128)] = out_ref[...]
            keep_out(pair).start()

    lse_own_ref[...] = lse_ref[: pairs // 2]
    lse_away_ref[...] = lse_ref[pairs // 2 :]
    for copy in keeping:
        copy.wait()
    for pair in range(pairs // 2, pairs):
        keep_out(pair).wait()


def attend_forward(length, place, unit, unit_away, gathered):
    rows, width = unit.shape
    pairs = width // 128
    count = 4
    half = pairs // 2
    lse = shape_of((half, 2, rows), f32)
    return call(
        attend_kernel,
        (
            shape_of((2,), jnp.int32),
            shape_of((rows, 128 * half), bf16),
            shape_of((rows, 128 * half), bf16),
            lse,
            lse,
            in_hbm((rows, 384 * half), bf16),
            in_hbm((rows, 384 * half), bf16),
            in_hbm((rows, 128 * half), bf16),
        ),
        (length, place, from_hbm(unit), from_hbm(unit_away), gathered),
        room=ATTEND_ROOM,
        in_specs=[SMEM, SMEM, HBM, HBM, VMEM],
        out_specs=[SMEM] + [VMEM] * 4 + [HBM] * 3,
        scratch_shapes=[
            pltpu.VMEM((3, rows // count, width), bf16),
            pltpu.VMEM((rows, 384 * pairs), bf16),
            pltpu.VMEM((rows, 128), bf16),
            pltpu.VMEM((pairs, 2, rows), f32),
            pltpu.VMEM((128, rows), bf16),
            DMA((2 * count,)),
            DMA((2 + pairs,)),
        ],
    )


def attend_back_kernel(side, lens_ref, qkv_ref, go_ref, o_ref, lse_ref, hint_ref, grad_ref, *scratch):
    @pl.loop(0, qkv_ref.shape[1] // 384)
    def _(pair):
        wide = pl.ds(pl.multiple_of(pair * 384, 384), 384)
        thin = pl.ds(pl.multiple_of(pair * 128, 128), 128)
        refs = [qkv_ref.at[:, wide], go_ref.at[:, thin], o_ref.at[:, thin], lse_ref.at[pl.ds(pair, 1)]]
        attend_back_pair(lens_ref[side], *refs, grad_ref.at[:, wide], *scratch)


def attend_back_pair(length, qkv_ref, go_ref, o_ref, lse_ref, grad_ref, gqt_ref, kt_ref, dl_ref):
    rows = qkv_ref.shape[0]
    step, ahead = 256, 2
    lane = head_lanes()
    kt_ref[...] = jnp.transpose(qkv_ref[:, 128:256]) * bf16(0.125)
    product = (go_ref[...].astype(f32) * o_ref[...].astype(f32)).astype(bf16)
    of_head = lax.broadcasted_iota(jnp.int32, (8, 128), 0) == lax.broadcasted_iota(jnp.int32, (8, 128), 1) // 64
    dl_ref[...] = dot(jnp.where(of_head, 1.0, 0.0).astype(bf16), product, NT)

    def run(end_of):
        items = []
        for low in range(0, rows, BQ):
            end = end_of(low)
            chunks = [(low, BQ)] + [(at, min(step, end - at)) for at in range(low + BQ, end, step)]
            for place, (at, wide) in enumerate(chunks):
                for head in range(2):
                    items.append((low, head, at, wide, place == 0, place == len(chunks) - 1))
        blocks = {}
        written = set()

        def products(low, head, at, wide, first, last):
            if (low, head) not in blocks:
                keys = qkv_ref[low : low + BQ, 128:256] * bf16(0.125)
                vals = qkv_ref[low : low + BQ, 256:384]
                blocks[low, head] = [jnp.where(lane == head, own, bf16(0)) for own in (keys, vals)]
            keys, vals = blocks[low, head]
            return (
                dot(keys, qkv_ref[at : at + wide, 0:128], NT),
                dot(vals, go_ref[at : at + wide, :], NT),
            )

        pending = [products(*item) for item in items[:ahead]]
        grad_k, grad_v = {}, {}
        for place, (low, head, at, wide, first, last) in enumerate(items):
            if place + ahead < len(items):
                pending.append(products(*items[place + ahead]))
            scores, grad_probs = pending.pop(0)
            here = slice(at, at + wide)
            probs = jnp.exp(scores - lse_ref[0, head : head + 1, here])
            if first:
                probs = jnp.where(lower_mask(), probs, 0.0)
            grad_scores = (probs * (grad_probs - dl_ref[head : head + 1, here])).astype(bf16)
            more_v = dot(probs.astype(bf16), go_ref[here, :])
            more_k = dot(grad_scores, qkv_ref[here, 0:128])
            grad_v[head] = more_v if first else grad_v[head] + more_v
            grad_k[head] = more_k if first else grad_k[head] + more_k
            span = slice(64 * head, 64 * head + 64)
            more_q = dot(kt_ref[span, low : low + BQ], grad_scores)
            fresh = (head, at + wide) not in written
            written.update((head, top) for top in range(at + BQ, at + wide + BQ, BQ))
            if fresh:
                gqt_ref[span, here] = more_q
            else:
                gqt_ref[span, here] += more_q
            if last and head == 1:
                there = slice(low, low + BQ)
                grad_ref[there, 128:256] = (jnp.where(lane == 0, grad_k[0], grad_k[1]) * 0.125).astype(bf16)
                grad_ref[there, 256:384] = jnp.where(lane == 0, grad_v[0], grad_v[1]).astype(bf16)

    @pl.when(length == BQ)
    def _():
        run(lambda low: low + BQ)

    @pl.when(length != BQ)
    def _():
        run(lambda low: rows)

    grad_ref[:, 0:128] = jnp.transpose(gqt_ref[...]).astype(bf16)


def attend_backward(side, lengths, qkv, grad_attended, attended, log_totals, hint):
    rows = qkv.shape[0]
    return call(
        functools.partial(attend_back_kernel, side),
        shape_of(qkv.shape, bf16),
        (lengths, qkv, grad_attended, attended, log_totals, hint),
        room=ATTEND_ROOM,
        in_specs=[SMEM, VMEM, VMEM, VMEM, VMEM, ANY],
        out_specs=VMEM,
        scratch_shapes=[pltpu.VMEM((128, rows), f32), pltpu.VMEM((128, rows), bf16), pltpu.VMEM((8, rows), f32)],
    )


STEP = 512
UNMIX_ROOM = (24, 12)
MIX_ROOM = (12, 12)
ATTEND_ROOM = 24
EXPERT_ROOM = (20, 16)
GRAD_ROOM = (16, 20)
EXPERT_ROWS = 512
MIX_ROWS = 1024


def member_mask(gid_ref, groups):
    wide = gid_ref.shape[1]
    return lax.broadcasted_iota(jnp.int32, (groups, wide), 0) == gid_ref[...]


def mix_kernel(
    tok_ref, own_ref, away_ref, w_all_ref, gid_ref, cot_ref,
    kept_hidden_ref, wt_ref, sent_ref, kept_own_ref, kept_away_ref, normed_ref, w_ref, hidden_ref, mixed_ref, sems, send_sems,
):
    copies = [push(away_ref, kept_away_ref, sems.at[0]), push(own_ref, kept_own_ref, sems.at[2])]
    rows, width = tok_ref.shape
    experts, _, groups, _ = mixed_ref.shape
    half = width // 2
    out_w = w_all_ref[:, 3 * width : 4 * width]
    small = jnp.transpose(w_all_ref[:, 4 * width :])
    gain = small[experts : experts + 1, :].astype(f32)
    for at in range(0, rows, 512):
        here = slice(at, at + 512)
        hidden = tok_ref[here, :].astype(f32) + dot(own_ref[here, :], out_w[:half])
        hidden = (hidden + dot(away_ref[here, :], out_w[half:])).astype(bf16)
        hidden_ref[here, :] = hidden
        hidden = hidden.astype(f32)
        normed_ref[here, :] = (hidden * rms_scale(hidden) * gain).astype(bf16)
    copies.append(push(hidden_ref, kept_hidden_ref, sems.at[1]))
    logits = dot(small[:experts], normed_ref[...], NT)
    mask = member_mask(gid_ref, groups)
    for slot in range(experts):
        wide = jnp.where(mask, logits[slot : slot + 1, :], masked_value)
        wide = jnp.exp(wide - jnp.max(wide, axis=1, keepdims=True))
        wide = wide * (1.0 / jnp.sum(wide, axis=1, keepdims=True))
        wt_ref[slot : slot + 1, :] = jnp.sum(wide, axis=0, keepdims=True)
        w_ref[slot * groups : (slot + 1) * groups, :] = wide.astype(bf16)
    many = min(512 // groups, experts)
    for place, ref in enumerate((normed_ref, cot_ref)):
        for slot in range(0, experts, many):
            mixed = dot(w_ref[slot * groups : (slot + many) * groups, :], ref[...]).astype(bf16)
            own = slice(slot, slot + many)
            mixed_ref[own, place] = mixed.reshape(many, groups, width)
            copies.append(push(mixed_ref.at[own, place], sent_ref.at[own, place], send_sems.at[place, slot // many]))
    for copy in copies:
        copy.wait()


def mix(tokens, att_own, att_away, gathered, gid, cotangent, experts):
    rows, width = tokens.shape
    groups = rows // G
    sent = (experts, 2, groups, width)
    return call(
        mix_kernel,
        (
            in_hbm((rows, width), bf16),
            shape_of((experts, rows), f32),
            in_hbm(sent, bf16),
            in_hbm(att_own.shape, bf16),
            in_hbm(att_away.shape, bf16),
        ),
        (tokens, att_own, att_away, gathered, gid, cotangent),
        room=room_for(MIX_ROOM, experts * groups),
        in_specs=[VMEM] * 6,
        out_specs=[HBM, VMEM, HBM, HBM, HBM],
        scratch_shapes=[
            pltpu.VMEM((rows, width), bf16),
            pltpu.VMEM((experts * groups, rows), bf16),
            pltpu.VMEM((rows, width), bf16),
            pltpu.VMEM(sent, bf16),
            DMA((3,)),
            DMA((2, max(experts * groups // 512, 1))),
        ],
    )


def turn_kernel(wt_ref, gid_ref, kept_ref, mark_ref, turned_ref, sem):
    set_mark(mark_ref)
    experts, rows = wt_ref.shape
    groups = turned_ref.shape[1] // experts
    many = 256 // groups
    for at in range(0, rows, STEP):
        here = slice(at, at + STEP)
        mask = lax.broadcasted_iota(jnp.int32, (groups, STEP), 0) == gid_ref[:, here]
        for slot in range(0, experts, many):
            parts = [
                jnp.where(mask, wt_ref[own : own + 1, here], 0.0).astype(bf16) for own in range(slot, slot + many)
            ]
            turned_ref[here, slot * groups : (slot + many) * groups] = jnp.transpose(jnp.concatenate(parts, 0))
    push(turned_ref, kept_ref, sem).wait()


def turn(weights, gid, groups):
    experts, rows = weights.shape
    return call(
        turn_kernel,
        (in_hbm((rows, experts * groups), bf16), shape_of(MARK, f32)),
        (weights, gid),
        room=16,
        in_specs=[VMEM] * 2,
        out_specs=[HBM, VMEM],
        scratch_shapes=[pltpu.VMEM((rows, experts * groups), bf16), DMA],
    )


def unmix_kernel(
    back_ref, wt_ref, gid_ref, w_all_ref, kept_turned_ref, kept_cot_ref, kept_hidden_ref, kept_own_ref,
    kept_away_ref, kept_out_ref, kept_gh_ref, gown_ref, gaway_ref, small_ref,
    turned_ref, cot_ref, hidden_ref, own_ref, away_ref, rest_ref, normed_ref, part_ref, total_ref, gl_ref,
    sems,
):
    experts, _, groups, width = back_ref.shape
    rows = cot_ref.shape[0]
    half = width // 2
    many = min(MIX_ROWS // groups, experts)
    blocks = [slice(at, at + STEP) for at in range(0, rows, STEP)]
    sources = (kept_cot_ref, kept_hidden_ref, kept_turned_ref)
    targets = (cot_ref, hidden_ref, turned_ref)
    arriving = {}

    def load(kinds, at):
        for kind in kinds:
            here = blocks[at]
            arriving[kind, at] = push(sources[kind].at[here], targets[kind].at[here], sems.at[kind, at])

    rest = push(w_all_ref.at[:, 3 * width :], rest_ref, sems.at[6, 0])
    load((0, 1), 0)
    rest.wait()
    out_w = rest_ref[:, :width]
    small = jnp.transpose(rest_ref[:, width:])
    gain = small[experts : experts + 1, :].astype(f32)
    total_ref[...] = jnp.zeros_like(total_ref)

    def slots(place, first=0, count=experts):
        return back_ref[first : first + count, place].reshape(count * groups, width)

    for at, here in enumerate(blocks):
        arriving[0, at].wait()
        arriving[1, at].wait()
        if at + 1 < len(blocks):
            load((0, 1), at + 1)
        else:
            load((2,), 0)
            atts = [push(kept_own_ref, own_ref, sems.at[3, 0]), push(kept_away_ref, away_ref, sems.at[3, 1])]
        hidden = hidden_ref[here, :].astype(f32)
        normed = (hidden * rms_scale(hidden) * gain).astype(bf16)
        normed_ref[here, :] = normed
        mask = lax.broadcasted_iota(jnp.int32, (groups, STEP), 0) == gid_ref[:, here]
        for slot in range(0, experts, many):
            wide = dot(slots(0, slot, many), cot_ref[here, :], NT) + dot(slots(1, slot, many), normed, NT)
            for own in range(slot, slot + many):
                part = wide[(own - slot) * groups : (own - slot + 1) * groups]
                scaled = jnp.where(mask, part * wt_ref[own : own + 1, here], 0.0)
                part_ref[own : own + 1, here] = jnp.sum(scaled, axis=0, keepdims=True)
                total_ref[own] += jnp.sum(scaled, axis=1, keepdims=True)
    gain_total = jnp.zeros((1, width), f32)
    leaving = []
    for at, here in enumerate(blocks):
        mask = lax.broadcasted_iota(jnp.int32, (groups, STEP), 0) == gid_ref[:, here]
        for slot in range(experts):
            own = slice(slot, slot + 1)
            total = jnp.sum(jnp.where(mask, total_ref[slot], 0.0), axis=0, keepdims=True)
            gl_ref[own, here] = (part_ref[own, here] - wt_ref[own, here] * total).astype(bf16)
        hidden = hidden_ref[here, :].astype(f32)
        scale = rms_scale(hidden)
        unit = hidden * scale
        arriving[2, at].wait()
        if at + 1 < len(blocks):
            load((2,), at + 1)
        hidden_ref[here, :] = (hidden + dot(turned_ref[here, :], slots(0))).astype(bf16)
        leaving.append(push(hidden_ref.at[here], kept_out_ref.at[here], sems.at[4, at]))
        grad_normed = dot(turned_ref[here, :], slots(1)) + dot(gl_ref[:, here], small[:experts], TN)
        weighted = gain * grad_normed
        gain_total = gain_total + jnp.sum(grad_normed * unit, axis=0, keepdims=True)
        back = scale * (weighted - unit * jnp.mean(weighted * unit, axis=-1, keepdims=True))
        low = (cot_ref[here, :].astype(f32) + back).astype(bf16)
        cot_ref[here, :] = low
        leaving.append(push(cot_ref.at[here], kept_gh_ref.at[here], sems.at[5, at]))
        grad_att = dot(low, out_w, NT).astype(bf16)
        gown_ref[here, :] = grad_att[:, :half]
        gaway_ref[here, :] = grad_att[:, half:]
    for copy in atts:
        copy.wait()
    small_ref[:half, :width] = dot(own_ref[...], cot_ref[...], TN).astype(bf16)
    small_ref[half:, :width] = dot(away_ref[...], cot_ref[...], TN).astype(bf16)
    tail = [dot(gl_ref[...], normed_ref[...]), gain_total, jnp.zeros((127 - experts, width), f32)]
    small_ref[:, width:] = jnp.transpose(jnp.concatenate(tail, 0)).astype(bf16)
    for copy in leaving:
        copy.wait()


def unmix(back, weights, gid, gathered, turned, cotangent, hidden, att_own, att_away):
    rows, width = cotangent.shape
    experts, _, groups, _ = back.shape
    kept = (turned, cotangent, hidden, att_own, att_away)
    return call(
        unmix_kernel,
        (
            in_hbm((rows, width), bf16),
            in_hbm((rows, width), bf16),
            shape_of((rows, width // 2), bf16),
            shape_of((rows, width // 2), bf16),
            shape_of((width, width + 128), bf16),
        ),
        (pltpu.with_memory_space_constraint(back, pltpu.VMEM), weights, gid, from_hbm(gathered), *[from_hbm(array) for array in kept]),
        room=room_for(UNMIX_ROOM, experts * groups),
        in_specs=[VMEM, VMEM, VMEM] + [HBM] * 6,
        out_specs=[HBM] * 2 + [VMEM] * 3,
        scratch_shapes=[pltpu.VMEM(array.shape, bf16) for array in kept]
        + [
            pltpu.VMEM((width, width + 128), bf16),
            pltpu.VMEM((rows, width), bf16),
            pltpu.VMEM((experts, rows), f32),
            pltpu.VMEM((experts, groups, 1), f32),
            pltpu.VMEM((experts, rows), bf16),
            DMA((7, max(rows // STEP, 4))),
        ],
    )


def expert_kernel(
    pick_ref, in_ref, up_all_ref, down_all_ref, hint_ref,
    sent_ref, kept_act_ref, kept_pre_ref, kept_in_ref, mark_ref,
    up_ref, down_ref, act_ref, pre_ref, out_ref, load_sems, sems,
):
    parts, _, groups, width = in_ref.shape
    many = min(EXPERT_ROWS // groups, parts)
    pick = pick_ref[0]
    load_up = push(up_all_ref.at[pick], up_ref, load_sems.at[0])
    set_mark(mark_ref)
    copies = []
    for at, part in enumerate(range(0, parts, many)):
        here = slice(part * groups, (part + many) * groups)
        owners = slice(part, part + many)
        rows, grad = [in_ref[owners, place].reshape(many * groups, width) for place in range(2)]
        if at == 0:
            load_up.wait()
            load_down = push(down_all_ref.at[pick], down_ref, load_sems.at[1])
        pre = dot(rows, up_ref[...])
        if at == 0:
            load_down.wait()
            copies.append(push(in_ref, kept_in_ref, load_sems.at[2]))
        cdf = 0.5 + 0.5 * lax.erf(pre * 0.7071067811865476)
        slope = cdf + pre * (jnp.exp(-0.5 * pre * pre) * 0.3989422804014327)
        act = (pre * cdf).astype(bf16)
        act_ref[here, :] = act
        copies.append(push(act_ref.at[here], kept_act_ref.at[here], sems.at[0, at]))
        grad_pre = (dot(grad, down_ref[...], NT) * slope).astype(bf16)
        pre_ref[here, :] = grad_pre
        copies.append(push(pre_ref.at[here], kept_pre_ref.at[here], sems.at[1, at]))
        for place, result in enumerate((dot(act, down_ref[...]), dot(grad_pre, up_ref[...], NT))):
            out_ref[owners, place] = result.astype(bf16).reshape(many, groups, width)
            copies.append(push(out_ref.at[owners, place], sent_ref.at[owners, place], sems.at[2 + place, at]))
    for copy in copies:
        copy.wait()


def expert_pass(pick, arrived, w_up, w_down, hint):
    parts, _, groups, width = arrived.shape
    rows = parts * groups
    hidden = w_up.shape[2]
    return call(
        expert_kernel,
        (
            in_hbm(arrived.shape, bf16),
            in_hbm((rows, hidden), bf16),
            in_hbm((rows, hidden), bf16),
            in_hbm(arrived.shape, bf16),
            shape_of(MARK, f32),
        ),
        (pick, pltpu.with_memory_space_constraint(arrived, pltpu.VMEM), from_hbm(w_up), from_hbm(w_down), hint),
        room=room_for(EXPERT_ROOM, rows),
        in_specs=[SMEM, VMEM, HBM, HBM, ANY],
        out_specs=[HBM, HBM, HBM, HBM, VMEM],
        scratch_shapes=[
            pltpu.VMEM(w_up.shape[1:], bf16),
            pltpu.VMEM(w_down.shape[1:], bf16),
            pltpu.VMEM((rows, hidden), bf16),
            pltpu.VMEM((rows, hidden), bf16),
            pltpu.VMEM(arrived.shape, bf16),
            DMA((3,)),
            DMA((4, max(rows // EXPERT_ROWS, 1))),
        ],
    )


def expert_grad_kernel(
    in_ref, kept_act_ref, kept_pre_ref, hint_ref, grad_ref, mark_ref, act_ref, pre_ref, out_ref, load_sems, sems
):
    shards, pieces, per, width = grad_ref.shape
    rows, hidden = act_ref.shape
    slabs = [slice(at, at + width) for at in range(0, hidden, width)]
    loads = [
        [push(kept.at[:, slab], ref.at[:, slab], load_sems.at[place, at]) for at, slab in enumerate(slabs)]
        for place, (kept, ref) in enumerate(((kept_act_ref, act_ref), (kept_pre_ref, pre_ref)))
    ]
    down_pieces = hidden // shards // per
    set_mark(mark_ref)
    mixed, grad = [in_ref[:, place].reshape(rows, width) for place in range(2)]
    for at, slab in enumerate(slabs):
        loads[0][at].wait()
        grad_down = dot(act_ref[:, slab], grad, TN).astype(bf16)
        span = width // (down_pieces * per)
        out_ref[at * span : (at + 1) * span, :down_pieces] = grad_down.reshape(span, down_pieces, per, width)
    copies = [push(out_ref.at[:, :down_pieces], grad_ref.at[:, :down_pieces], sems.at[0])]
    for at, slab in enumerate(slabs):
        loads[1][at].wait()
        grad_up = dot(mixed, pre_ref[:, slab], TN).astype(bf16)
        out_ref[:, down_pieces + at] = grad_up.reshape(shards, per, width)
    copies.append(push(out_ref.at[:, down_pieces:], grad_ref.at[:, down_pieces:], sems.at[1]))
    for copy in copies:
        copy.wait()


def expert_grads(arrived, act, grad_pre, shards, hint):
    width = arrived.shape[3]
    hidden = act.shape[1]
    per = width // shards
    grad = (shards, (hidden // shards) // per + hidden // width, per, width)
    return call(
        expert_grad_kernel,
        (in_hbm(grad, bf16), shape_of(MARK, f32)),
        (arrived, from_hbm(act), from_hbm(grad_pre), hint),
        room=room_for(GRAD_ROOM, act.shape[0]),
        in_specs=[VMEM, HBM, HBM, ANY],
        out_specs=[HBM, VMEM],
        scratch_shapes=[
            pltpu.VMEM(act.shape, bf16),
            pltpu.VMEM(act.shape, bf16),
            pltpu.VMEM(grad, bf16),
            DMA((2, hidden // width)),
            DMA((2,)),
        ],
    )


def shard_sum_kernel(in_ref, *refs):
    down_ref, up_ref, mark_ref = refs[-3:]
    set_mark(mark_ref)
    total = in_ref[0, 0].astype(f32)
    for part in range(1, in_ref.shape[0]):
        total = total + in_ref[part, 0].astype(f32)
    down_rows, width = down_ref.shape[1:]
    down_ref[0] = total[:down_rows]
    per = up_ref.shape[1]
    for at in range(0, up_ref.shape[2] // width):
        here = down_rows + at * per
        up_ref[0, :, at * width : (at + 1) * width] = total[here : here + per]


def shard_sum(parts, per_owner, down_rows, up_rows, experts, before=()):
    shards, tall, width = parts.shape
    parts = parts.reshape(shards // per_owner, per_owner, tall, width)
    hidden = (tall - down_rows) // up_rows * width
    first = experts.start
    return call(
        shard_sum_kernel,
        (
            in_hbm((per_owner, down_rows, width), f32),
            in_hbm((per_owner, up_rows, hidden), f32),
            shape_of(MARK, f32),
        ),
        (parts, *before),
        grid=(len(experts),),
        in_specs=[pl.BlockSpec((parts.shape[0], 1, tall, width), lambda at: (0, first + at, 0, 0))]
        + [ANY] * len(before),
        out_specs=[
            pl.BlockSpec((1, down_rows, width), lambda at: (first + at, 0, 0)),
            pl.BlockSpec((1, up_rows, hidden), lambda at: (first + at, 0, 0)),
            pl.BlockSpec(MARK, lambda at: (0, 0)),
        ],
        input_output_aliases={1 + at: at for at in range(len(before))},
    )


def own_grad_kernel(unit_t_ref, grad_ref, w_ref, grad_w_ref, part_ref):
    wide = grad_ref.shape[1]
    grad_w_ref[...] = dot(unit_t_ref[...], grad_ref[...])
    for at in range(0, part_ref.shape[0], 1024):
        here = slice(at, at + 1024)
        part_ref[here, :] = dot(grad_ref[here, :], w_ref[:, :wide], NT)


def own_grad(unit_t, grad, weights):
    width, rows = unit_t.shape
    return call(
        own_grad_kernel,
        (shape_of((width, grad.shape[1]), f32), shape_of((rows, width), f32)),
        (unit_t, grad, weights),
        room=16,
        in_specs=[VMEM] * 3,
        out_specs=[VMEM] * 2,
    )


def away_grad_kernel(mine_ref, unit_t_ref, grad_ref, own_ref, small_ref, keep_ref, send_ref, total_ref):
    total_ref[...] = dot(unit_t_ref[...], grad_ref[...])
    many, per, _ = keep_ref.shape
    mine = mine_ref[0]
    left = own_ref.shape[1]
    right = left + total_ref.shape[1]
    for place in range(many):
        for part, ref in ((mine, keep_ref), (1 - mine, send_ref)):
            rows = pl.ds(pl.multiple_of((2 * place + part) * per, per), per)
            ref[place, :, :left] = own_ref[rows, :].astype(ref.dtype)
            ref[place, :, left:right] = total_ref[rows, :].astype(ref.dtype)
            ref[place, :, right:] = small_ref[rows, :].astype(ref.dtype)


def halves(array, mine):
    keep, send = [lax.dynamic_index_in_dim(array, part[0], 1, keepdims=False) for part in (mine, 1 - mine)]
    return keep, send.astype(bf16)


def away_grad(mine, unit_t, grad, own, small, devices):
    width, rows = unit_t.shape
    wide = grad.shape[1]
    per = width // devices
    if per % 16:
        total = jnp.concatenate([own, dot(unit_t, grad), small.astype(f32)], 1)
        return halves(total.reshape(devices // 2, 2, per, -1), mine)
    dims = (devices // 2, per, own.shape[1] + wide + small.shape[1])
    return call(
        away_grad_kernel,
        (shape_of(dims, f32), shape_of(dims, bf16)),
        (mine, unit_t, grad, own, small),
        room=16,
        in_specs=[SMEM] + [VMEM] * 4,
        out_specs=[VMEM] * 2,
        scratch_shapes=[pltpu.VMEM((width, wide), f32)],
    )


def token_grad_kernel(part_ref, grad_ref, w_ref, tok_ref, gh_ref, out_ref, mark_ref):
    set_mark(mark_ref)
    wide = grad_ref.shape[1]
    for at in range(0, tok_ref.shape[0], 512):
        here = slice(at, at + 512)
        weighted = part_ref[here, :] + dot(grad_ref[here, :], w_ref[:, wide : 2 * wide], NT)
        source = tok_ref[here, :].astype(f32)
        scale = rms_scale(source)
        unit = source * scale
        back = scale * (weighted - unit * jnp.mean(weighted * unit, axis=-1, keepdims=True))
        out_ref[here, :] = (gh_ref[here, :].astype(f32) + back).astype(bf16)


def token_grad(part, grad, weights, tokens, grad_hidden):
    return call(
        token_grad_kernel,
        (shape_of(tokens.shape, bf16), shape_of(MARK, f32)),
        (part, grad, weights, tokens, grad_hidden),
        room=16,
        in_specs=[VMEM] * 5,
        out_specs=[VMEM] * 2,
    )


def swap(array, axis, size, bit):
    return lax.ppermute(array, axis, [(at, at ^ bit) for at in range(size)])


def axis_bits(sizes):
    bits = []
    for axis, size in sizes:
        bit = size // 2
        while bit:
            bits.append((axis, size, bit))
            bit //= 2
    return bits


def gather_rows(shard, sizes, meanwhile):
    bits = axis_bits(sizes)
    held = shard[(None,) * len(bits)]
    for place, (axis, size, bit) in enumerate(bits):
        other = swap(held, axis, size, bit)
        if place == len(bits) - 2:
            other, meanwhile = lax.optimization_barrier((other, meanwhile))
        upper = (lax.axis_index(axis) // bit) % 2 == 1
        first = jnp.where(upper, other, held)
        second = jnp.where(upper, held, other)
        held = jnp.concatenate([first, second], axis=place)
    return held.reshape((shard.shape[0] * 2 ** len(bits),) + shard.shape[1:]), meanwhile


def add_split_kernel(mine_ref, keep_ref, got_ref, hint_ref, next_keep_ref, send_ref):
    mine = mine_ref[0]
    for part, ref in ((mine, next_keep_ref), (1 - mine, send_ref)):
        value = keep_ref[:, pl.ds(part, 1)] + got_ref[:, pl.ds(part, 1)].astype(f32)
        ref[...] = value[:, 0].astype(ref.dtype)


def add_split(mine, keep, got, hint):
    many, per, wide = keep.shape
    dims = (many // 2, per, wide)
    keep, got = [array.reshape(many // 2, 2, per, wide) for array in (keep, got)]
    if per % 16:
        return halves(keep + got.astype(f32), mine)
    return call(
        add_split_kernel,
        (shape_of(dims, f32), shape_of(dims, bf16)),
        (mine, keep, got, hint),
        room=16,
        in_specs=[SMEM, VMEM, VMEM, ANY],
        out_specs=[VMEM] * 2,
    )


def scatter_rows(keep, send, sizes, hints):
    bits = axis_bits(sizes)[::-1]
    for place, (axis, size, bit) in enumerate(bits):
        got = swap(send, axis, size, bit)
        if place + 1 == len(bits):
            return keep, got
        axis, size, bit = bits[place + 1]
        mine = ((lax.axis_index(axis) // bit) % 2).astype(jnp.int32).reshape(1)
        keep, send = add_split(mine, keep, got, hints.get(place, got))


def on_device(
    n_dp, n_owner, tokens, seq_lengths, group_map, gain_attn, gain_mix, w_qkv, w_out, w_ctrl, w_up, w_down, cotangent
):
    rows, width = tokens.shape
    experts = w_ctrl.shape[1]
    per_owner = w_up.shape[0]
    groups = rows // G
    parts = n_dp // per_owner
    sizes = (("dp", n_dp), ("expert", n_owner))
    dp = lax.axis_index("dp")
    pick = (dp % per_owner).astype(jnp.int32).reshape(1)

    gain_row = gain_attn.reshape(1, -1)
    shard = call(
        functools.partial(pack_kernel, n_owner),
        shape_of((w_ctrl.shape[0], 4 * width + 128), bf16),
        (seq_lengths, *[from_hbm(array) for array in (w_qkv, gain_row, w_out, w_ctrl, gain_mix.reshape(1, -1))]),
        room=8,
        in_specs=[SMEM] + [VMEM] * 5,
        out_specs=VMEM,
    )

    def neighbour(array):
        return swap(array, "expert", n_owner, 1)

    unit_one, unit_away, unit_t, gid = call(
        prep_kernel,
        (
            in_hbm((rows, width), bf16),
            in_hbm((rows, width), bf16),
            in_hbm((width, rows), bf16),
            shape_of((1, rows), jnp.int32),
        ),
        (tokens, neighbour(tokens), group_map.reshape(groups, G)),
        room=16,
        in_specs=[VMEM] * 3,
        out_specs=[HBM, HBM, HBM, VMEM],
        scratch_shapes=[pltpu.VMEM((rows, width), bf16)] * 2 + [pltpu.VMEM((width, rows), bf16), DMA((3, rows // 512))],
    )
    gathered, (unit_one, unit_away) = gather_rows(shard, sizes, (unit_one, unit_away))
    triple = 3 * width

    near = (dp * n_owner + (lax.axis_index("expert") ^ 1)) * w_ctrl.shape[0]
    lengths, att_own, att_away, lse_own, lse_away, own_qkv, away_qkv, kept_away = attend_forward(
        seq_lengths, near.astype(jnp.int32).reshape(1), unit_one, unit_away, gathered
    )
    hidden, weights, mixed, kept_own, kept_back = mix(
        tokens, att_own, neighbour(att_away), gathered, gid, cotangent, experts
    )

    teams = [
        [(part * per_owner + low) * n_owner + owner for low in range(per_owner) for owner in range(n_owner)]
        for part in range(parts)
    ]

    def exchange(array):
        return lax.all_to_all(
            array, ("dp", "expert"), split_axis=0, concat_axis=0, axis_index_groups=teams, tiled=True
        )

    arrived = exchange(mixed)
    turned, mark = turn(weights, gid, groups)
    results, act, grad_pre, arrived, mark = expert_pass(pick, arrived, w_up, w_down, mark)
    back = exchange(results)
    grad_experts, mark = expert_grads(arrived, act, grad_pre, n_dp, mark)
    shards = lax.all_to_all(
        grad_experts.reshape(n_dp, -1, width), "dp", split_axis=0, concat_axis=0, tiled=True
    )
    output, grad_hidden, grad_own, grad_away, grad_small = unmix(
        back, weights, gid, gathered, turned, cotangent, hidden, kept_own, kept_back
    )

    grad_here = neighbour(grad_away)
    grad_one = attend_backward(0, lengths, own_qkv, grad_own, kept_own, lse_own, grad_own)
    grad_two = neighbour(attend_backward(1, lengths, away_qkv, grad_here, kept_away, lse_away, grad_one))
    grad_w_own, token_part = own_grad(unit_t, grad_one, gathered)
    axis, size, bit = axis_bits(sizes)[-1]
    mine = ((lax.axis_index(axis) // bit) % 2).astype(jnp.int32).reshape(1)
    keep, send = away_grad(mine, unit_t, grad_two, grad_w_own, grad_small, n_dp * n_owner)
    grad_tokens, token_mark = token_grad(token_part, grad_two, gathered, tokens, grad_hidden)
    shapes = (per_owner, w_down.shape[1] // n_dp, width // n_dp)
    *some, shard_mark = shard_sum(shards, *shapes, range(per_owner // 2))
    grad_down_shard, grad_up_shard, _ = shard_sum(shards, *shapes, range(per_owner // 2, per_owner), some)
    keep, got = scatter_rows(keep, send, sizes, {1: token_mark, len(axis_bits(sizes)) - 2: shard_mark})
    own_rows = w_qkv.shape[0]
    shard_qkv, shard_out, shard_ctrl, shard_gain_one, shard_gain_two = call(
        functools.partial(finish_kernel, n_owner),
        (
            shape_of(w_qkv.shape, f32),
            shape_of(w_out.shape, f32),
            shape_of(w_ctrl.shape, f32),
            shape_of((1, own_rows), f32),
            shape_of((1, own_rows), f32),
        ),
        (keep, got, gain_row, w_qkv),
        room=8,
        in_specs=[VMEM] * 4,
        out_specs=[VMEM] * 5,
    )
    return (
        output,
        grad_tokens,
        shard_gain_one.reshape(-1),
        shard_gain_two.reshape(-1),
        shard_qkv,
        shard_out,
        shard_ctrl,
        grad_up_shard,
        grad_down_shard,
    )


def solution(mesh):
    both = ("dp", "expert")
    rows = P(both, None)
    return jax.shard_map(
        functools.partial(on_device, mesh.shape["dp"], mesh.shape["expert"]),
        mesh=mesh,
        in_specs=(
            rows, P(both), rows, P(both), P(both), rows, rows, rows,
            P("expert", None, None), P("expert", None, None), rows,
        ),
        out_specs=(
            rows, rows, P(both), P(both), rows, rows, rows,
            P("expert", "dp", None), P("expert", "dp", None),
        ),
        check_vma=False,
    )
```

```python
import functools

import jax
import jax.numpy as jnp
from jax import lax
from jax.experimental import pallas as pl
from jax.experimental.pallas import tpu as pltpu
from jax.sharding import PartitionSpec as P

HEADS = 8
G = 32
BQ = 256

ANY = pl.BlockSpec(memory_space=pl.ANY)
VMEM = pl.BlockSpec(memory_space=pltpu.VMEM)
HBM = pl.BlockSpec(memory_space=pltpu.HBM)
DMA = pltpu.SemaphoreType.DMA
SMEM = pl.BlockSpec(memory_space=pltpu.SMEM)

eps_norm = 1e-05
masked_value = -1e30
bf16 = jnp.bfloat16
f32 = jnp.float32
NN = (((1,), (0,)), ((), ()))
NT = (((1,), (1,)), ((), ()))
TN = (((0,), (0,)), ((), ()))


def dot(left, right, dims=NN):
    return lax.dot_general(left, right, dims, preferred_element_type=f32)


def rms_scale(values):
    return lax.rsqrt(jnp.mean(values * values, axis=-1, keepdims=True) + eps_norm)


def call(body, out_shape, args, room=28, **extra):
    return pl.pallas_call(
        body,
        out_shape=out_shape,
        compiler_params=pltpu.CompilerParams(vmem_limit_bytes=room * 2**20),
        name=getattr(body, "func", body).__name__,
        **extra,
    )(*args)


def shape_of(dims, kind):
    return jax.ShapeDtypeStruct(dims, kind)


def in_hbm(dims, kind):
    return pltpu.HBM(dims, kind)


def in_vmem(dims, kind):
    return pltpu.VMEM(dims, kind)


def from_hbm(array):
    return pltpu.with_memory_space_constraint(array, pltpu.HBM)


def room_for(parts, rows):
    fixed, per_block = parts
    return fixed + per_block * rows // 1024


def push(source, target, sem):
    copy = pltpu.make_async_copy(source, target, sem)
    copy.start()
    return copy


MARK = (8, 128)


def set_mark(ref):
    ref[...] = jnp.zeros(MARK, f32)


def diagonal(size):
    return lax.broadcasted_iota(jnp.int32, (size, size), 0) == lax.broadcasted_iota(jnp.int32, (size, size), 1)


def column_of(row):
    return jnp.sum(jnp.where(diagonal(row.shape[1]), row, 0.0), axis=1, keepdims=True)


def row_of(column):
    return jnp.sum(jnp.where(diagonal(column.shape[0]), column, 0.0), axis=0, keepdims=True)


def slot_matrix(experts, wide, n_owner, kind):
    expert = lax.broadcasted_iota(jnp.int32, (experts, wide), 0)
    slot = lax.broadcasted_iota(jnp.int32, (experts, wide), 1)
    per_owner = experts // n_owner
    return jnp.where(expert % per_owner * n_owner + expert // per_owner == slot, 1.0, 0.0).astype(kind)


def pack_kernel(n_owner, len_ref, wqkv_ref, gain_ref, wout_ref, ctrl_ref, mix_ref, out_ref):
    width = wout_ref.shape[1]
    experts = ctrl_ref.shape[1]
    gain = column_of(gain_ref[...].astype(f32))
    for pair in range(width // 128):
        for part in range(3):
            at = part * width + pair * 128
            to = pair * 384 + part * 128
            out_ref[:, to : to + 128] = (wqkv_ref[:, at : at + 128].astype(f32) * gain).astype(bf16)
    out_ref[:, 3 * width : 4 * width] = wout_ref[...]
    small = dot(ctrl_ref[...], slot_matrix(experts, 128, n_owner, bf16))
    lane = lax.broadcasted_iota(jnp.int32, small.shape, 1)
    small = jnp.where(lane == experts, column_of(mix_ref[...].astype(f32)), small)
    small = jnp.where(lane == 127, len_ref[0].astype(f32), small)
    out_ref[:, 4 * width :] = small.astype(bf16)


def finish_kernel(n_owner, keep_ref, got_ref, gain_ref, wqkv_ref, qkv_ref, out_ref, ctrl_ref, one_ref, mix_ref):
    width = out_ref.shape[1]
    experts = ctrl_ref.shape[1]
    total = keep_ref[0] + got_ref[0].astype(f32)
    gain = column_of(gain_ref[...].astype(f32))
    grad_gain = jnp.zeros((total.shape[0], 128), f32)
    for pair in range(width // 128):
        for part in range(3):
            to = part * width + pair * 128
            at = pair * 384 + part * 128
            grad = total[:, at : at + 128]
            qkv_ref[:, to : to + 128] = gain * grad
            grad_gain = grad_gain + wqkv_ref[:, to : to + 128].astype(f32) * grad
    out_ref[...] = total[:, 3 * width : 4 * width]
    small = total[:, 4 * width :]
    slots = slot_matrix(experts, 128, n_owner, f32)
    ctrl_ref[...] = lax.dot_general(small, slots, NT, precision=lax.Precision.HIGHEST, preferred_element_type=f32)
    one_ref[...] = row_of(jnp.sum(grad_gain, axis=1, keepdims=True))
    lane = lax.broadcasted_iota(jnp.int32, small.shape, 1)
    mix_ref[...] = row_of(jnp.sum(jnp.where(lane == experts, small, 0.0), axis=1, keepdims=True))


def prep_kernel(
    tok_ref, tok_away_ref, gmap_ref, kept_ref, kept_away_ref, kept_t_ref, gid_ref, unit_ref, away_ref, unit_t_ref, sems
):
    rows = tok_ref.shape[0]
    step = 512
    copies = []
    sides = ((tok_ref, unit_ref, kept_ref), (tok_away_ref, away_ref, kept_away_ref))
    for side, (source, target, kept) in enumerate(sides):
        for at in range(0, rows, step):
            here = slice(at, at + step)
            block = source[here, :].astype(f32)
            unit = (block * rms_scale(block)).astype(bf16)
            target[here, :] = unit
            copies.append(push(target.at[here], kept.at[here], sems.at[side, at // step]))
            if side == 0:
                unit_t_ref[:, here] = jnp.transpose(unit)
        if side == 0:
            copies.append(push(unit_t_ref, kept_t_ref, sems.at[2, 0]))
    groups = rows // G
    places = lax.broadcasted_iota(jnp.int32, (groups, rows), 1)
    group_at = lax.broadcasted_iota(jnp.int32, (groups, rows), 0)
    gmap = gmap_ref[...]
    member = jnp.zeros((groups, rows), jnp.int32)
    for slot in range(G):
        member = jnp.where(gmap[:, slot : slot + 1] == places, group_at, member)
    gid_ref[...] = jnp.sum(member.astype(f32), axis=0, keepdims=True).astype(jnp.int32)
    for copy in copies:
        copy.wait()


def lower_mask():
    return lax.broadcasted_iota(jnp.int32, (BQ, BQ), 0) <= lax.broadcasted_iota(jnp.int32, (BQ, BQ), 1)


def head_lanes():
    return lax.broadcasted_iota(jnp.int32, (1, 128), 1) // 64


def attend_pair(length, pair, qkv_all_ref, out_ref, lse_all_ref, vt_ref):
    qkv_ref = qkv_all_ref.at[:, pl.ds(pl.multiple_of(pair * 384, 384), 384)]
    lse_ref = lse_all_ref.at[pl.ds(pair, 1)]
    rows = qkv_ref.shape[0]
    step, ahead = 512, 6
    lane = head_lanes()
    vt_ref[...] = jnp.transpose(qkv_ref[:, 256:384])

    def run(low_of):
        items = []
        for at in range(0, rows, BQ):
            chunks = [(at, BQ)]
            top = at
            while top > low_of(at):
                down = max(low_of(at), top - step)
                chunks.append((down, top - down))
                top = down
            for place, (low, wide) in enumerate(chunks):
                for head in range(2):
                    items.append((at, head, low, wide, place == 0, place == len(chunks) - 1))

        def score(at, head, low, wide, first, last):
            own = jnp.where(lane == head, qkv_ref[at : at + BQ, 0:128] * bf16(0.125), bf16(0))
            scores = dot(qkv_ref[low : low + wide, 128:256], own, NT)
            return jnp.where(lower_mask(), scores, masked_value) if first else scores

        pending = [score(*item) for item in items[:ahead]]
        state = {}
        for place, (at, head, low, wide, first, last) in enumerate(items):
            if place + ahead < len(items):
                pending.append(score(*items[place + ahead]))
            scores = pending.pop(0)
            peak = jnp.max(scores, axis=0, keepdims=True)
            if not first:
                old_peak, old_total, old_mixed = state[head]
                peak = jnp.maximum(old_peak, peak)
                shrink = jnp.exp(old_peak - peak)
            probs = jnp.exp(scores - peak)
            total = jnp.sum(probs, axis=0, keepdims=True)
            mixed = dot(vt_ref[64 * head : 64 * head + 64, low : low + wide], probs.astype(bf16))
            if not first:
                total = total + old_total * shrink
                mixed = mixed + old_mixed * shrink
            state[head] = (peak, total, mixed)
            if last:
                lse_ref[0, head : head + 1, at : at + BQ] = peak + jnp.log(total)
                if head == 1:
                    both = [state[own][2] * (1.0 / state[own][1]) for own in range(2)]
                    out_ref[at : at + BQ, :] = jnp.transpose(jnp.concatenate(both, 0)).astype(bf16)

    @pl.when(length == BQ)
    def _():
        run(lambda at: at)

    @pl.when(length != BQ)
    def _():
        run(lambda at: 0)


def attend_kernel(
    len_ref, place_ref, kept_own_ref, kept_away_ref, w_ref,
    lens_ref, own_ref, away_ref, lse_own_ref, lse_away_ref, kept_qkv_own_ref, kept_qkv_away_ref, kept_out_ref,
    unit_ref, qkv_ref, out_ref, lse_ref, vt_ref, unit_sems, sems,
):
    row = pl.multiple_of(place_ref[0] // 16 * 16, 16)
    tile = w_ref[pl.ds(row, 16), w_ref.shape[1] - 128 :].astype(f32)
    chosen = lax.broadcasted_iota(jnp.int32, tile.shape, 1) == 127
    chosen = chosen & (lax.broadcasted_iota(jnp.int32, tile.shape, 0) == place_ref[0] % 16)
    lens_ref[0] = len_ref[0]
    lens_ref[1] = jnp.max(jnp.where(chosen, tile, 0.0)).astype(jnp.int32)
    rows, wide = qkv_ref.shape
    half = wide // 2
    pairs = wide // 384
    count = unit_sems.shape[0] // 2
    blocks = [slice(at, at + rows // count) for at in range(0, rows, rows // count)]
    kept = (kept_qkv_own_ref, kept_qkv_away_ref)
    copies, keeping = [], []

    def load(at):
        if at < 2 * count:
            source = (kept_own_ref, kept_away_ref)[at // count]
            copies.append(push(source.at[blocks[at % count]], unit_ref.at[at % 3], unit_sems.at[at]))

    load(0)
    load(1)
    for at in range(2 * count):
        side = at // count
        copies[at].wait()
        load(at + 2)
        columns = slice(side * half, (side + 1) * half)
        qkv_ref[blocks[at % count], columns] = dot(unit_ref[at % 3], w_ref[:, columns]).astype(bf16)
        if at % count == count - 1:
            keeping.append(push(qkv_ref.at[:, columns], kept[side], sems.at[side]))

    def keep_out(pair):
        thin = pl.ds(pl.multiple_of((pair - pairs // 2) * 128, 128), 128)
        return pltpu.make_async_copy(away_ref.at[:, thin], kept_out_ref.at[:, thin], sems.at[2 + pair])

    @pl.loop(0, pairs)
    def _(pair):
        mine = pair < pairs // 2
        attend_pair(lens_ref[jnp.where(mine, 0, 1)], pair, qkv_ref, out_ref, lse_ref, vt_ref)

        @pl.when(mine)
        def _():
            own_ref[:, pl.ds(pl.multiple_of(pair * 128, 128), 128)] = out_ref[...]

        @pl.when(jnp.logical_not(mine))
        def _():
            away_ref[:, pl.ds(pl.multiple_of((pair - pairs // 2) * 128, 128), 128)] = out_ref[...]
            keep_out(pair).start()

    lse_own_ref[...] = lse_ref[: pairs // 2]
    lse_away_ref[...] = lse_ref[pairs // 2 :]
    for copy in keeping:
        copy.wait()
    for pair in range(pairs // 2, pairs):
        keep_out(pair).wait()


def attend_forward(length, place, unit, unit_away, gathered):
    rows, width = unit.shape
    pairs = width // 128
    count = 4
    half = pairs // 2
    lse = shape_of((half, 2, rows), f32)
    return call(
        attend_kernel,
        (
            shape_of((2,), jnp.int32),
            shape_of((rows, 128 * half), bf16),
            shape_of((rows, 128 * half), bf16),
            lse,
            lse,
            in_hbm((rows, 384 * half), bf16),
            in_hbm((rows, 384 * half), bf16),
            in_hbm((rows, 128 * half), bf16),
        ),
        (length, place, from_hbm(unit), from_hbm(unit_away), gathered),
        room=ATTEND_ROOM,
        in_specs=[SMEM, SMEM, HBM, HBM, VMEM],
        out_specs=[SMEM] + [VMEM] * 4 + [HBM] * 3,
        scratch_shapes=[
            pltpu.VMEM((3, rows // count, width), bf16),
            pltpu.VMEM((rows, 384 * pairs), bf16),
            pltpu.VMEM((rows, 128), bf16),
            pltpu.VMEM((pairs, 2, rows), f32),
            pltpu.VMEM((128, rows), bf16),
            DMA((2 * count,)),
            DMA((2 + pairs,)),
        ],
    )


def attend_back_kernel(side, lens_ref, qkv_ref, go_ref, o_ref, lse_ref, hint_ref, grad_ref, *scratch):
    @pl.loop(0, qkv_ref.shape[1] // 384)
    def _(pair):
        wide = pl.ds(pl.multiple_of(pair * 384, 384), 384)
        thin = pl.ds(pl.multiple_of(pair * 128, 128), 128)
        refs = [qkv_ref.at[:, wide], go_ref.at[:, thin], o_ref.at[:, thin], lse_ref.at[pl.ds(pair, 1)]]
        attend_back_pair(lens_ref[side], *refs, grad_ref.at[:, wide], *scratch)


def attend_back_pair(length, qkv_ref, go_ref, o_ref, lse_ref, grad_ref, gqt_ref, kt_ref, dl_ref):
    rows = qkv_ref.shape[0]
    step, ahead = 256, 2
    lane = head_lanes()
    kt_ref[...] = jnp.transpose(qkv_ref[:, 128:256]) * bf16(0.125)
    product = (go_ref[...].astype(f32) * o_ref[...].astype(f32)).astype(bf16)
    of_head = lax.broadcasted_iota(jnp.int32, (8, 128), 0) == lax.broadcasted_iota(jnp.int32, (8, 128), 1) // 64
    dl_ref[...] = dot(jnp.where(of_head, 1.0, 0.0).astype(bf16), product, NT)

    def run(end_of):
        items = []
        for low in range(0, rows, BQ):
            end = end_of(low)
            chunks = [(low, BQ)] + [(at, min(step, end - at)) for at in range(low + BQ, end, step)]
            for place, (at, wide) in enumerate(chunks):
                for head in range(2):
                    items.append((low, head, at, wide, place == 0, place == len(chunks) - 1))
        blocks = {}
        written = set()

        def products(low, head, at, wide, first, last):
            if (low, head) not in blocks:
                keys = qkv_ref[low : low + BQ, 128:256] * bf16(0.125)
                vals = qkv_ref[low : low + BQ, 256:384]
                blocks[low, head] = [jnp.where(lane == head, own, bf16(0)) for own in (keys, vals)]
            keys, vals = blocks[low, head]
            return (
                dot(keys, qkv_ref[at : at + wide, 0:128], NT),
                dot(vals, go_ref[at : at + wide, :], NT),
            )

        pending = [products(*item) for item in items[:ahead]]
        grad_k, grad_v = {}, {}
        for place, (low, head, at, wide, first, last) in enumerate(items):
            if place + ahead < len(items):
                pending.append(products(*items[place + ahead]))
            scores, grad_probs = pending.pop(0)
            here = slice(at, at + wide)
            probs = jnp.exp(scores - lse_ref[0, head : head + 1, here])
            if first:
                probs = jnp.where(lower_mask(), probs, 0.0)
            grad_scores = (probs * (grad_probs - dl_ref[head : head + 1, here])).astype(bf16)
            more_v = dot(probs.astype(bf16), go_ref[here, :])
            more_k = dot(grad_scores, qkv_ref[here, 0:128])
            grad_v[head] = more_v if first else grad_v[head] + more_v
            grad_k[head] = more_k if first else grad_k[head] + more_k
            span = slice(64 * head, 64 * head + 64)
            more_q = dot(kt_ref[span, low : low + BQ], grad_scores)
            fresh = (head, at + wide) not in written
            written.update((head, top) for top in range(at + BQ, at + wide + BQ, BQ))
            if fresh:
                gqt_ref[span, here] = more_q
            else:
                gqt_ref[span, here] += more_q
            if last and head == 1:
                there = slice(low, low + BQ)
                grad_ref[there, 128:256] = (jnp.where(lane == 0, grad_k[0], grad_k[1]) * 0.125).astype(bf16)
                grad_ref[there, 256:384] = jnp.where(lane == 0, grad_v[0], grad_v[1]).astype(bf16)

    @pl.when(length == BQ)
    def _():
        run(lambda low: low + BQ)

    @pl.when(length != BQ)
    def _():
        run(lambda low: rows)

    grad_ref[:, 0:128] = jnp.transpose(gqt_ref[...]).astype(bf16)


def attend_backward(side, lengths, qkv, grad_attended, attended, log_totals, hint):
    rows = qkv.shape[0]
    return call(
        functools.partial(attend_back_kernel, side),
        shape_of(qkv.shape, bf16),
        (lengths, qkv, grad_attended, attended, log_totals, hint),
        room=ATTEND_ROOM,
        in_specs=[SMEM, VMEM, VMEM, VMEM, VMEM, ANY],
        out_specs=VMEM,
        scratch_shapes=[pltpu.VMEM((128, rows), f32), pltpu.VMEM((128, rows), bf16), pltpu.VMEM((8, rows), f32)],
    )


STEP = 512
UNMIX_ROOM = (24, 12)
MIX_ROOM = (12, 12)
ATTEND_ROOM = 24
EXPERT_ROOM = (20, 16)
GRAD_ROOM = (16, 20)
EXPERT_ROWS = 512
MIX_ROWS = 1024


def member_mask(gid_ref, groups):
    wide = gid_ref.shape[1]
    return lax.broadcasted_iota(jnp.int32, (groups, wide), 0) == gid_ref[...]


def mix_kernel(
    tok_ref, own_ref, away_ref, w_all_ref, gid_ref, cot_ref,
    kept_hidden_ref, wt_ref, sent_ref, kept_own_ref, kept_away_ref, normed_ref, w_ref, hidden_ref, mixed_ref, sems, send_sems,
):
    copies = [push(away_ref, kept_away_ref, sems.at[0]), push(own_ref, kept_own_ref, sems.at[2])]
    rows, width = tok_ref.shape
    experts, _, groups, _ = mixed_ref.shape
    half = width // 2
    out_w = w_all_ref[:, 3 * width : 4 * width]
    small = jnp.transpose(w_all_ref[:, 4 * width :])
    gain = small[experts : experts + 1, :].astype(f32)
    for at in range(0, rows, 512):
        here = slice(at, at + 512)
        hidden = tok_ref[here, :].astype(f32) + dot(own_ref[here, :], out_w[:half])
        hidden = (hidden + dot(away_ref[here, :], out_w[half:])).astype(bf16)
        hidden_ref[here, :] = hidden
        hidden = hidden.astype(f32)
        normed_ref[here, :] = (hidden * rms_scale(hidden) * gain).astype(bf16)
    copies.append(push(hidden_ref, kept_hidden_ref, sems.at[1]))
    logits = dot(small[:experts], normed_ref[...], NT)
    mask = member_mask(gid_ref, groups)
    for slot in range(experts):
        wide = jnp.where(mask, logits[slot : slot + 1, :], masked_value)
        wide = jnp.exp(wide - jnp.max(wide, axis=1, keepdims=True))
        wide = wide * (1.0 / jnp.sum(wide, axis=1, keepdims=True))
        wt_ref[slot : slot + 1, :] = jnp.sum(wide, axis=0, keepdims=True)
        w_ref[slot * groups : (slot + 1) * groups, :] = wide.astype(bf16)
    many = min(512 // groups, experts)
    for place, ref in enumerate((normed_ref, cot_ref)):
        for slot in range(0, experts, many):
            mixed = dot(w_ref[slot * groups : (slot + many) * groups, :], ref[...]).astype(bf16)
            own = slice(slot, slot + many)
            mixed_ref[own, place] = mixed.reshape(many, groups, width)
            copies.append(push(mixed_ref.at[own, place], sent_ref.at[own, place], send_sems.at[place, slot // many]))
    for copy in copies:
        copy.wait()


def mix(tokens, att_own, att_away, gathered, gid, cotangent, experts):
    rows, width = tokens.shape
    groups = rows // G
    sent = (experts, 2, groups, width)
    return call(
        mix_kernel,
        (
            in_hbm((rows, width), bf16),
            shape_of((experts, rows), f32),
            in_hbm(sent, bf16),
            in_hbm(att_own.shape, bf16),
            in_hbm(att_away.shape, bf16),
        ),
        (tokens, att_own, att_away, gathered, gid, cotangent),
        room=room_for(MIX_ROOM, experts * groups),
        in_specs=[VMEM] * 6,
        out_specs=[HBM, VMEM, HBM, HBM, HBM],
        scratch_shapes=[
            pltpu.VMEM((rows, width), bf16),
            pltpu.VMEM((experts * groups, rows), bf16),
            pltpu.VMEM((rows, width), bf16),
            pltpu.VMEM(sent, bf16),
            DMA((3,)),
            DMA((2, max(experts * groups // 512, 1))),
        ],
    )


def turn_kernel(wt_ref, gid_ref, kept_ref, mark_ref, turned_ref, sem):
    set_mark(mark_ref)
    experts, rows = wt_ref.shape
    groups = turned_ref.shape[1] // experts
    many = 256 // groups
    for at in range(0, rows, STEP):
        here = slice(at, at + STEP)
        mask = lax.broadcasted_iota(jnp.int32, (groups, STEP), 0) == gid_ref[:, here]
        for slot in range(0, experts, many):
            parts = [
                jnp.where(mask, wt_ref[own : own + 1, here], 0.0).astype(bf16) for own in range(slot, slot + many)
            ]
            turned_ref[here, slot * groups : (slot + many) * groups] = jnp.transpose(jnp.concatenate(parts, 0))
    push(turned_ref, kept_ref, sem).wait()


def turn(weights, gid, groups):
    experts, rows = weights.shape
    return call(
        turn_kernel,
        (in_hbm((rows, experts * groups), bf16), shape_of(MARK, f32)),
        (weights, gid),
        room=16,
        in_specs=[VMEM] * 2,
        out_specs=[HBM, VMEM],
        scratch_shapes=[pltpu.VMEM((rows, experts * groups), bf16), DMA],
    )


def unmix_kernel(
    back_ref, wt_ref, gid_ref, w_all_ref, kept_turned_ref, kept_cot_ref, kept_hidden_ref, kept_own_ref,
    kept_away_ref, kept_out_ref, kept_gh_ref, gown_ref, gaway_ref, small_ref,
    turned_ref, cot_ref, hidden_ref, own_ref, away_ref, rest_ref, normed_ref, part_ref, total_ref, gl_ref,
    sems,
):
    experts, _, groups, width = back_ref.shape
    rows = cot_ref.shape[0]
    half = width // 2
    many = min(MIX_ROWS // groups, experts)
    blocks = [slice(at, at + STEP) for at in range(0, rows, STEP)]
    sources = (kept_cot_ref, kept_hidden_ref, kept_turned_ref)
    targets = (cot_ref, hidden_ref, turned_ref)
    arriving = {}

    def load(kinds, at):
        for kind in kinds:
            here = blocks[at]
            arriving[kind, at] = push(sources[kind].at[here], targets[kind].at[here], sems.at[kind, at])

    rest = push(w_all_ref.at[:, 3 * width :], rest_ref, sems.at[6, 0])
    load((0, 1), 0)
    rest.wait()
    out_w = rest_ref[:, :width]
    small = jnp.transpose(rest_ref[:, width:])
    gain = small[experts : experts + 1, :].astype(f32)
    total_ref[...] = jnp.zeros_like(total_ref)

    def slots(place, first=0, count=experts):
        return back_ref[first : first + count, place].reshape(count * groups, width)

    for at, here in enumerate(blocks):
        arriving[0, at].wait()
        arriving[1, at].wait()
        if at + 1 < len(blocks):
            load((0, 1), at + 1)
        else:
            load((2,), 0)
            atts = [push(kept_own_ref, own_ref, sems.at[3, 0]), push(kept_away_ref, away_ref, sems.at[3, 1])]
        hidden = hidden_ref[here, :].astype(f32)
        normed = (hidden * rms_scale(hidden) * gain).astype(bf16)
        normed_ref[here, :] = normed
        mask = lax.broadcasted_iota(jnp.int32, (groups, STEP), 0) == gid_ref[:, here]
        for slot in range(0, experts, many):
            wide = dot(slots(0, slot, many), cot_ref[here, :], NT) + dot(slots(1, slot, many), normed, NT)
            for own in range(slot, slot + many):
                part = wide[(own - slot) * groups : (own - slot + 1) * groups]
                scaled = jnp.where(mask, part * wt_ref[own : own + 1, here], 0.0)
                part_ref[own : own + 1, here] = jnp.sum(scaled, axis=0, keepdims=True)
                total_ref[own] += jnp.sum(scaled, axis=1, keepdims=True)
    gain_total = jnp.zeros((1, width), f32)
    leaving = []
    for at, here in enumerate(blocks):
        mask = lax.broadcasted_iota(jnp.int32, (groups, STEP), 0) == gid_ref[:, here]
        for slot in range(experts):
            own = slice(slot, slot + 1)
            total = jnp.sum(jnp.where(mask, total_ref[slot], 0.0), axis=0, keepdims=True)
            gl_ref[own, here] = (part_ref[own, here] - wt_ref[own, here] * total).astype(bf16)
        hidden = hidden_ref[here, :].astype(f32)
        scale = rms_scale(hidden)
        unit = hidden * scale
        arriving[2, at].wait()
        if at + 1 < len(blocks):
            load((2,), at + 1)
        hidden_ref[here, :] = (hidden + dot(turned_ref[here, :], slots(0))).astype(bf16)
        leaving.append(push(hidden_ref.at[here], kept_out_ref.at[here], sems.at[4, at]))
        grad_normed = dot(turned_ref[here, :], slots(1)) + dot(gl_ref[:, here], small[:experts], TN)
        weighted = gain * grad_normed
        gain_total = gain_total + jnp.sum(grad_normed * unit, axis=0, keepdims=True)
        back = scale * (weighted - unit * jnp.mean(weighted * unit, axis=-1, keepdims=True))
        low = (cot_ref[here, :].astype(f32) + back).astype(bf16)
        cot_ref[here, :] = low
        leaving.append(push(cot_ref.at[here], kept_gh_ref.at[here], sems.at[5, at]))
        grad_att = dot(low, out_w, NT).astype(bf16)
        gown_ref[here, :] = grad_att[:, :half]
        gaway_ref[here, :] = grad_att[:, half:]
    for copy in atts:
        copy.wait()
    small_ref[:half, :width] = dot(own_ref[...], cot_ref[...], TN).astype(bf16)
    small_ref[half:, :width] = dot(away_ref[...], cot_ref[...], TN).astype(bf16)
    tail = [dot(gl_ref[...], normed_ref[...]), gain_total, jnp.zeros((127 - experts, width), f32)]
    small_ref[:, width:] = jnp.transpose(jnp.concatenate(tail, 0)).astype(bf16)
    for copy in leaving:
        copy.wait()


def unmix(back, weights, gid, gathered, turned, cotangent, hidden, att_own, att_away):
    rows, width = cotangent.shape
    experts, _, groups, _ = back.shape
    kept = (turned, cotangent, hidden, att_own, att_away)
    return call(
        unmix_kernel,
        (
            in_hbm((rows, width), bf16),
            in_hbm((rows, width), bf16),
            shape_of((rows, width // 2), bf16),
            shape_of((rows, width // 2), bf16),
            shape_of((width, width + 128), bf16),
        ),
        (pltpu.with_memory_space_constraint(back, pltpu.VMEM), weights, gid, from_hbm(gathered), *[from_hbm(array) for array in kept]),
        room=room_for(UNMIX_ROOM, experts * groups),
        in_specs=[VMEM, VMEM, VMEM] + [HBM] * 6,
        out_specs=[HBM] * 2 + [VMEM] * 3,
        scratch_shapes=[pltpu.VMEM(array.shape, bf16) for array in kept]
        + [
            pltpu.VMEM((width, width + 128), bf16),
            pltpu.VMEM((rows, width), bf16),
            pltpu.VMEM((experts, rows), f32),
            pltpu.VMEM((experts, groups, 1), f32),
            pltpu.VMEM((experts, rows), bf16),
            DMA((7, max(rows // STEP, 4))),
        ],
    )


def expert_kernel(
    pick_ref, in_ref, up_all_ref, down_all_ref, hint_ref,
    sent_ref, kept_act_ref, kept_pre_ref, kept_in_ref, mark_ref,
    up_ref, down_ref, act_ref, pre_ref, out_ref, load_sems, sems,
):
    parts, _, groups, width = in_ref.shape
    many = min(EXPERT_ROWS // groups, parts)
    pick = pick_ref[0]
    load_up = push(up_all_ref.at[pick], up_ref, load_sems.at[0])
    set_mark(mark_ref)
    copies = []
    for at, part in enumerate(range(0, parts, many)):
        here = slice(part * groups, (part + many) * groups)
        owners = slice(part, part + many)
        rows, grad = [in_ref[owners, place].reshape(many * groups, width) for place in range(2)]
        if at == 0:
            load_up.wait()
            load_down = push(down_all_ref.at[pick], down_ref, load_sems.at[1])
        pre = dot(rows, up_ref[...])
        cdf = 0.5 + 0.5 * lax.erf(pre * 0.7071067811865476)
        slope = cdf + pre * (jnp.exp(-0.5 * pre * pre) * 0.3989422804014327)
        act = (pre * cdf).astype(bf16)
        act_ref[here, :] = act
        copies.append(push(act_ref.at[here], kept_act_ref.at[here], sems.at[0, at]))
        if at == 0:
            load_down.wait()
            copies.append(push(in_ref, kept_in_ref, load_sems.at[2]))
        grad_pre = (dot(grad, down_ref[...], NT) * slope).astype(bf16)
        pre_ref[here, :] = grad_pre
        copies.append(push(pre_ref.at[here], kept_pre_ref.at[here], sems.at[1, at]))
        for place, result in enumerate((dot(act, down_ref[...]), dot(grad_pre, up_ref[...], NT))):
            out_ref[owners, place] = result.astype(bf16).reshape(many, groups, width)
            copies.append(push(out_ref.at[owners, place], sent_ref.at[owners, place], sems.at[2 + place, at]))
    for copy in copies:
        copy.wait()


def expert_pass(pick, arrived, w_up, w_down, hint):
    parts, _, groups, width = arrived.shape
    rows = parts * groups
    hidden = w_up.shape[2]
    return call(
        expert_kernel,
        (
            in_hbm(arrived.shape, bf16),
            in_hbm((rows, hidden), bf16),
            in_hbm((rows, hidden), bf16),
            in_hbm(arrived.shape, bf16),
            shape_of(MARK, f32),
        ),
        (pick, pltpu.with_memory_space_constraint(arrived, pltpu.VMEM), from_hbm(w_up), from_hbm(w_down), hint),
        room=room_for(EXPERT_ROOM, rows),
        in_specs=[SMEM, VMEM, HBM, HBM, ANY],
        out_specs=[HBM, HBM, HBM, HBM, VMEM],
        scratch_shapes=[
            pltpu.VMEM(w_up.shape[1:], bf16),
            pltpu.VMEM(w_down.shape[1:], bf16),
            pltpu.VMEM((rows, hidden), bf16),
            pltpu.VMEM((rows, hidden), bf16),
            pltpu.VMEM(arrived.shape, bf16),
            DMA((3,)),
            DMA((4, max(rows // EXPERT_ROWS, 1))),
        ],
    )


def expert_grad_kernel(
    in_ref, kept_act_ref, kept_pre_ref, hint_ref, grad_ref, mark_ref, act_ref, pre_ref, out_ref, load_sems, sems
):
    shards, pieces, per, width = grad_ref.shape
    rows, hidden = act_ref.shape
    slabs = [slice(at, at + width) for at in range(0, hidden, width)]
    loads = [
        [push(kept.at[:, slab], ref.at[:, slab], load_sems.at[place, at]) for at, slab in enumerate(slabs)]
        for place, (kept, ref) in enumerate(((kept_act_ref, act_ref), (kept_pre_ref, pre_ref)))
    ]
    down_pieces = hidden // shards // per
    set_mark(mark_ref)
    mixed, grad = [in_ref[:, place].reshape(rows, width) for place in range(2)]
    for at, slab in enumerate(slabs):
        loads[0][at].wait()
        grad_down = dot(act_ref[:, slab], grad, TN).astype(bf16)
        span = width // (down_pieces * per)
        out_ref[at * span : (at + 1) * span, :down_pieces] = grad_down.reshape(span, down_pieces, per, width)
    copies = [push(out_ref.at[:, :down_pieces], grad_ref.at[:, :down_pieces], sems.at[0])]
    for at, slab in enumerate(slabs):
        loads[1][at].wait()
        grad_up = dot(mixed, pre_ref[:, slab], TN).astype(bf16)
        out_ref[:, down_pieces + at] = grad_up.reshape(shards, per, width)
    copies.append(push(out_ref.at[:, down_pieces:], grad_ref.at[:, down_pieces:], sems.at[1]))
    for copy in copies:
        copy.wait()


def expert_grads(arrived, act, grad_pre, shards, hint):
    width = arrived.shape[3]
    hidden = act.shape[1]
    per = width // shards
    grad = (shards, (hidden // shards) // per + hidden // width, per, width)
    return call(
        expert_grad_kernel,
        (in_hbm(grad, bf16), shape_of(MARK, f32)),
        (arrived, from_hbm(act), from_hbm(grad_pre), hint),
        room=room_for(GRAD_ROOM, act.shape[0]),
        in_specs=[VMEM, HBM, HBM, ANY],
        out_specs=[HBM, VMEM],
        scratch_shapes=[
            pltpu.VMEM(act.shape, bf16),
            pltpu.VMEM(act.shape, bf16),
            pltpu.VMEM(grad, bf16),
            DMA((2, hidden // width)),
            DMA((2,)),
        ],
    )


def shard_sum_kernel(in_ref, *refs):
    down_ref, up_ref, mark_ref = refs[-3:]
    set_mark(mark_ref)
    total = in_ref[0, 0].astype(f32)
    for part in range(1, in_ref.shape[0]):
        total = total + in_ref[part, 0].astype(f32)
    down_rows, width = down_ref.shape[1:]
    down_ref[0] = total[:down_rows]
    per = up_ref.shape[1]
    for at in range(0, up_ref.shape[2] // width):
        here = down_rows + at * per
        up_ref[0, :, at * width : (at + 1) * width] = total[here : here + per]


def shard_sum(parts, per_owner, down_rows, up_rows, experts, before=()):
    shards, tall, width = parts.shape
    parts = parts.reshape(shards // per_owner, per_owner, tall, width)
    hidden = (tall - down_rows) // up_rows * width
    first = experts.start
    return call(
        shard_sum_kernel,
        (
            in_hbm((per_owner, down_rows, width), f32),
            in_hbm((per_owner, up_rows, hidden), f32),
            shape_of(MARK, f32),
        ),
        (parts, *before),
        grid=(len(experts),),
        in_specs=[pl.BlockSpec((parts.shape[0], 1, tall, width), lambda at: (0, first + at, 0, 0))]
        + [ANY] * len(before),
        out_specs=[
            pl.BlockSpec((1, down_rows, width), lambda at: (first + at, 0, 0)),
            pl.BlockSpec((1, up_rows, hidden), lambda at: (first + at, 0, 0)),
            pl.BlockSpec(MARK, lambda at: (0, 0)),
        ],
        input_output_aliases={1 + at: at for at in range(len(before))},
    )


def own_grad_kernel(unit_t_ref, grad_ref, w_ref, grad_w_ref, part_ref):
    wide = grad_ref.shape[1]
    grad_w_ref[...] = dot(unit_t_ref[...], grad_ref[...])
    for at in range(0, part_ref.shape[0], 1024):
        here = slice(at, at + 1024)
        part_ref[here, :] = dot(grad_ref[here, :], w_ref[:, :wide], NT)


def own_grad(unit_t, grad, weights):
    width, rows = unit_t.shape
    return call(
        own_grad_kernel,
        (shape_of((width, grad.shape[1]), f32), shape_of((rows, width), f32)),
        (unit_t, grad, weights),
        room=16,
        in_specs=[VMEM] * 3,
        out_specs=[VMEM] * 2,
    )


def away_grad_kernel(mine_ref, unit_t_ref, grad_ref, own_ref, small_ref, keep_ref, send_ref, total_ref):
    total_ref[...] = dot(unit_t_ref[...], grad_ref[...])
    many, per, _ = keep_ref.shape
    mine = mine_ref[0]
    left = own_ref.shape[1]
    right = left + total_ref.shape[1]
    for place in range(many):
        for part, ref in ((mine, keep_ref), (1 - mine, send_ref)):
            rows = pl.ds(pl.multiple_of((2 * place + part) * per, per), per)
            ref[place, :, :left] = own_ref[rows, :].astype(ref.dtype)
            ref[place, :, left:right] = total_ref[rows, :].astype(ref.dtype)
            ref[place, :, right:] = small_ref[rows, :].astype(ref.dtype)


def halves(array, mine):
    keep, send = [lax.dynamic_index_in_dim(array, part[0], 1, keepdims=False) for part in (mine, 1 - mine)]
    return keep, send.astype(bf16)


def away_grad(mine, unit_t, grad, own, small, devices):
    width, rows = unit_t.shape
    wide = grad.shape[1]
    per = width // devices
    if per % 16:
        total = jnp.concatenate([own, dot(unit_t, grad), small.astype(f32)], 1)
        return halves(total.reshape(devices // 2, 2, per, -1), mine)
    dims = (devices // 2, per, own.shape[1] + wide + small.shape[1])
    return call(
        away_grad_kernel,
        (shape_of(dims, f32), shape_of(dims, bf16)),
        (mine, unit_t, grad, own, small),
        room=16,
        in_specs=[SMEM] + [VMEM] * 4,
        out_specs=[VMEM] * 2,
        scratch_shapes=[pltpu.VMEM((width, wide), f32)],
    )


def token_grad_kernel(part_ref, grad_ref, w_ref, tok_ref, gh_ref, out_ref, mark_ref):
    set_mark(mark_ref)
    wide = grad_ref.shape[1]
    for at in range(0, tok_ref.shape[0], 512):
        here = slice(at, at + 512)
        weighted = part_ref[here, :] + dot(grad_ref[here, :], w_ref[:, wide : 2 * wide], NT)
        source = tok_ref[here, :].astype(f32)
        scale = rms_scale(source)
        unit = source * scale
        back = scale * (weighted - unit * jnp.mean(weighted * unit, axis=-1, keepdims=True))
        out_ref[here, :] = (gh_ref[here, :].astype(f32) + back).astype(bf16)


def token_grad(part, grad, weights, tokens, grad_hidden):
    return call(
        token_grad_kernel,
        (shape_of(tokens.shape, bf16), shape_of(MARK, f32)),
        (part, grad, weights, tokens, grad_hidden),
        room=16,
        in_specs=[VMEM] * 5,
        out_specs=[VMEM] * 2,
    )


def swap(array, axis, size, bit):
    return lax.ppermute(array, axis, [(at, at ^ bit) for at in range(size)])


def axis_bits(sizes):
    bits = []
    for axis, size in sizes:
        bit = size // 2
        while bit:
            bits.append((axis, size, bit))
            bit //= 2
    return bits


def gather_rows(shard, sizes, meanwhile):
    bits = axis_bits(sizes)
    held = shard[(None,) * len(bits)]
    for place, (axis, size, bit) in enumerate(bits):
        other = swap(held, axis, size, bit)
        if place == len(bits) - 2:
            other, meanwhile = lax.optimization_barrier((other, meanwhile))
        upper = (lax.axis_index(axis) // bit) % 2 == 1
        first = jnp.where(upper, other, held)
        second = jnp.where(upper, held, other)
        held = jnp.concatenate([first, second], axis=place)
    return held.reshape((shard.shape[0] * 2 ** len(bits),) + shard.shape[1:]), meanwhile


def add_split_kernel(mine_ref, keep_ref, got_ref, hint_ref, next_keep_ref, send_ref):
    mine = mine_ref[0]
    for part, ref in ((mine, next_keep_ref), (1 - mine, send_ref)):
        value = keep_ref[:, pl.ds(part, 1)] + got_ref[:, pl.ds(part, 1)].astype(f32)
        ref[...] = value[:, 0].astype(ref.dtype)


def add_split(mine, keep, got, hint):
    many, per, wide = keep.shape
    dims = (many // 2, per, wide)
    keep, got = [array.reshape(many // 2, 2, per, wide) for array in (keep, got)]
    if per % 16:
        return halves(keep + got.astype(f32), mine)
    return call(
        add_split_kernel,
        (shape_of(dims, f32), shape_of(dims, bf16)),
        (mine, keep, got, hint),
        room=16,
        in_specs=[SMEM, VMEM, VMEM, ANY],
        out_specs=[VMEM] * 2,
    )


def scatter_rows(keep, send, sizes, hints):
    bits = axis_bits(sizes)[::-1]
    for place, (axis, size, bit) in enumerate(bits):
        got = swap(send, axis, size, bit)
        if place + 1 == len(bits):
            return keep, got
        axis, size, bit = bits[place + 1]
        mine = ((lax.axis_index(axis) // bit) % 2).astype(jnp.int32).reshape(1)
        keep, send = add_split(mine, keep, got, hints.get(place, got))


def on_device(
    n_dp, n_owner, tokens, seq_lengths, group_map, gain_attn, gain_mix, w_qkv, w_out, w_ctrl, w_up, w_down, cotangent
):
    rows, width = tokens.shape
    experts = w_ctrl.shape[1]
    per_owner = w_up.shape[0]
    groups = rows // G
    parts = n_dp // per_owner
    sizes = (("dp", n_dp), ("expert", n_owner))
    dp = lax.axis_index("dp")
    pick = (dp % per_owner).astype(jnp.int32).reshape(1)

    gain_row = gain_attn.reshape(1, -1)
    shard = call(
        functools.partial(pack_kernel, n_owner),
        shape_of((w_ctrl.shape[0], 4 * width + 128), bf16),
        (seq_lengths, *[from_hbm(array) for array in (w_qkv, gain_row, w_out, w_ctrl, gain_mix.reshape(1, -1))]),
        room=8,
        in_specs=[SMEM] + [VMEM] * 5,
        out_specs=VMEM,
    )

    def neighbour(array):
        return swap(array, "expert", n_owner, 1)

    unit_one, unit_away, unit_t, gid = call(
        prep_kernel,
        (
            in_hbm((rows, width), bf16),
            in_hbm((rows, width), bf16),
            in_hbm((width, rows), bf16),
            shape_of((1, rows), jnp.int32),
        ),
        (tokens, neighbour(tokens), group_map.reshape(groups, G)),
        room=16,
        in_specs=[VMEM] * 3,
        out_specs=[HBM, HBM, HBM, VMEM],
        scratch_shapes=[pltpu.VMEM((rows, width), bf16)] * 2 + [pltpu.VMEM((width, rows), bf16), DMA((3, rows // 512))],
    )
    gathered, (unit_one, unit_away) = gather_rows(shard, sizes, (unit_one, unit_away))
    triple = 3 * width

    near = (dp * n_owner + (lax.axis_index("expert") ^ 1)) * w_ctrl.shape[0]
    lengths, att_own, att_away, lse_own, lse_away, own_qkv, away_qkv, kept_away = attend_forward(
        seq_lengths, near.astype(jnp.int32).reshape(1), unit_one, unit_away, gathered
    )
    hidden, weights, mixed, kept_own, kept_back = mix(
        tokens, att_own, neighbour(att_away), gathered, gid, cotangent, experts
    )

    teams = [
        [(part * per_owner + low) * n_owner + owner for low in range(per_owner) for owner in range(n_owner)]
        for part in range(parts)
    ]

    def exchange(array):
        return lax.all_to_all(
            array, ("dp", "expert"), split_axis=0, concat_axis=0, axis_index_groups=teams, tiled=True
        )

    arrived = exchange(mixed)
    turned, mark = turn(weights, gid, groups)
    results, act, grad_pre, arrived, mark = expert_pass(pick, arrived, w_up, w_down, mark)
    back = exchange(results)
    grad_experts, mark = expert_grads(arrived, act, grad_pre, n_dp, mark)
    shards = lax.all_to_all(
        grad_experts.reshape(n_dp, -1, width), "dp", split_axis=0, concat_axis=0, tiled=True
    )
    output, grad_hidden, grad_own, grad_away, grad_small = unmix(
        back, weights, gid, gathered, turned, cotangent, hidden, kept_own, kept_back
    )

    grad_here = neighbour(grad_away)
    grad_one = attend_backward(0, lengths, own_qkv, grad_own, kept_own, lse_own, grad_own)
    grad_two = neighbour(attend_backward(1, lengths, away_qkv, grad_here, kept_away, lse_away, grad_one))
    grad_w_own, token_part = own_grad(unit_t, grad_one, gathered)
    axis, size, bit = axis_bits(sizes)[-1]
    mine = ((lax.axis_index(axis) // bit) % 2).astype(jnp.int32).reshape(1)
    keep, send = away_grad(mine, unit_t, grad_two, grad_w_own, grad_small, n_dp * n_owner)
    grad_tokens, token_mark = token_grad(token_part, grad_two, gathered, tokens, grad_hidden)
    shapes = (per_owner, w_down.shape[1] // n_dp, width // n_dp)
    *some, shard_mark = shard_sum(shards, *shapes, range(per_owner // 2))
    grad_down_shard, grad_up_shard, _ = shard_sum(shards, *shapes, range(per_owner // 2, per_owner), some)
    keep, got = scatter_rows(keep, send, sizes, {1: token_mark, len(axis_bits(sizes)) - 2: shard_mark})
    own_rows = w_qkv.shape[0]
    shard_qkv, shard_out, shard_ctrl, shard_gain_one, shard_gain_two = call(
        functools.partial(finish_kernel, n_owner),
        (
            shape_of(w_qkv.shape, f32),
            shape_of(w_out.shape, f32),
            shape_of(w_ctrl.shape, f32),
            shape_of((1, own_rows), f32),
            shape_of((1, own_rows), f32),
        ),
        (keep, got, gain_row, w_qkv),
        room=8,
        in_specs=[VMEM] * 4,
        out_specs=[VMEM] * 5,
    )
    return (
        output,
        grad_tokens,
        shard_gain_one.reshape(-1),
        shard_gain_two.reshape(-1),
        shard_qkv,
        shard_out,
        shard_ctrl,
        grad_up_shard,
        grad_down_shard,
    )


def solution(mesh):
    both = ("dp", "expert")
    rows = P(both, None)
    return jax.shard_map(
        functools.partial(on_device, mesh.shape["dp"], mesh.shape["expert"]),
        mesh=mesh,
        in_specs=(
            rows, P(both), rows, P(both), P(both), rows, rows, rows,
            P("expert", None, None), P("expert", None, None), rows,
        ),
        out_specs=(
            rows, rows, P(both), P(both), rows, rows, rows,
            P("expert", "dp", None), P("expert", "dp", None),
        ),
        check_vma=False,
    )
```
